128 devices in a mesh: seq: 8 (over y, core), head: 16 (over z, x).
Axes of the slice: x: 4, y: 4, z: 4, core: 2. Of those that a mesh axis runs over, the one named last changes fastest.
Arguments:
- layer_input: bfloat16 [16384, 1024], P(('seq', 'head')), may hold values from -6 to 6
- second_start: int32 [8], P('seq'), may hold values from 1921 to 2048, as said below
- mixer_gain: bfloat16 [1024], replicated, may hold values from 0.099609375 to 1.8984375
- w_query: bfloat16 [1024, 1024], replicated, may hold values from -0.1875 to 0.1875
- w_query_rope: bfloat16 [1024, 512], replicated, may hold values from -0.1875 to 0.1875
- w_latent: bfloat16 [1024, 512], replicated, may hold values from -0.1875 to 0.1875
- w_key_rope: bfloat16 [1024, 32], replicated, may hold values from -0.1875 to 0.1875
- w_key_up: bfloat16 [2, 256, 512], replicated, may hold values from -0.375 to 0.375
- w_value_up: bfloat16 [2, 256, 512], replicated, may hold values from -0.375 to 0.375
- w_out: bfloat16 [1024, 1024], replicated, may hold values from -0.75 to 0.75
- feed_gain: bfloat16 [1024], replicated, may hold values from 0.099609375 to 1.8984375
- w_gate: bfloat16 [1024, 2816], replicated, may hold values from -0.1875 to 0.1875
- w_up: bfloat16 [1024, 2816], replicated, may hold values from -0.1875 to 0.1875
- w_down: bfloat16 [2816, 1024], replicated, may hold values from -0.109375 to 0.109375
- cotangent: bfloat16 [16384, 1024], P(('seq', 'head')), may hold values from -6 to 6
Outputs:
- output: bfloat16 [16384, 1024], P(('seq', 'head'))
- grad_input: float32 [16384, 1024], P(('seq', 'head'))
- grad_mixer_gain: float32 [1024], P(('seq', 'head'))
- grad_w_query: float32 [1024, 1024], P(('seq', 'head'))
- grad_w_query_rope: float32 [1024, 512], P(('seq', 'head'))
- grad_w_latent: float32 [1024, 512], P(('seq', 'head'))
- grad_w_key_rope: float32 [1024, 32], P(('seq', 'head'))
- grad_w_key_up: float32 [2, 256, 512], P(None, None, ('seq', 'head'))
- grad_w_value_up: float32 [2, 256, 512], P(None, None, ('seq', 'head'))
- grad_w_out: float32 [1024, 1024], P(('seq', 'head'))
- grad_feed_gain: float32 [1024], P(('seq', 'head'))
- grad_w_gate: float32 [1024, 2816], P(('seq', 'head'))
- grad_w_up: float32 [1024, 2816], P(('seq', 'head'))
- grad_w_down: float32 [2816, 1024], P(None, ('seq', 'head'))
The draws below stay inside these ranges and needn't reach their ends.
Inputs may be any that keep to these rules, and one draw needn't show every extreme that they name: Each group's first sequence reaches into its last 128 tokens: second_start is 2048 (one sequence) or lies within the group's last 128 tokens; both ends of the range occur in every draw.
All inputs are finite; a program needn't handle non-finite values.
Results may differ from the reference program's by a relative error of at most 0.015.
Values may be sent and summed in bfloat16 or wider, within the bound.
A program may use at most 192 MiB of HBM per device.

```python
import math
import jax
import jax.numpy as jnp
from jax import lax

D = 1024
HEADS = 16
HEAD_DIM = 64
ROPE = 32
LATENT = 256
LATENT_HEADS = 2
FF = 2816
TOK_DEV = 128
TOKENS = 16384
GROUP = 2048
SHARE = 8
QBLOCK = 512
N_SEQ = 8


def draw_second_start(key, part):
    key = jax.random.fold_in(key, 7)
    order = jax.random.permutation(jax.random.fold_in(key, 1), N_SEQ)
    values = jax.random.randint(jax.random.fold_in(key, 2), (N_SEQ,), GROUP - TOK_DEV + 1, GROUP + 1)
    values = values.at[order[0]].set(GROUP)
    values = values.at[order[1]].set(GROUP - TOK_DEV + 1)
    return values.astype(jnp.int32)


def block_scale(rng, shape, cuts, smallest, high):
    factor_of = 1.0
    for dim, parts in cuts:
        heights = jax.random.uniform(jax.random.fold_in(jax.random.fold_in(rng, 6), dim), (parts,), jnp.float32, smallest / len(cuts), high / len(cuts))
        factor_of = factor_of * jnp.repeat(jnp.exp(heights), shape[dim] // parts).reshape((-1,) + (1,) * (len(shape) - 1 - dim))
    return factor_of


def gaussian(own_key, dims, deviation, bound, cuts=(), kind=jnp.bfloat16):
    values = deviation * jax.random.normal(own_key, dims, jnp.float32)
    if cuts:
        values = values * block_scale(own_key, dims, cuts, -0.22, 0.18)
    return jnp.clip(values, -bound, bound).astype(kind)


def setup_inputs(seed: int = 0) -> dict:
    arg_keys = jax.random.split(jax.random.key(seed), 16)
    layer_input = gaussian(arg_keys[0], (TOKENS, D), 1.0, 6.0, ((0, 128),))
    second_start = draw_second_start(jax.random.fold_in(arg_keys[15], 71), 0)
    mixer_gain = jnp.clip(1.0 + 0.18 * jax.random.normal(arg_keys[2], (D,), jnp.float32), 0.099609375, 1.8984375).astype(jnp.bfloat16)
    w_query = gaussian(arg_keys[3], (D, HEADS * HEAD_DIM), D ** -0.5, 0.1875)
    w_query_rope = gaussian(arg_keys[4], (D, HEADS * ROPE), D ** -0.5, 0.1875)
    w_latent = gaussian(arg_keys[5], (D, LATENT_HEADS * LATENT), D ** -0.5, 0.1875)
    w_key_rope = gaussian(arg_keys[6], (D, ROPE), D ** -0.5, 0.1875)
    w_key_up = gaussian(arg_keys[7], (LATENT_HEADS, LATENT, SHARE * HEAD_DIM), LATENT ** -0.5, 0.375)
    w_value_up = gaussian(arg_keys[8], (LATENT_HEADS, LATENT, SHARE * HEAD_DIM), LATENT ** -0.5, 0.375)
    w_out = gaussian(arg_keys[9], (HEADS * HEAD_DIM, D), (HEADS * HEAD_DIM // 16) ** -0.5, 0.75)
    feed_gain = jnp.clip(1.0 + 0.18 * jax.random.normal(arg_keys[10], (D,), jnp.float32), 0.099609375, 1.8984375).astype(jnp.bfloat16)
    w_gate = gaussian(arg_keys[11], (D, FF), D ** -0.5, 0.1875)
    w_up = gaussian(arg_keys[12], (D, FF), D ** -0.5, 0.1875)
    w_down = gaussian(arg_keys[13], (FF, D), FF ** -0.5, 0.109375)
    cotangent = gaussian(arg_keys[14], (TOKENS, D), 1.0, 6.0, ((0, 128),))
    return {"layer_input": layer_input, "second_start": second_start, "mixer_gain": mixer_gain, "w_query": w_query, "w_query_rope": w_query_rope, "w_latent": w_latent, "w_key_rope": w_key_rope, "w_key_up": w_key_up, "w_value_up": w_value_up, "w_out": w_out, "feed_gain": feed_gain, "w_gate": w_gate, "w_up": w_up, "w_down": w_down, "cotangent": cotangent}


@jax.custom_vjp
def low(v):
    return lax.optimization_barrier(v.astype(jnp.bfloat16)).astype(jnp.float32)

@jax.custom_vjp
def low_back(v):
    return v

def low_keep(v):
    return (low(v), None)

def low_pass(kept, grad):
    return (grad,)

def back_keep(v):
    return (v, None)

def back_low(kept, grad):
    return (low(grad),)
low.defvjp(low_keep, low_pass)
low_back.defvjp(back_keep, back_low)

def matmul(left, right):
    return jnp.dot(left, right, precision=lax.Precision.HIGHEST, preferred_element_type=jnp.float32)

def turning(positions, width):
    half = width // 2
    freqs = 10000.0 ** (-jnp.arange(half, dtype=jnp.float32) * 2.0 / width)
    angles = positions.astype(jnp.float32)[:, None] * freqs[None, :]
    return (jnp.cos(angles), jnp.sin(angles))

def rotate(values, cosine, sine):
    half = values.shape[-1] // 2
    first = values[..., :half]
    second = values[..., half:]
    return jnp.concatenate([first * cosine - second * sine, first * sine + second * cosine], -1)

def normalize(values, gain):
    return values * lax.rsqrt(lax.optimization_barrier(jnp.mean(values * values, -1, keepdims=True)) + 1e-06) * gain

def reference(layer_input, second_start, mixer_gain, w_query, w_query_rope, w_latent, w_key_rope, w_key_up, w_value_up, w_out, feed_gain, w_gate, w_up, w_down, cotangent):
    highest = lax.Precision.HIGHEST
    index = jnp.arange(GROUP, dtype=jnp.int32)
    boundary_col = second_start.astype(jnp.int32)[:, None]
    positions = (index[None, :] - jnp.where(index[None, :] >= boundary_col, boundary_col, 0)).reshape(TOKENS)
    cosine, sine = turning(positions, ROPE)
    scale = 1.0 / math.sqrt(HEAD_DIM + ROPE)
    block_starts = jnp.arange(GROUP // QBLOCK, dtype=jnp.int32) * QBLOCK

    def attend(query, query_rope, latent, key_rope, boundary, key_up, value_up):
        key = low(low_back(jnp.einsum('tgl,glf->tgf', latent, key_up, precision=highest))).reshape(GROUP, HEADS, HEAD_DIM)
        value = low(low_back(jnp.einsum('tgl,glf->tgf', latent, value_up, precision=highest))).reshape(GROUP, HEADS, HEAD_DIM)
        later = index >= boundary

        def block(start):
            rows = start + jnp.arange(QBLOCK, dtype=jnp.int32)
            block_query = lax.dynamic_slice_in_dim(query, start, QBLOCK, 0)
            block_rope = lax.dynamic_slice_in_dim(query_rope, start, QBLOCK, 0)
            raw = jnp.einsum('bhd,khd->hbk', block_query, key, precision=highest)
            raw = raw + jnp.einsum('bhr,kr->hbk', block_rope, key_rope, precision=highest)
            raw = low_back(raw * scale)
            allowed = (index[None, :] <= rows[:, None]) & (later[None, :] == (rows[:, None] >= boundary))
            masked = jnp.where(allowed[None], raw, -1e+30)
            top = lax.optimization_barrier(jnp.max(masked, -1, keepdims=True))
            weights = jnp.exp(masked - top)
            probs = low(weights / lax.optimization_barrier(jnp.sum(weights, -1, keepdims=True)))
            return low(low_back(jnp.einsum('hbk,khd->bhd', probs, value, precision=highest)))
        return lax.map(jax.checkpoint(block), block_starts).reshape(GROUP, HEADS * HEAD_DIM)

    def forward(inputs, gain_one, wq, wqr, wlat, wkr, wku, wvu, wout, gain_two, wgate, wupper, wdown):
        normed_one = low(normalize(inputs, gain_one))
        query = low(low_back(matmul(normed_one, wq)))
        turned = low_back(matmul(normed_one, wqr)).reshape(TOKENS, HEADS, ROPE)
        query_rope = low(low_back(rotate(turned, cosine[:, None], sine[:, None])))
        latent = low(low_back(matmul(normed_one, wlat)))
        key_rope = low(low_back(rotate(low_back(matmul(normed_one, wkr)), cosine, sine)))

        def step(carry, pieces):
            return (carry, attend(pieces[0], pieces[1], pieces[2], pieces[3], pieces[4], wku, wvu))
        pieces = (query.reshape(N_SEQ, GROUP, HEADS, HEAD_DIM), query_rope.reshape(N_SEQ, GROUP, HEADS, ROPE), latent.reshape(N_SEQ, GROUP, LATENT_HEADS, LATENT), key_rope.reshape(N_SEQ, GROUP, ROPE), second_start.astype(jnp.int32))
        unused, attended = lax.scan(step, jnp.zeros((), jnp.float32), pieces)
        attended = attended.reshape(TOKENS, HEADS * HEAD_DIM)
        middle = inputs + low_back(matmul(attended, wout))
        normed_two = low(normalize(middle, gain_two))
        gate = low_back(matmul(normed_two, wgate))
        upward = low_back(matmul(normed_two, wupper))
        activated = low(jax.nn.silu(gate) * upward)
        return middle + matmul(activated, wdown)
    arrays = (layer_input, mixer_gain, w_query, w_query_rope, w_latent, w_key_rope, w_key_up, w_value_up, w_out, feed_gain, w_gate, w_up, w_down)
    arrays = tuple((item.astype(jnp.float32) for item in arrays))
    result, pullback = jax.vjp(forward, *arrays)
    grads = pullback(cotangent.astype(jnp.float32))
    return (result.astype(jnp.bfloat16), grads[0], grads[1], grads[2], grads[3], grads[4], grads[5], grads[6], grads[7], grads[8], grads[9], grads[10], grads[11], grads[12])
```

```python
import math

import jax
import jax.numpy as jnp
import numpy as np
from jax import lax
from jax.experimental import pallas as pl
from jax.experimental.pallas import tpu as pltpu
from jax.sharding import PartitionSpec as P

HEADS = 16
HEAD_DIM = 64
ROPE = 32
LATENT = 256
LATENT_HEADS = 2


epsilon = 1e-06


def for_sending(x):

    def short(part):
        return part.astype(jnp.bfloat16) if part.dtype == jnp.float32 else part

    return jax.tree.map(short, x)


def across(left, right):
    return lax.dot_general(
        left, right, (((0,), (0,)), ((), ())), preferred_element_type=jnp.float32
    )


def against(left, right):
    return lax.dot_general(
        left, right, (((1,), (1,)), ((), ())), preferred_element_type=jnp.float32
    )


def turning(positions, width):
    half = width // 2
    freqs = 10000.0 ** (-jnp.arange(half, dtype=jnp.float32) * 2.0 / width)
    angles = positions.astype(jnp.float32)[:, None] * freqs[None, :]
    return (jnp.cos(angles), jnp.sin(angles))


def rotate(values, cosine, sine):
    half = values.shape[-1] // 2
    first = values[..., :half]
    second = values[..., half:]
    return jnp.concatenate([first * cosine - second * sine, first * sine + second * cosine], -1)


def normalize(values, gain):
    inverse = lax.rsqrt(jnp.mean(values * values, -1, keepdims=True) + epsilon)
    return (values * inverse * gain, inverse)


def norm_back(values, inverse, gain, upstream):
    scaled = upstream * gain
    grad_values = inverse * scaled - values * (inverse * inverse * inverse) * jnp.mean(
        values * scaled, -1, keepdims=True
    )
    grad_gain = jnp.sum(upstream * values * inverse, 0)
    return (grad_values, grad_gain)


MESH = pl.DeviceIdType.MESH
W = 256
RING = 4
ORDERS = (("y", "z", "x"), ("z", "x", "y"), ("x", "y", "z"))
FIRST, LATER = 11, 4
JOBS = FIRST + LATER


def place():
    s, h = lax.axis_index("seq"), lax.axis_index("head")
    return {"y": s // 2, "core": s % 2, "z": h // 4, "x": h % 4}


def device(at):
    return (at["y"] * 2 + at["core"], at["z"] * 4 + at["x"])


def beside(at, axis, step):
    return device({**at, axis: (at[axis] + step) % 4})


def other_core(at):
    return device({**at, "core": 1 - at["core"]})


def chosen_rows(order, core):
    row = lax.broadcasted_iota(jnp.int32, (512, 1024), 0)
    part = {"core": core}
    for shift, axis in zip((7, 5, 3), order):
        part[axis] = (row >> shift) & 3
    column = (part["y"] << 8) + (core << 7) + (part["z"] << 5) + (part["x"] << 3) + (row & 7)
    return (lax.broadcasted_iota(jnp.int32, (512, 1024), 1) == column).astype(jnp.bfloat16)


def sum_kernel(*refs):
    lefts, rights = refs[:6], refs[6:13]
    (outs, at_own, at_send, at, g, d, s1, s2, sa, sb, sc, sd, se, sf, ra, rb, rc, rd, re, rf,
     send_sem, recv_sem, at_sem, g_send, g_recv, g_local) = refs[13:]
    me = place()
    barrier = pltpu.get_barrier_semaphore()
    peers = [other_core(me)] + [beside(me, a, s) for a in "xyz" for s in (1, -1)]
    for peer in peers:
        pl.semaphore_signal(barrier, inc=1, device_id=peer, device_id_type=MESH)
    pl.semaphore_wait(barrier, len(peers))

    def remote(src, dst, send, recv, to):
        return pltpu.make_async_remote_copy(
            src_ref=src, dst_ref=dst, send_sem=send, recv_sem=recv, device_id=to, device_id_type=MESH
        )

    twin = other_core(me)
    sources = (((rights[0], 11), (rights[1], 4)), ((rights[2], 11), (rights[3], 4)), ((rights[4], 11), (rights[5], 2), (rights[6], 2)))
    for order in range(3):
        job = 0
        for ref, count in sources[order]:
            for c in range(count):
                piece = ref.at[:, c * W : (c + 1) * W]
                remote(piece, g.at[order, job, 128:256], g_send.at[order, job], g_recv.at[order, job], twin).start()
                pltpu.make_async_copy(piece, g.at[order, job, 0:128], g_local.at[order, job]).start()
                job += 1

    def from_twin(order, job):
        ref = g.at[order, job, 0:128]
        return remote(ref, g.at[order, job, 128:256], g_send.at[order, job], g_recv.at[order, job], twin)

    def from_here(order, job):
        ref = g.at[order, job, 0:128]
        return pltpu.make_async_copy(ref, ref, g_local.at[order, job])

    for order in range(3):
        for which in range(2):
            left = lefts[order * 2 + which][...]
            for mine in (0, 1):
                core = me["core"] if mine else 1 - me["core"]
                picked = lax.dot_general(chosen_rows(ORDERS[order], core), left, (((1,), (1,)), ((), ())), preferred_element_type=jnp.float32).astype(jnp.bfloat16)
                if mine:
                    at[order, which, :, 0:128] = picked
                else:
                    at_send[order, which] = picked
                    remote(at_send.at[order, which], at.at[order, which, :, 128:256], at_sem.at[0, order, which], at_sem.at[1, order, which], twin).start()
    for order in range(3):
        for which in range(2):
            remote(at_send.at[order, which], at.at[order, which, :, 128:256], at_sem.at[0, order, which], at_sem.at[1, order, which], twin).wait()

    sends = (sa, sb, sc, sd, se, sf)
    recvs = (ra, rb, rc, rd, re, rf)

    def message(order, phase, way, job):
        axis = ORDERS[order][phase // 2]
        slot = job % RING
        return remote(
            sends[phase].at[order, slot, way],
            recvs[phase].at[order, job, way],
            send_sem.at[order, phase, way, slot],
            recv_sem.at[order, phase, way, job],
            beside(me, axis, 1 if way == 0 else -1),
        )

    def free(order, phase, job):
        @pl.when(job >= RING)
        def _():
            for way in (0, 1):
                message(order, phase, way, job - RING).wait_send()

    def first_half(order, stage, job, block):
        phase = stage * 2
        free(order, phase, job)
        for way in (0, 1):
            ref = sends[phase].at[order, job % RING, way]
            ref[...] = block[:, way * (W // 2) : (way + 1) * (W // 2)].astype(ref.dtype)
            message(order, phase, way, job).start()

    def second_half(order, stage, job, block_of):
        phase = stage * 2 + 1
        free(order, phase, job)
        for way in (0, 1):
            message(order, phase - 1, way, job).wait_recv()
            ref = sends[phase].at[order, job % RING, way]
            block = block_of(1 if way == 0 else -1)
            here = slice(way * (W // 2), (way + 1) * (W // 2))
            there = slice((1 - way) * (W // 2), (2 - way) * (W // 2))
            ref[:, here] = (block[:, here] + recvs[phase - 1][order, job, way].astype(jnp.float32)).astype(ref.dtype)
            ref[:, there] = block[:, there].astype(ref.dtype)
            message(order, phase, way, job).start()

    def total(order, stage, job, block):
        phase = stage * 2 + 1
        for way in (0, 1):
            message(order, phase, way, job).wait_recv()
            block = block + recvs[phase][order, job, way].astype(jnp.float32)
        return block

    def block_of(order, stage, job):
        axis = ORDERS[order][stage]
        slot = job % RING

        def get(step):
            index = (me[axis] + step) % 4
            if stage == 0:
                return d[order, slot, pl.ds(pl.multiple_of(index * 128, 128), 128), :]
            if stage == 1:
                return s1[order, slot, pl.ds(pl.multiple_of(index * 32, 32), 32), :]
            return s2[order, slot, pl.ds(pl.multiple_of(index * 8, 8), 8), :]

        return get

    def step0(order, job):
        from_twin(order, job).wait_recv()
        from_here(order, job).wait()
        which = jnp.where(job >= FIRST, 1, 0)
        d[order, job % RING] = jnp.dot(at[order, which], g[order, job], preferred_element_type=jnp.float32)
        first_half(order, 0, job, block_of(order, 0, job)(2))

    def step1(order, job):
        second_half(order, 0, job, block_of(order, 0, job))

    def step2(order, job):
        s1[order, job % RING] = total(order, 0, job, block_of(order, 0, job)(0))
        first_half(order, 1, job, block_of(order, 1, job)(2))

    def step3(order, job):
        second_half(order, 1, job, block_of(order, 1, job))

    def step4(order, job):
        s2[order, job % RING] = total(order, 1, job, block_of(order, 1, job)(0))
        first_half(order, 2, job, block_of(order, 2, job)(2))

    def step5(order, job):
        second_half(order, 2, job, block_of(order, 2, job))

    def step6(order, job):
        outs[order, :, pl.ds(pl.multiple_of(job * W, W), W)] = total(order, 2, job, block_of(order, 2, job)(0))

    steps = (step0, step1, step2, step3, step4, step5, step6)

    @pl.loop(0, JOBS + 6)
    def _(t):
        for k in reversed(range(7)):
            job = t - k

            @pl.when((job >= 0) & (job < JOBS))
            def _():
                for order in range(3):
                    steps[k](order, job)

    for order in range(3):
        for phase in range(6):
            for way in (0, 1):
                for job in range(JOBS - RING, JOBS):
                    message(order, phase, way, job).wait_send()

        @pl.loop(0, JOBS)
        def _(job):
            from_twin(order, job).wait_send()


def sum_gradients(lefts, rights):
    bf, f32 = jnp.bfloat16, jnp.float32
    vm = lambda shape, kind=bf: pltpu.VMEM(shape, kind)
    dma = pltpu.SemaphoreType.DMA
    R, J = RING, JOBS
    return pl.pallas_call(
        sum_kernel,
        out_shape=jax.ShapeDtypeStruct((3, 8, JOBS * W), f32),
        in_specs=[pl.BlockSpec(memory_space=pltpu.VMEM)] * 13,
        out_specs=pl.BlockSpec(memory_space=pltpu.VMEM),
        scratch_shapes=[
            vm((8, 128)), vm((3, 2, 512, 128)), vm((3, 2, 512, 256)), vm((3, J, 256, W)),
            vm((3, R, 512, W), f32), vm((3, R, 128, W), f32), vm((3, R, 32, W), f32),
            vm((3, R, 2, 128, W // 2)), vm((3, R, 2, 128, W)),
            vm((3, R, 2, 32, W // 2)), vm((3, R, 2, 32, W)),
            vm((3, R, 2, 8, W // 2), f32), vm((3, R, 2, 8, W), f32),
            vm((3, J, 2, 128, W // 2)), vm((3, J, 2, 128, W)),
            vm((3, J, 2, 32, W // 2)), vm((3, J, 2, 32, W)),
            vm((3, J, 2, 8, W // 2), f32), vm((3, J, 2, 8, W), f32),
            dma((3, 6, 2, R)), dma((3, 6, 2, J)), dma((2, 3, 2)), dma((3, J)), dma((3, J)), dma((3, J)),
        ],
        compiler_params=pltpu.CompilerParams(collective_id=0, has_side_effects=True, vmem_limit_bytes=60 * 2**20),
        name="sum_gradients",
    )(*lefts, *rights)


def body(
    layer_input,
    second_start,
    mixer_gain,
    w_query,
    w_query_rope,
    w_latent,
    w_key_rope,
    w_key_up,
    w_value_up,
    w_out,
    feed_gain,
    w_gate,
    w_up,
    w_down,
    cotangent,
):
    local_rows = layer_input.shape[0]
    head_devs = lax.axis_size("head")
    per_device = HEADS // head_devs
    share = HEADS // LATENT_HEADS
    group_rows = local_rows * head_devs
    block_rows = min(512, group_rows)
    blocks = group_rows // block_rows
    scale = 1.0 / math.sqrt(HEAD_DIM + ROPE)
    query_width = per_device * HEAD_DIM
    rope_width = per_device * ROPE
    mine = lax.axis_index("head")
    boundary = second_start[0]
    inputs32 = layer_input.astype(jnp.float32)
    gain_one = mixer_gain.astype(jnp.float32)
    gain_two = feed_gain.astype(jnp.float32)
    hidden_one, inverse_one = normalize(inputs32, gain_one)
    normed_one = hidden_one.astype(jnp.bfloat16)
    local_index = mine * local_rows + jnp.arange(local_rows, dtype=jnp.int32)
    local_pos = local_index - jnp.where(local_index >= boundary, boundary, 0)
    cosine, sine = turning(local_pos, ROPE)
    query = jnp.dot(normed_one, w_query, preferred_element_type=jnp.float32).astype(jnp.bfloat16)
    turned = jnp.dot(normed_one, w_query_rope, preferred_element_type=jnp.float32).reshape(
        local_rows, HEADS, ROPE
    )
    query_rope = rotate(turned, cosine[:, None], sine[:, None]).astype(jnp.bfloat16)
    latent = jnp.dot(normed_one, w_latent, preferred_element_type=jnp.float32).astype(jnp.bfloat16)
    key_rope = rotate(
        jnp.dot(normed_one, w_key_rope, preferred_element_type=jnp.float32), cosine, sine
    ).astype(jnp.bfloat16)
    latent_three = latent.reshape(local_rows, LATENT_HEADS, LATENT)
    rope_spread = jnp.broadcast_to(key_rope[:, None], (local_rows, head_devs, ROPE))
    first_head = mine * per_device
    latent_index = first_head // share
    column = first_head % share * HEAD_DIM
    anchor = jnp.zeros((), jnp.int32)
    key_up = lax.dynamic_slice(w_key_up, (latent_index, anchor, column), (1, LATENT, query_width))[
        0
    ]
    value_up = lax.dynamic_slice(
        w_value_up, (latent_index, anchor, column), (1, LATENT, query_width)
    )[0]
    query_send = jnp.concatenate(
        [query.reshape(local_rows, head_devs, query_width), query_rope], -1
    )
    targets = np.arange(head_devs) * per_device // share
    latent_send = jnp.concatenate([latent_three[:, targets], rope_spread], -1)
    got_query, got_latent = (
        lax.all_to_all(query_send, "head", split_axis=1, concat_axis=0, tiled=True),
        lax.all_to_all(latent_send, "head", split_axis=1, concat_axis=0, tiled=True),
    )
    head_query = got_query[:, 0, :query_width].reshape(group_rows, per_device, HEAD_DIM)
    head_query_rope = got_query[:, 0, query_width:].reshape(group_rows, per_device, ROPE)
    group_latent = got_latent[:, 0, :LATENT]
    group_key_rope = got_latent[:, 0, LATENT:]
    head_key = (
        jnp.dot(group_latent, key_up, preferred_element_type=jnp.float32)
        .astype(jnp.bfloat16)
        .reshape(group_rows, per_device, HEAD_DIM)
    )
    head_value = (
        jnp.dot(group_latent, value_up, preferred_element_type=jnp.float32)
        .astype(jnp.bfloat16)
        .reshape(group_rows, per_device, HEAD_DIM)
    )
    positions = jnp.arange(group_rows, dtype=jnp.int32)
    later = positions >= boundary

    def scores(start):
        rows = start + jnp.arange(block_rows, dtype=jnp.int32)
        block_query = lax.dynamic_slice_in_dim(head_query, start, block_rows, 0)
        block_rope = lax.dynamic_slice_in_dim(head_query_rope, start, block_rows, 0)
        raw = jnp.einsum("bhd,khd->hbk", block_query, head_key, preferred_element_type=jnp.float32)
        raw = (
            raw
            + jnp.einsum(
                "bhr,kr->hbk", block_rope, group_key_rope, preferred_element_type=jnp.float32
            )
        ) * scale
        allowed = (positions[None, :] <= rows[:, None]) & (
            later[None, :] == (rows[:, None] >= boundary)
        )
        return (jnp.where(allowed[None], raw, -1e30), block_query, block_rope)

    def forward_block(start):
        masked, unused_query, unused_rope = scores(start)
        top = jnp.max(masked, -1, keepdims=True)
        weights = jnp.exp(masked - top)
        total = jnp.sum(weights, -1, keepdims=True)
        probs = (weights / total).astype(jnp.bfloat16)
        result = jnp.einsum(
            "hbk,khd->bhd", probs, head_value, preferred_element_type=jnp.float32
        ).astype(jnp.bfloat16)
        return (result, (top + jnp.log(total))[..., 0])

    starts = jnp.arange(blocks, dtype=jnp.int32) * block_rows
    head_out, log_totals = lax.map(forward_block, starts)
    returned = lax.all_to_all(
        for_sending(head_out.reshape(group_rows, 1, query_width)),
        "head",
        split_axis=0,
        concat_axis=1,
        tiled=True,
    )
    attended = returned.reshape(local_rows, HEADS * HEAD_DIM)
    middle = inputs32 + jnp.dot(attended, w_out, preferred_element_type=jnp.float32)
    hidden_two, inverse_two = normalize(middle, gain_two)
    normed_two = hidden_two.astype(jnp.bfloat16)
    gate = jnp.dot(normed_two, w_gate, preferred_element_type=jnp.float32)
    upward = jnp.dot(normed_two, w_up, preferred_element_type=jnp.float32)
    sigma = jax.nn.sigmoid(gate)
    swish = gate * sigma
    activated = (swish * upward).astype(jnp.bfloat16)
    output = (middle + jnp.dot(activated, w_down, preferred_element_type=jnp.float32)).astype(
        jnp.bfloat16
    )
    grad_act = against(cotangent, w_down)
    grad_gate = (grad_act * upward * sigma * (1.0 + gate * (1.0 - sigma))).astype(jnp.bfloat16)
    grad_upward = (grad_act * swish).astype(jnp.bfloat16)
    grad_two = against(grad_gate, w_gate) + against(grad_upward, w_up)
    grad_mid_norm, grad_gain_two = norm_back(middle, inverse_two, gain_two, grad_two)
    grad_middle = cotangent.astype(jnp.float32) + grad_mid_norm
    grad_branch = grad_middle.astype(jnp.bfloat16)
    grad_attended = against(grad_branch, w_out).astype(jnp.bfloat16)
    head_grad = lax.all_to_all(
        grad_attended.reshape(local_rows, head_devs, query_width),
        "head",
        split_axis=1,
        concat_axis=0,
        tiled=True,
    )

    def backward_block(carry, inputs):
        grad_key, grad_value, grad_key_rope = carry
        start, block_log = inputs
        masked, block_query, block_rope = scores(start)
        probs = jnp.exp(masked - block_log[..., None])
        block_grad = lax.dynamic_slice_in_dim(head_grad, start, block_rows, 0)
        grad_value = grad_value + jnp.einsum(
            "hbk,bhd->khd",
            probs.astype(jnp.bfloat16),
            block_grad,
            preferred_element_type=jnp.float32,
        )
        grad_probs = jnp.einsum(
            "bhd,khd->hbk", block_grad, head_value, preferred_element_type=jnp.float32
        )
        inner = jnp.sum(probs * grad_probs, -1, keepdims=True)
        grad_scores = (probs * (grad_probs - inner)).astype(jnp.bfloat16)
        grad_query = (
            jnp.einsum("hbk,khd->bhd", grad_scores, head_key, preferred_element_type=jnp.float32)
            * scale
        ).astype(jnp.bfloat16)
        grad_turned = (
            jnp.einsum(
                "hbk,kr->bhr", grad_scores, group_key_rope, preferred_element_type=jnp.float32
            )
            * scale
        ).astype(jnp.bfloat16)
        grad_key = (
            grad_key
            + jnp.einsum(
                "hbk,bhd->khd", grad_scores, block_query, preferred_element_type=jnp.float32
            )
            * scale
        )
        grad_key_rope = (
            grad_key_rope
            + jnp.einsum("hbk,bhr->kr", grad_scores, block_rope, preferred_element_type=jnp.float32)
            * scale
        )
        return ((grad_key, grad_value, grad_key_rope), (grad_query, grad_turned))

    initial = (
        jnp.zeros((group_rows, per_device, HEAD_DIM), jnp.float32),
        jnp.zeros((group_rows, per_device, HEAD_DIM), jnp.float32),
        jnp.zeros((group_rows, ROPE), jnp.float32),
    )
    sums_kept, per_block = lax.scan(backward_block, initial, (starts, log_totals))
    key_grad_low = sums_kept[0].astype(jnp.bfloat16).reshape(group_rows, query_width)
    value_grad_low = sums_kept[1].astype(jnp.bfloat16).reshape(group_rows, query_width)
    query_back = jnp.concatenate(
        [
            per_block[0].reshape(group_rows, query_width),
            per_block[1].reshape(group_rows, rope_width),
        ],
        -1,
    )[:, None]
    got_qgrad = lax.all_to_all(query_back, "head", split_axis=0, concat_axis=1, tiled=True)
    grad_kup = lax.dynamic_update_slice(
        jnp.zeros(w_key_up.shape, jnp.float32),
        across(group_latent, key_grad_low)[None],
        (latent_index, anchor, column),
    )
    grad_vup = lax.dynamic_update_slice(
        jnp.zeros(w_value_up.shape, jnp.float32),
        across(group_latent, value_grad_low)[None],
        (latent_index, anchor, column),
    )
    grad_group_latent = against(key_grad_low, key_up) + against(value_grad_low, value_up)
    latent_back = jnp.concatenate([grad_group_latent, sums_kept[2]], -1)[:, None]
    got_lgrad = lax.all_to_all(
        latent_back.astype(jnp.bfloat16), "head", split_axis=0, concat_axis=1, tiled=True
    ).astype(latent_back.dtype)
    grouped = jnp.sum(
        got_lgrad.reshape(local_rows, LATENT_HEADS, head_devs // LATENT_HEADS, LATENT + ROPE), 2
    )
    grad_latent = (
        grouped[:, :, :LATENT].reshape(local_rows, LATENT_HEADS * LATENT).astype(jnp.bfloat16)
    )
    grad_kturn = lax.optimization_barrier(
        jnp.sum(grouped[:, :, LATENT:], 1).astype(jnp.bfloat16)
    ).astype(jnp.float32)
    grad_query_all = got_qgrad[:, :, :query_width].reshape(local_rows, HEADS * HEAD_DIM)
    grad_qturn = got_qgrad[:, :, query_width:].reshape(local_rows, HEADS, ROPE).astype(jnp.float32)
    grad_qrope = (
        rotate(grad_qturn, cosine[:, None], -sine[:, None])
        .astype(jnp.bfloat16)
        .reshape(local_rows, HEADS * ROPE)
    )
    grad_kpre = rotate(grad_kturn, cosine, -sine).astype(jnp.bfloat16)
    grad_wkr = across(normed_one, grad_kpre)
    grad_one = (
        against(grad_query_all, w_query)
        + against(grad_qrope, w_query_rope)
        + against(grad_latent, w_latent)
        + against(grad_kpre, w_key_rope)
    )
    grad_in_norm, grad_gain_one = norm_back(inputs32, inverse_one, gain_one, grad_one)
    grad_input = grad_middle + grad_in_norm
    parts = sum_gradients(
        (normed_two, normed_one, normed_two, attended, cotangent, normed_one),
        (grad_gate, grad_query_all, grad_upward, grad_branch, activated, grad_qrope, grad_latent),
    )
    summed = (
        lax.psum_scatter(grad_gain_one, ("seq", "head"), scatter_dimension=0, tiled=True),
        parts[0, :, 2816:],
        parts[2, :, 2816:3328],
        parts[2, :, 3328:],
        lax.psum_scatter(grad_wkr, ("seq", "head"), scatter_dimension=0, tiled=True),
        lax.psum_scatter(grad_kup, ("seq", "head"), scatter_dimension=2, tiled=True),
        lax.psum_scatter(grad_vup, ("seq", "head"), scatter_dimension=2, tiled=True),
        parts[1, :, 2816:],
        lax.psum_scatter(grad_gain_two, ("seq", "head"), scatter_dimension=0, tiled=True),
        parts[0, :, :2816],
        parts[1, :, :2816],
        parts[2, :, :2816].T,
    )
    return (
        output,
        grad_input,
        summed[0],
        summed[1],
        summed[2],
        summed[3],
        summed[4],
        summed[5],
        summed[6],
        summed[7],
        summed[8],
        summed[9],
        summed[10],
        summed[11],
    )


def solution(mesh):
    in_specs = (
        P(("seq", "head"), None),
        P("seq"),
        P(),
        P(),
        P(),
        P(),
        P(),
        P(),
        P(),
        P(),
        P(),
        P(),
        P(),
        P(),
        P(("seq", "head"), None),
    )
    out_specs = (
        P(("seq", "head"), None),
        P(("seq", "head"), None),
        P(("seq", "head")),
        P(("seq", "head"), None),
        P(("seq", "head"), None),
        P(("seq", "head"), None),
        P(("seq", "head"), None),
        P(None, None, ("seq", "head")),
        P(None, None, ("seq", "head")),
        P(("seq", "head"), None),
        P(("seq", "head")),
        P(("seq", "head"), None),
        P(("seq", "head"), None),
        P(None, ("seq", "head")),
    )
    return jax.shard_map(body, mesh=mesh, in_specs=in_specs, out_specs=out_specs, check_vma=False)
```

```python
import math
import types
import numpy as np
import jax
import jax.numpy as jnp
from jax import lax
from jax.experimental import pallas as pl
from jax.experimental.pallas import tpu as pltpu
from jax.sharding import PartitionSpec as P

MESH = pl.DeviceIdType.MESH
bf, f32 = jnp.bfloat16, jnp.float32
W = 256
EPS = 1e-6
SCALE = 1.0 / math.sqrt(96)
DEPTH = 4


def dot(a, b, ca=1, cb=0):
    return lax.dot_general(a, b, (((ca,), (cb,)), ((), ())), preferred_element_type=f32)


def place():
    s, h = lax.axis_index("seq"), lax.axis_index("head")
    return {"y": s // 2, "core": s % 2, "z": h // 4, "x": h % 4}


def device(at):
    return (at["y"] * 2 + at["core"], at["z"] * 4 + at["x"])


def remote(src, dst, send, recv, to):
    return pltpu.make_async_remote_copy(
        src_ref=src, dst_ref=dst, send_sem=send, recv_sem=recv, device_id=to, device_id_type=MESH
    )


def lanes(start, size):
    return pl.ds(pl.multiple_of(start, size), size)


def rows_of(block):
    return pl.ds(pl.multiple_of((block % 2) * 128, 128), 128)


def turn(u, cosine, sine):
    first, second = u[..., :16, :], u[..., 16:, :]
    return jnp.concatenate([first * cosine - second * sine, first * sine + second * cosine], -2)


def load_first(r, again=False):
    for i in range(2):
        pltpu.make_async_copy(r.wq.at[:, i * 512 : (i + 1) * 512], r.pool.at[i], r.first_sem.at[i]).start()
    pltpu.make_async_copy(r.wqr, r.pool.at[2], r.first_sem.at[2]).start()
    pltpu.make_async_copy(r.wl, r.pool.at[3], r.first_sem.at[3]).start()
    if not again:
        pltpu.make_async_copy(r.wo_hbm, r.wo, r.first_sem.at[4]).start()


def wait_first(r, i):
    ref = r.wo if i == 4 else r.pool.at[i]
    pltpu.make_async_copy(ref, ref, r.first_sem.at[i]).wait()


def chunk_copies(r, j):
    slot = j % DEPTH
    here = lanes(j * W, W)
    return (
        pltpu.make_async_copy(r.wg.at[:, here], r.pool.at[slot, :, 0:W], r.chunk_sem.at[slot, 0]),
        pltpu.make_async_copy(r.wu.at[:, here], r.pool.at[slot, :, W : 2 * W], r.chunk_sem.at[slot, 1]),
        pltpu.make_async_copy(r.wd.at[here, :], r.wdpool.at[slot], r.chunk_sem.at[slot, 2]),
    )


def project(r, seq, h):
    x = r.x[...].astype(f32)
    inverse = lax.rsqrt(jnp.mean(x * x, -1, keepdims=True) + EPS)
    n1 = (x * inverse * r.gain1[...].astype(f32)).astype(bf)
    r.n1[...] = n1
    bound = r.second[0]
    token = h * 128 + lax.broadcasted_iota(jnp.int32, (16, 128), 1)
    position = token - jnp.where(token >= bound, bound, 0)
    angle = position.astype(f32) * r.freq[...]
    cosine, sine = jnp.cos(angle), jnp.sin(angle)
    r.cos[...], r.sin[...] = cosine, sine
    wait_first(r, 3)
    lat = dot(n1, r.pool[3]).astype(bf)
    kr = turn(dot(r.wkr[...], n1, 1, 1), cosine, sine)
    flag = jnp.where(h == 15, 0.0, 1.0)
    flags = jnp.where(lax.broadcasted_iota(jnp.int32, (96, 128), 0) == 0, flag, 0.0)
    own = jnp.concatenate([kr, flags], 0).T.astype(bf)
    b = h // 2
    mine = r.lx.at[b, rows_of(h)]
    mine[:, 0:256] = lat[:, 0:256]
    mine[:, 256:384] = own
    mine[:, 384:640] = lat[:, 256:512]

    @pl.when(h % 2 == 0)
    def _():
        r.lx[b, 128:256] = jnp.zeros((128, 640), bf)

    for k in range(1, 16):
        @pl.when(h + k < 16)
        def _():
            remote(mine, mine, r.gather_send.at[k], r.gather_recv.at[h], (seq, h + k)).start()

    for i in range(2):
        wait_first(r, i)
        r.qt[i * 512 : (i + 1) * 512] = dot(n1, r.pool[i]).T.astype(bf)
    wait_first(r, 2)
    qr = (turn(dot(n1, r.pool[2]).T.reshape(16, 32, 128), cosine, sine) * SCALE).astype(bf)
    for j in range(DEPTH):
        for copy in chunk_copies(r, j):
            copy.start()
    late = (h * 128 + (lax.broadcasted_iota(jnp.int32, (96, 1024), 1) & 127)) >= bound
    bias = jnp.where(late & (lax.broadcasted_iota(jnp.int32, (96, 1024), 0) == 0), -1e30, 0.0).astype(bf)
    for g in range(2):
        kt = r.kup[g].T
        r.kt[g] = kt
        r.vt[g] = r.vup[g].T
        at, rope = (0, 256) if g == 0 else (128, 0)
        r.qxt[g, rope + 32 : rope + 128] = bias
        for e in range(8):
            head = g * 8 + e
            cols = slice(e * 128, (e + 1) * 128)
            r.qxt[g, rope : rope + 32, cols] = qr[head]
            r.qxt[g, at : at + 256, cols] = (
                dot(r.kt[g, e * 64 : (e + 1) * 64, :], r.qt[head * 64 : (head + 1) * 64], 0, 0) * SCALE
            ).astype(bf)


def gather_wait(r, seq, h, i):
    ref = r.lx.at[i // 2, rows_of(i)]

    @pl.when(i < h)
    def _():
        remote(ref, ref, r.gather_send.at[0], r.gather_recv.at[i], (seq, 0)).wait_recv()


def attend_step(r, seq, h, b, diag):
    gather_wait(r, seq, h, 2 * b)
    gather_wait(r, seq, h, 2 * b + 1)
    r.lxt[...] = r.lx[b].T
    if diag:
        bound = r.second[0]
        key = b * 256 + lax.broadcasted_iota(jnp.int32, (256, 128), 0)
        row = h * 128 + lax.broadcasted_iota(jnp.int32, (256, 128), 1)
        ok = (key <= row) & ((key >= bound) == (row >= bound))
        mask = jnp.where(ok, 0.0, 1.0)
        mask = jnp.concatenate([mask, mask], 1)
    for g in range(2):
        at = 0 if g == 0 else 384
        for c in range(4):
            cols = slice(c * 256, (c + 1) * 256)
            s = dot(r.lx[b, :, g * 256 : g * 256 + 384], r.qxt[g, :, cols])
            if diag:
                s = jnp.where(mask > 0.5, -1e30, s)
            top = jnp.max(s, 0, keepdims=True)
            if not diag:
                before = r.top[g : g + 1, cols]
                top = jnp.maximum(top, before)
            p = jnp.exp(s - top)
            total = jnp.sum(p, 0, keepdims=True)
            pb = p.astype(bf)
            r.p[b, g, :, cols] = pb
            o = dot(r.lxt[at : at + 256], pb)
            if not diag:
                fade = jnp.exp(before - top)
                total = total + r.total[g : g + 1, cols] * fade
                o = o + r.acc[g, 0:256, cols] * fade
            r.acc[g, 0:256, cols] = o
            r.total[g : g + 1, cols] = total
            r.top[g : g + 1, cols] = top
            r.tops[b, g : g + 1, cols] = top


def attend(r, seq, h):
    last = h // 2
    attend_step(r, seq, h, last, True)

    @pl.loop(0, last)
    def _(i):
        attend_step(r, seq, h, last - 1 - i, False)

    for g in range(2):
        back = 1.0 / r.total[g : g + 1]
        r.back[g : g + 1] = back
        r.ot[g] = (r.acc[g, 0:256] * back).astype(bf)
        for e in range(8):
            head = g * 8 + e
            r.attt[head * 64 : (head + 1) * 64] = dot(
                r.vt[g, e * 64 : (e + 1) * 64], r.ot[g, :, e * 128 : (e + 1) * 128]
            ).astype(bf)
    r.att[...] = r.attt[...].T


def feed(r, begin, each):
    wait_first(r, 4)
    r.mid[...] = r.x[...].astype(f32) + dot(r.att[...], r.wo[...])
    mid = r.mid[...]
    inverse = lax.rsqrt(jnp.mean(mid * mid, -1, keepdims=True) + EPS)
    gain = r.gain2[...].astype(f32)
    r.n2[...] = (mid * inverse * gain).astype(bf)
    r.grad_input[...] = mid
    r.g_acc[...] = jnp.zeros((128, 1024), f32)
    begin()

    @pl.loop(0, 11)
    def _(j):
        slot = j % DEPTH
        for copy in chunk_copies(r, j):
            copy.wait()
        n2, cot = r.n2[...], r.cot[...]
        gate = dot(n2, r.pool[slot, :, 0:W])
        up = dot(n2, r.pool[slot, :, W : 2 * W])
        grad = dot(cot, r.wdpool[slot], 1, 1)
        sigma = jax.nn.sigmoid(gate)
        swish = gate * sigma
        act = (swish * up).astype(bf)
        grad_gate = (grad * up * sigma * (1.0 + gate * (1.0 - sigma))).astype(bf)
        grad_up = (grad * swish).astype(bf)
        r.grad_input[...] += dot(act, r.wdpool[slot])
        r.g_acc[...] += dot(grad_gate, r.pool[slot, :, 0:W], 1, 1) + dot(grad_up, r.pool[slot, :, W : 2 * W], 1, 1)

        @pl.when(j + DEPTH < 11)
        def _():
            for copy in chunk_copies(r, j + DEPTH):
                copy.start()

        each(j, grad_gate, grad_up, act)

    r.output[...] = r.grad_input[...].astype(bf)
    up = r.g_acc[...]
    mid = r.mid[...]
    inverse = lax.rsqrt(jnp.mean(mid * mid, -1, keepdims=True) + EPS)
    r.gains[1:2] = jnp.sum(up * mid * inverse, 0, keepdims=True)
    scaled = up * gain
    grad_mid = r.cot[...].astype(f32) + inverse * scaled - mid * (inverse * inverse * inverse) * jnp.mean(mid * scaled, -1, keepdims=True)
    r.mid[...] = grad_mid
    r.gb[...] = grad_mid.astype(bf)
    r.ga[...] = dot(r.gb[...], r.wo[...], 1, 1).T.astype(bf)


RING = 4
ORDERS = (("y", "z", "x"), ("z", "x", "y"), ("x", "y", "z"))
EARLY = (12, 13, 13)
JOBS = 16
FEED, OUT, ONE = 0, 1, 2
PHASES = ("a", "b", "c", "d", "e", "f")


def beside(at, axis, step):
    return device({**at, axis: (at[axis] + step) % 4})


def other_core(at):
    return device({**at, "core": 1 - at["core"]})


def choose_rows(r, me, order, which):
    for mine in (True, False):
        core = me["core"] if mine else 1 - me["core"]
        parts = []
        for i in range(64):
            part = dict(zip(ORDERS[order], (i >> 4, (i >> 2) & 3, i & 3)))
            start = part["y"] * 256 + part["z"] * 32 + part["x"] * 8
            parts.append(r.nt[pl.ds(pl.multiple_of(core * 128 + start, 8), 8), :])
        picked = jnp.concatenate(parts, 0).astype(bf)
        if mine:
            r.at[order, which, :, 0:128] = picked
        else:
            r.at_send[order, which] = picked
    at_copy(r, me, order, which).start()


def at_copy(r, me, order, which):
    return remote(
        r.at_send.at[order, which], r.at.at[order, which, :, 128:256],
        r.at_sem.at[0, order, which], r.at_sem.at[1, order, which], other_core(me),
    )


def g_copy(r, me, order, job):
    return remote(
        r.g.at[order, job, 0:128], r.g.at[order, job, 128:256],
        r.g_send.at[order, job], r.g_recv.at[order, job], other_core(me),
    )


def give(r, me, order, job, value):
    r.g[order, job, 0:128] = value
    g_copy(r, me, order, job).start()


def dense_copy(r, me, which):
    return remote(
        r.dense_send.at[which], r.dense.at[which, :, 128:256],
        r.dense_sem.at[0, which], r.dense_sem.at[1, which], other_core(me),
    )


def give_heads(r, me, which, left, right):
    for mine in (True, False):
        core = me["core"] if mine else 1 - me["core"]
        for q in range(4):
            for g in range(2):
                e = q * 2 + core
                rows = lanes((g * 8 + e) * 64, 64)
                block = dot(left[rows, :], right[g, :, lanes(e * 128, 128)], 1, 1).astype(bf)
                if mine:
                    r.dense[which, q, g * 64 : g * 64 + 64] = block
                else:
                    r.dense_send[which, q, g * 64 : g * 64 + 64] = block
    dense_copy(r, me, which).start()


def message(r, me, order, phase, way, job):
    slot = job % RING
    kind = PHASES[phase]
    return remote(
        getattr(r, "s" + kind).at[order, slot, way],
        getattr(r, "r" + kind).at[order, slot, way],
        r.sum_send.at[order, phase, way, slot],
        r.sum_recv.at[order, phase, way, slot],
        beside(me, ORDERS[order][phase // 2], 1 if way == 0 else -1),
    )


def first_half(r, me, order, stage, job, block):
    phase = stage * 2

    @pl.when(job >= RING)
    def _():
        for way in (0, 1):
            message(r, me, order, phase, way, job - RING).wait_send()

    ref = getattr(r, "s" + PHASES[phase])
    for way in (0, 1):
        half = block[:, way * (W // 2) : (way + 1) * (W // 2)]
        ref[order, job % RING, way] = half.astype(ref.dtype)
        message(r, me, order, phase, way, job).start()


def second_half(r, me, order, stage, job, block_of):
    phase = stage * 2 + 1

    @pl.when(job >= RING)
    def _():
        for way in (0, 1):
            message(r, me, order, phase, way, job - RING).wait_send()

    ref, got = getattr(r, "s" + PHASES[phase]), getattr(r, "r" + PHASES[phase - 1])
    slot = job % RING
    for way in (0, 1):
        message(r, me, order, phase - 1, way, job).wait_recv()
        block = block_of(1 if way == 0 else -1)
        here = slice(way * (W // 2), (way + 1) * (W // 2))
        there = slice((1 - way) * (W // 2), (2 - way) * (W // 2))
        ref[order, slot, way, :, here] = (block[:, here] + got[order, slot, way].astype(f32)).astype(ref.dtype)
        ref[order, slot, way, :, there] = block[:, there].astype(ref.dtype)
        message(r, me, order, phase, way, job).start()


def total(r, me, order, stage, job, block):
    phase = stage * 2 + 1
    got = getattr(r, "r" + PHASES[phase])
    for way in (0, 1):
        message(r, me, order, phase, way, job).wait_recv()
        block = block + got[order, job % RING, way].astype(f32)
    return block


def block_of(r, me, order, stage, job):
    axis = ORDERS[order][stage]
    slot = job % RING

    def get(step):
        index = (me[axis] + step) % 4
        if stage == 0:
            return r.d[order, slot, lanes(index * 128, 128), :].astype(f32)
        if stage == 1:
            return r.s1[order, slot, lanes(index * 32, 32), :]
        return r.s2[order, slot, lanes(index * 8, 8), :]

    return get


def products(r, me, order, job, late):
    slot = job % RING

    def plain(which):
        g_copy(r, me, order, job).wait_recv()
        r.d[order, slot] = dot(r.at[order, which], r.g[order, job]).astype(bf)

    def thick(which):
        dense_copy(r, me, which).wait_recv()
        row = lax.broadcasted_iota(jnp.int32, (128, 256), 0)
        column = lax.broadcasted_iota(jnp.int32, (128, 256), 1) & 127
        if which < 2:
            row = ((row >> 2) & 1) * 64 + (row >> 3) * 4 + (row & 3)
        pick = (row == column).astype(bf)
        for q in range(4):
            r.d[order, slot, q * 128 : (q + 1) * 128] = dot(pick, r.dense[which, q]).astype(bf)

    if order == 0:
        if late:
            pl.when(job == 12)(lambda: thick(1))
            pl.when((job == 13) | (job == 14))(lambda: plain(ONE))
            pl.when(job == 15)(lambda: thick(2))
        else:
            pl.when(job < 11)(lambda: plain(FEED))
            pl.when(job == 11)(lambda: thick(0))
    elif late:
        plain(ONE)
    else:
        plain(jnp.where(job < 11, FEED, OUT))


def sum_step(r, me, order, k, job, late):
    get = block_of(r, me, order, min(k // 2, 2), job)
    if k == 0:
        products(r, me, order, job, late)
        first_half(r, me, order, 0, job, get(2))
    elif k % 2:
        second_half(r, me, order, k // 2, job, get)
    elif k == 2:
        r.s1[order, job % RING] = total(r, me, order, 0, job, block_of(r, me, order, 0, job)(0))
        first_half(r, me, order, 1, job, get(2))
    elif k == 4:
        r.s2[order, job % RING] = total(r, me, order, 1, job, block_of(r, me, order, 1, job)(0))
        first_half(r, me, order, 2, job, get(2))
    else:
        own = block_of(r, me, order, 2, job)(0)
        r.sums[order, :, lanes(job * W, W)] = total(r, me, order, 2, job, own)


def sum_slot(r, me, t, late=False):
    for k in reversed(range(7)):
        for order in range(3):
            base = EARLY[order] if late else 0
            end = JOBS if late else EARLY[order]
            job = base + t - 1 - k

            @pl.when((job >= base) & (job < end))
            def _():
                sum_step(r, me, order, k, job, late)


def sum_end(r, me):
    for order in range(3):
        for phase in range(6):
            for way in (0, 1):
                for job in range(JOBS - RING, JOBS):
                    message(r, me, order, phase, way, job).wait_send()
        for job in range(JOBS):
            if order or job < 11 or job in (13, 14):
                g_copy(r, me, order, job).wait_send()
        for which in (FEED, OUT, ONE):
            if order or which != OUT:
                at_copy(r, me, order, which).wait_send()
    for which in range(3):
        dense_copy(r, me, which).wait_send()


def wait_rows(r, me, which):
    for order in range(3):
        if order or which != OUT:
            at_copy(r, me, order, which).wait_recv()


def prepare_back(r):
    for g in range(2):
        r.qxn[g] = r.qxt[g].T
        for e in range(8):
            head = g * 8 + e
            cols = slice(e * 128, (e + 1) * 128)
            ga = r.ga[head * 64 : (head + 1) * 64]
            back = r.back[g : g + 1, cols]
            inner = jnp.sum(ga.astype(f32) * r.attt[head * 64 : (head + 1) * 64].astype(f32), 0, keepdims=True)
            r.inner[g : g + 1, cols] = inner * back
            r.dt[g, :, cols] = (dot(r.vt[g, e * 64 : (e + 1) * 64, :], ga, 0, 0) * back).astype(bf)
        r.dn[g] = r.dt[g].T
    r.acc[...] = jnp.zeros((2, 384, 1024), f32)


def latent_copy(r, seq, h, b, s):
    slot = b % 4
    return remote(
        r.wdpool.at[slot, s * 128 : s * 128 + 128, 0:640], r.lg.at[h],
        r.lg_send.at[slot, s], r.lg_recv.at[h], (seq, b * 2 + s),
    )


def back_step(r, seq, h, b):
    @pl.when(b >= 4)
    def _():
        for s in (0, 1):
            latent_copy(r, seq, h, b - 4, s).wait_send()

    slot = b % 4
    r.lxt[...] = r.lx[b].T
    rope = None
    for g in range(2):
        at = 0 if g == 0 else 384
        for c in range(4):
            cols = slice(c * 256, (c + 1) * 256)
            fade = jnp.exp(r.tops[b, g : g + 1, cols] - r.top[g : g + 1, cols])
            p = r.p[b, g, :, cols].astype(f32) * fade
            dp = dot(r.lx[b, :, at : at + 256], r.dt[g, :, cols])
            r.ds[:, cols] = (p * (dp - r.inner[g : g + 1, cols])).astype(bf)
            r.pf[:, cols] = p.astype(bf)
        ds = r.ds[...]
        gl = dot(ds, r.qxn[g])
        gp = dot(r.pf[...], r.dn[g])
        r.acc[g] += dot(r.lxt[g * 256 : g * 256 + 384], ds)
        if g == 0:
            left = gl[:, 0:256] + gp
            rope = gl[:, 256:384]
        else:
            rope = rope + gl[:, 0:128]
            right = gl[:, 128:384] + gp
    whole = jnp.concatenate([left, rope, right], 1)
    r.wdpool[slot, :, 0:640] = whole.astype(bf)
    for s in (0, 1):
        @pl.when(2 * b + s < h)
        def _():
            latent_copy(r, seq, h, b, s).start()

        @pl.when(2 * b + s == h)
        def _():
            r.own[...] = whole[s * 128 : s * 128 + 128]


def back_end(r, seq, h):
    last = h // 2
    for d in range(4):
        b = last - d
        for s in (0, 1):
            @pl.when((b >= 0) & (2 * b + s < h))
            def _():
                latent_copy(r, seq, h, b, s).wait_send()


def finish_queries(r, me):
    for g in range(2):
        at, rope = (0, 256) if g == 0 else (128, 0)
        r.ot[g] = (r.acc[g, at : at + 256] * SCALE).astype(bf)
        for e in range(8):
            head = g * 8 + e
            cols = slice(e * 128, (e + 1) * 128)
            r.attt[head * 64 : (head + 1) * 64] = dot(r.kt[g, e * 64 : (e + 1) * 64], r.ot[g, :, cols]).astype(bf)
            turned = (r.acc[g, rope : rope + 32, cols] * SCALE).astype(bf).astype(f32)
            r.nt[head * 32 : (head + 1) * 32] = turn(turned, r.cos[...], -r.sin[...])
    r.n2[...] = r.attt[...].T
    r.gb[:, 0:512] = r.nt[0:512].T.astype(bf)
    for c in range(3):
        give(r, me, 1, 13 + c, r.n2[:, c * 256 : (c + 1) * 256])
    give(r, me, 2, 13, r.n2[:, 768:1024])
    for c in range(2):
        give(r, me, 0, 13 + c, r.gb[:, c * 256 : (c + 1) * 256])
    give_heads(r, me, 1, r.qt, r.ot)


def finish_latent(r, me, seq, h):
    @pl.loop(0, 16)
    def _(j):
        @pl.when(j > h)
        def _():
            remote(r.lg.at[j], r.lg.at[j], r.lg_send.at[0, 0], r.lg_recv.at[j], (seq, 0)).wait_recv()
            r.own[...] += r.lg[j].astype(f32)

    r.gb[:, 512:768] = r.own[:, 0:256].astype(bf)
    r.gb[:, 768:1024] = r.own[:, 384:640].astype(bf)
    for c in range(2):
        give(r, me, 2, 14 + c, r.gb[:, 512 + c * 256 : 768 + c * 256])
    turned = r.own[:, 256:384].astype(bf).astype(f32).T[0:32]
    kr = turn(turned, r.cos[...], -r.sin[...])
    r.gkr[...] = jnp.concatenate([kr, jnp.zeros((96, 128), f32)], 0).T.astype(bf)


def finish_input(r):
    grad = dot(r.gkr[:, 0:32], r.wkr[...])
    for i in range(2):
        grad = grad + dot(r.n2[:, i * 512 : (i + 1) * 512], r.pool[i], 1, 1)
    grad = grad + dot(r.gb[:, 0:512], r.pool[2], 1, 1) + dot(r.gb[:, 512:1024], r.pool[3], 1, 1)
    x = r.x[...].astype(f32)
    inverse = lax.rsqrt(jnp.mean(x * x, -1, keepdims=True) + EPS)
    r.gains[0:1] = jnp.sum(grad * x * inverse, 0, keepdims=True)
    scaled = grad * r.gain1[...].astype(f32)
    r.grad_input[...] = r.mid[...] + inverse * scaled - x * (inverse * inverse * inverse) * jnp.mean(x * scaled, -1, keepdims=True)


def finish_rope(r, me):
    wide = jnp.concatenate([r.gkr[...], jnp.zeros((128, 128), bf)], 1)
    row = lax.broadcasted_iota(jnp.int32, (16, 256), 0)
    column = lax.broadcasted_iota(jnp.int32, (16, 256), 1)
    spread = ((row < 4) & (column == 32 + row // 2)).astype(bf)
    for mine in (True, False):
        core = me["core"] if mine else 1 - me["core"]
        for q in range(4):
            gains = r.gains[0:2, lanes(q * 256 + core * 128, 128)]
            high = gains.astype(bf).astype(f32)
            low = gains - high
            stack = jnp.concatenate([high[0:1], low[0:1], high[1:2], low[1:2], jnp.zeros((12, 128), f32)], 0).astype(bf)
            left = r.at[0, ONE, q * 128 : (q + 1) * 128, 0:128] if mine else r.at_send[0, ONE, q * 128 : (q + 1) * 128]
            block = (dot(left, wide) + dot(stack, spread, 0, 0)).astype(bf)
            if mine:
                r.dense[2, q, 0:128] = block
            else:
                r.dense_send[2, q] = block
    dense_copy(r, me, 2).start()


INPUTS = ("x", "cot", "second", "gain1", "gain2", "freq", "wkr", "kup", "vup", "wq", "wqr", "wl", "wo_hbm", "wg", "wu", "wd")


def scratch():
    vm = lambda *shape, kind=bf: pltpu.VMEM(shape, kind)
    dma = pltpu.SemaphoreType.DMA
    return dict(
        pool=vm(4, 1024, 512), wdpool=vm(4, 256, 1024), wo=vm(1024, 1024),
        first_sem=dma((5,)), chunk_sem=dma((4, 3)),
        n1=vm(128, 1024), n2=vm(128, 1024), gb=vm(128, 1024), ga=vm(1024, 128), att=vm(128, 1024), attt=vm(1024, 128),
        cos=vm(16, 128, kind=f32), sin=vm(16, 128, kind=f32),
        lx=vm(8, 256, 640), lxt=vm(640, 256), qt=vm(1024, 128), kt=vm(2, 512, 256), vt=vm(2, 512, 256),
        qxt=vm(2, 384, 1024), p=vm(8, 2, 256, 1024), acc=vm(2, 384, 1024, kind=f32), ot=vm(2, 256, 1024),
        top=vm(8, 1024, kind=f32), total=vm(8, 1024, kind=f32), back=vm(8, 1024, kind=f32), tops=vm(8, 8, 1024, kind=f32),
        gains=vm(8, 1024, kind=f32), mid=vm(128, 1024, kind=f32), g_acc=vm(128, 1024, kind=f32),
        gather_send=dma((16,)), gather_recv=dma((16,)),
        nt=vm(1024, 128, kind=f32), qxn=vm(2, 1024, 384), dt=vm(2, 256, 1024), dn=vm(2, 1024, 256),
        inner=vm(8, 1024, kind=f32), ds=vm(256, 1024), pf=vm(256, 1024), own=vm(128, 640, kind=f32), lg=vm(16, 128, 640),
        lg_send=dma((4, 2)), lg_recv=dma((16,)),
        gkr=vm(128, 128),
        at=vm(3, 3, 512, 256), at_send=vm(3, 3, 512, 128), at_sem=dma((2, 3, 3)),
        g=vm(3, JOBS, 256, W), g_send=dma((3, JOBS)), g_recv=dma((3, JOBS)),
        dense=vm(3, 4, 256, W), dense_send=vm(3, 4, 128, W), dense_sem=dma((2, 3)),
        d=vm(3, RING, 512, W), s1=vm(3, RING, 128, W, kind=f32), s2=vm(3, RING, 32, W, kind=f32),
        sum_send=dma((3, 6, 2, RING)), sum_recv=dma((3, 6, 2, RING)),
        **{
            side + name: vm(3, RING, 2, rows, width, kind=kind)
            for side in "sr"
            for name, rows, width, kind in (
                ("a", 128, W // 2, bf), ("b", 128, W, bf), ("c", 32, W // 2, bf),
                ("d", 32, W, bf), ("e", 8, W // 2, f32), ("f", 8, W, f32),
            )
        },
    )


def kernel(names, *refs):
    r = types.SimpleNamespace(**dict(zip(names, refs)))
    seq, h = lax.axis_index("seq"), lax.axis_index("head")
    me = place()
    load_first(r)
    barrier = pltpu.get_barrier_semaphore()
    peers = [(seq, (h + k) % 16) for k in range(1, 16)] + [other_core(me), beside(me, "y", 1), beside(me, "y", -1)]
    for peer in peers:
        pl.semaphore_signal(barrier, inc=1, device_id=peer, device_id_type=MESH)
    pl.semaphore_wait(barrier, len(peers))
    project(r, seq, h)
    r.nt[...] = r.cot[...].astype(f32).T
    choose_rows(r, me, 2, FEED)
    r.nt[...] = r.n1[...].astype(f32).T
    for order in range(3):
        choose_rows(r, me, order, ONE)
    attend(r, seq, h)
    r.nt[...] = r.attt[...].astype(f32)
    for order in (1, 2):
        choose_rows(r, me, order, OUT)

    def each(j, grad_gate, grad_up, act):
        for order, value in enumerate((grad_gate, grad_up, act)):
            give(r, me, order, j, value)
        sum_slot(r, me, j)

    def begin():
        r.nt[...] = r.n2[...].astype(f32).T
        for order in (0, 1):
            choose_rows(r, me, order, FEED)
        wait_rows(r, me, FEED)

    feed(r, begin, each)
    load_first(r, again=True)
    for c in range(2):
        give(r, me, 1, 11 + c, r.gb[:, c * 256 : (c + 1) * 256])
        give(r, me, 2, 11 + c, r.gb[:, 512 + c * 256 : 768 + c * 256])
    give_heads(r, me, 0, r.ga, r.ot)
    wait_rows(r, me, OUT)
    sum_slot(r, me, 11)
    prepare_back(r)

    @pl.loop(0, 8)
    def _(b):
        @pl.when(b <= h // 2)
        def _():
            back_step(r, seq, h, b)

        sum_slot(r, me, 12 + b)

    wait_rows(r, me, ONE)
    finish_queries(r, me)
    sum_slot(r, me, 1, True)
    finish_latent(r, me, seq, h)
    sum_slot(r, me, 2, True)
    for i in range(4):
        wait_first(r, i)
    finish_input(r)
    finish_rope(r, me)

    @pl.loop(3, 11)
    def _(t):
        sum_slot(r, me, t, True)

    sum_end(r, me)
    back_end(r, seq, h)
    for k in range(1, 16):
        @pl.when(h + k < 16)
        def _():
            ref = r.lx.at[h // 2, rows_of(h)]
            remote(ref, ref, r.gather_send.at[k], r.gather_recv.at[h], (seq, h)).wait_send()


def run(layer_input, second_start, mixer_gain, w_query, w_query_rope, w_latent, w_key_rope, w_key_up, w_value_up, w_out, feed_gain, w_gate, w_up, w_down, cotangent):
    freq = jnp.broadcast_to((10000.0 ** (-jnp.arange(16, dtype=f32) * 2.0 / 32))[:, None], (16, 128))
    args = dict(x=layer_input, cot=cotangent, second=second_start, gain1=mixer_gain[None], gain2=feed_gain[None], freq=freq,
        wkr=w_key_rope.T, kup=w_key_up, vup=w_value_up, wq=w_query, wqr=w_query_rope, wl=w_latent, wo_hbm=w_out, wg=w_gate, wu=w_up, wd=w_down)
    V, A, S = (pl.BlockSpec(memory_space=m) for m in (pltpu.VMEM, pl.ANY, pltpu.SMEM))
    specs = {n: V for n in INPUTS}
    specs["second"] = S
    for n in ("wq", "wqr", "wl", "wo_hbm", "wg", "wu", "wd"):
        specs[n] = A
    outs = dict(output=((128, 1024), bf), grad_input=((128, 1024), f32), sums=((3, 8, JOBS * W), f32))
    sc = scratch()
    names = INPUTS + tuple(outs) + tuple(sc)
    output, grad_input, sums = pl.pallas_call(
        lambda *refs: kernel(names, *refs),
        out_shape=[jax.ShapeDtypeStruct(*o) for o in outs.values()],
        in_specs=[specs[n] for n in INPUTS], out_specs=[V] * len(outs),
        scratch_shapes=list(sc.values()),
        compiler_params=pltpu.CompilerParams(collective_id=0, has_side_effects=True, vmem_limit_bytes=66900000),
        name="layer",
    )(*[args[n] for n in INPUTS])

    first, second, third = sums[0], sums[1], sums[2]

    def heads(block):
        return block.reshape(2, 4, 256).transpose(0, 2, 1)

    rope = first[:, 3840:]
    return (
        output,
        grad_input,
        rope[:, 32],
        jnp.concatenate([second[:, 3328:], third[:, 3328:3584]], 1),
        first[:, 3328:3840],
        third[:, 3584:],
        rope[:, :32],
        heads(first[:, 3072:3328]),
        heads(first[:, 2816:3072]),
        jnp.concatenate([second[:, 2816:3328], third[:, 2816:3328]], 1),
        rope[:, 33],
        first[:, :2816],
        second[:, :2816],
        third[:, :2816].T,
    )


def solution(mesh):
    in_specs = (
        P(("seq", "head"), None),
        P("seq"),
        P(),
        P(),
        P(),
        P(),
        P(),
        P(),
        P(),
        P(),
        P(),
        P(),
        P(),
        P(),
        P(("seq", "head"), None),
    )
    out_specs = (
        P(("seq", "head"), None),
        P(("seq", "head"), None),
        P(("seq", "head")),
        P(("seq", "head"), None),
        P(("seq", "head"), None),
        P(("seq", "head"), None),
        P(("seq", "head"), None),
        P(None, None, ("seq", "head")),
        P(None, None, ("seq", "head")),
        P(("seq", "head"), None),
        P(("seq", "head")),
        P(("seq", "head"), None),
        P(("seq", "head"), None),
        P(None, ("seq", "head")),
    )
    return jax.shard_map(run, mesh=mesh, in_specs=in_specs, out_specs=out_specs, check_vma=False)
```

```python
import math
import types
import numpy as np
import jax
import jax.numpy as jnp
from jax import lax
from jax.experimental import pallas as pl
from jax.experimental.pallas import tpu as pltpu
from jax.sharding import PartitionSpec as P

MESH = pl.DeviceIdType.MESH
bf, f32 = jnp.bfloat16, jnp.float32
W = 256
EPS = 1e-6
RATES = [float(v) for v in 10000.0 ** (-np.arange(16) * 2.0 / 32)]
SCALE = 1.0 / math.sqrt(96)
DEPTH = 4
FEATURES, SPLIT = 560, 288


def dot(a, b, ca=1, cb=0):
    return lax.dot_general(a, b, (((ca,), (cb,)), ((), ())), preferred_element_type=f32)


def place():
    s, h = lax.axis_index("seq"), lax.axis_index("head")
    return {"y": s // 2, "core": s % 2, "z": h // 4, "x": h % 4}


def device(at):
    return (at["y"] * 2 + at["core"], at["z"] * 4 + at["x"])


def remote(src, dst, send, recv, to):
    return pltpu.make_async_remote_copy(
        src_ref=src, dst_ref=dst, send_sem=send, recv_sem=recv, device_id=to, device_id_type=MESH
    )


def lanes(start, size):
    return pl.ds(pl.multiple_of(start, size), size)


def rows_of(block):
    return pl.ds(pl.multiple_of((block % 2) * 128, 128), 128)


def turn(u, cosine, sine):
    first, second = u[..., :16, :], u[..., 16:, :]
    return jnp.concatenate([first * cosine - second * sine, first * sine + second * cosine], -2)


def load_first(r, again=False):
    for i in range(2):
        pltpu.make_async_copy(r.wq.at[:, i * 512 : (i + 1) * 512], r.pool.at[i], r.first_sem.at[i]).start()
    pltpu.make_async_copy(r.wqr, r.pool.at[2], r.first_sem.at[2]).start()
    pltpu.make_async_copy(r.wl, r.pool.at[3], r.first_sem.at[3]).start()
    if not again:
        pltpu.make_async_copy(r.wo_hbm, r.wo, r.first_sem.at[4]).start()


def wait_first(r, i):
    ref = r.wo if i == 4 else r.pool.at[i]
    pltpu.make_async_copy(ref, ref, r.first_sem.at[i]).wait()


def chunk_copies(r, j):
    slot = j % DEPTH
    here = lanes(j * W, W)
    return (
        pltpu.make_async_copy(r.wg.at[:, here], r.pool.at[slot, :, 0:W], r.chunk_sem.at[slot, 0]),
        pltpu.make_async_copy(r.wu.at[:, here], r.pool.at[slot, :, W : 2 * W], r.chunk_sem.at[slot, 1]),
        pltpu.make_async_copy(r.wd.at[here, :], r.wdpool.at[slot], r.chunk_sem.at[slot, 2]),
    )


def project(r, seq, h):
    x = r.x[...].astype(f32)
    inverse = lax.rsqrt(jnp.mean(x * x, -1, keepdims=True) + EPS)
    n1 = (x * inverse * r.gain1[...].astype(f32)[None]).astype(bf)
    r.n1[...] = n1
    bound = r.second[0]
    token = h * 128 + lax.broadcasted_iota(jnp.int32, (16, 128), 1)
    position = token - jnp.where(token >= bound, bound, 0)
    step = lax.broadcasted_iota(jnp.int32, (16, 128), 0)
    rate = jnp.ones((16, 128), f32)
    for i in range(1, 16):
        rate = jnp.where(step == i, RATES[i], rate)
    angle = position.astype(f32) * rate
    cosine, sine = jnp.cos(angle), jnp.sin(angle)
    r.cos[...], r.sin[...] = cosine, sine
    wait_first(r, 3)
    lat = dot(n1, r.pool[3]).astype(bf)
    kr = turn(dot(r.wkr[...], n1, 1, 1), cosine, sine)
    flag = jnp.where(h == 15, 0.0, 1.0)
    flags = jnp.where(lax.broadcasted_iota(jnp.int32, (16, 128), 0) == 0, flag, 0.0)
    latt = lat.T
    mine = r.lxt.at[h // 2, :, lanes((h % 2) * 128, 128)]
    mine[0:256] = latt[0:256]
    mine[256:304] = jnp.concatenate([kr, flags], 0).astype(bf)
    mine[304:560] = latt[256:512]

    @pl.when(h % 2 == 0)
    def _():
        r.lxt[h // 2, SPLIT:FEATURES, 128:256] = jnp.zeros((FEATURES - SPLIT, 128), bf)

    gather_first(r, seq, h)

    for i in range(2):
        wait_first(r, i)
        r.qt[i * 512 : (i + 1) * 512] = dot(n1, r.pool[i]).T.astype(bf)
    wait_first(r, 2)
    qr = (turn(dot(n1, r.pool[2]).T.reshape(16, 32, 128), cosine, sine) * SCALE).astype(bf)
    for j in range(DEPTH):
        for copy in chunk_copies(r, j):
            copy.start()
    late = (h * 128 + (lax.broadcasted_iota(jnp.int32, (96, 1024), 1) & 127)) >= bound
    bias = jnp.where(late & (lax.broadcasted_iota(jnp.int32, (96, 1024), 0) == 0), -1e30, 0.0).astype(bf)
    for g in range(2):
        kt = r.kup[g].T
        r.kt[g] = kt
        r.vt[g] = r.vup[g].T
        at, rope = (0, 256) if g == 0 else (128, 0)
        r.qxt[g, rope + 32 : rope + 128] = bias
        for e in range(8):
            head = g * 8 + e
            cols = slice(e * 128, (e + 1) * 128)
            r.qxt[g, rope : rope + 32, cols] = qr[head]
            r.qxt[g, at : at + 256, cols] = (
                dot(r.kt[g, e * 64 : (e + 1) * 64, :], r.qt[head * 64 : (head + 1) * 64], 0, 0) * SCALE
            ).astype(bf)


def latent_half(r, i, half):
    rows = slice(0, SPLIT) if half == 0 else slice(SPLIT, FEATURES)
    return r.lxt.at[i // 2, rows, lanes((i % 2) * 128, 128)]


def gather_copy(r, seq, i, half, send, to):
    ref = latent_half(r, i, half)
    return remote(ref, ref, send, r.gather_recv.at[half, i], (seq, to))


def first_targets(r, seq, h):
    z, x = h // 4, h % 4
    for k in range(1, 4):
        there = (z + k) % 4
        yield True, gather_copy(r, seq, h, 0, r.gather_send.at[0, k], z * 4 + (x + k) % 4)
        yield there > z, gather_copy(r, seq, h, 1, r.gather_send.at[1, k], there * 4 + x)


def second_targets(r, seq, h):
    z, x = h // 4, h % 4
    for j in range(4):
        i = z * 4 + (x + j) % 4
        sends = []
        for k in range(1, 4):
            there = (z + k) % 4
            sends.append((there > z, gather_copy(r, seq, i, 0, r.gather_send.at[2 + j, k], there * 4 + x)))
        yield (j > 0), gather_copy(r, seq, i, 0, r.gather_send.at[0, 0], h), sends
        row = (z + 4 - j) % 4
        i = row * 4 + x
        sends = []
        for k in range(1, 4):
            there = (x + k) % 4
            sends.append(((row < z) | ((row == z) & (there > x)), gather_copy(r, seq, i, 1, r.gather_send.at[6 + j, k], z * 4 + there)))
        yield (row < z), gather_copy(r, seq, i, 1, r.gather_send.at[0, 0], h), sends


def gather_first(r, seq, h):
    for use, copy in first_targets(r, seq, h):
        pl.when(use)(copy.start)


def gather_second(r, seq, h):
    for use, copy, sends in second_targets(r, seq, h):
        pl.when(use)(copy.wait_recv)
        for wanted, send in sends:
            pl.when(wanted)(send.start)


def gather_sent(r, seq, h):
    for use, copy in first_targets(r, seq, h):
        pl.when(use)(copy.wait_send)
    for _, _, sends in second_targets(r, seq, h):
        for wanted, send in sends:
            pl.when(wanted)(send.wait_send)


def gather_wait(r, seq, h, i):
    pl.when((i < h) & (i // 4 != h // 4))(gather_copy(r, seq, i, 0, r.gather_send.at[0, 0], h).wait_recv)
    pl.when((i < h) & (i % 4 != h % 4))(gather_copy(r, seq, i, 1, r.gather_send.at[0, 0], h).wait_recv)


def load_latents(r, b):
    r.lx[:, 0:256] = r.lxt[b, 0:256].T
    r.lx[:, 256:384] = jnp.concatenate([r.lxt[b, 256:304], jnp.zeros((80, 256), bf)], 0).T
    r.lx[:, 384:640] = r.lxt[b, 304:560].T


def attend_step(r, seq, h, b, diag):
    gather_wait(r, seq, h, 2 * b)
    gather_wait(r, seq, h, 2 * b + 1)
    load_latents(r, b)
    wide = 512
    units = [(g, slice(c * wide, (c + 1) * wide)) for g in range(2) for c in range(1024 // wide)]
    scores = [dot(r.lx[:, g * 256 : g * 256 + 384], r.qxt[g, :, cols]) for g, cols in units]
    if diag:
        bound = r.second[0]
        key = b * 256 + lax.broadcasted_iota(jnp.int32, (256, 128), 0)
        row = h * 128 + lax.broadcasted_iota(jnp.int32, (256, 128), 1)
        ok = (key <= row) & ((key >= bound) == (row >= bound))
        barred = jnp.where(ok, 0.0, 1.0)
        barred = jnp.concatenate([barred] * (wide // 128), 1)
    kept = []
    for (g, cols), s in zip(units, scores):
        if diag:
            s = jnp.where(barred > 0.5, -1e30, s)
        top = jnp.max(s, 0, keepdims=True)
        fade = None
        if not diag:
            before = r.top[g : g + 1, cols]
            top = jnp.maximum(top, before)
            fade = jnp.exp(before - top)
        p = jnp.exp(s - top)
        total = jnp.sum(p, 0, keepdims=True)
        if not diag:
            total = total + r.total[g : g + 1, cols] * fade
        p = p.astype(bf)
        r.p[b, g, :, cols] = p
        r.total[g : g + 1, cols] = total
        r.top[g : g + 1, cols] = top
        r.tops[pl.ds(b * 2 + g, 1), cols] = top
        kept.append((p, fade))
    for (g, cols), (p, fade) in zip(units, kept):
        at = 0 if g == 0 else 304
        o = dot(r.lxt[b, at : at + 256], p)
        r.acc[g, 0:256, cols] = o if diag else o + r.acc[g, 0:256, cols] * fade


def attend(r, seq, h):
    last = h // 2
    attend_step(r, seq, h, last, True)

    @pl.loop(0, last)
    def _(i):
        attend_step(r, seq, h, last - 1 - i, False)

    for g in range(2):
        back = 1.0 / r.total[g : g + 1]
        r.back[g : g + 1] = back
        r.ot[g] = (r.acc[g, 0:256] * back).astype(bf)
        for e in range(8):
            head = g * 8 + e
            r.attt[head * 64 : (head + 1) * 64] = dot(
                r.vt[g, e * 64 : (e + 1) * 64], r.ot[g, :, e * 128 : (e + 1) * 128]
            ).astype(bf)


def feed(r, begin, each):
    wait_first(r, 4)
    r.mid[...] = r.x[...].astype(f32) + dot(r.attt[...].T, r.wo[...])
    mid = r.mid[...]
    inverse = lax.rsqrt(jnp.mean(mid * mid, -1, keepdims=True) + EPS)
    gain = r.gain2[...].astype(f32)[None]
    r.n2[...] = (mid * inverse * gain).astype(bf)
    r.grad_input[...] = mid
    r.g_acc[...] = jnp.zeros((128, 1024), f32)
    begin()

    @pl.loop(0, 11)
    def _(j):
        slot = j % DEPTH
        for copy in chunk_copies(r, j):
            copy.wait()
        n2, cot = r.n2[...], r.cot[...]
        both = dot(n2, r.pool[slot])
        grad = dot(cot, r.wdpool[slot], 1, 1)
        gate, up = both[:, :W], both[:, W:]
        sigma = jax.nn.sigmoid(gate)
        swish = gate * sigma
        act = (swish * up).astype(bf)
        grad_gate = (grad * up * sigma * (1.0 + gate * (1.0 - sigma))).astype(bf)
        grad_up = (grad * swish).astype(bf)
        out = dot(act, r.wdpool[slot])
        back = dot(jnp.concatenate([grad_gate, grad_up], 1), r.pool[slot], 1, 1)
        r.grad_input[...] += out
        r.g_acc[...] += back

        @pl.when(j + DEPTH < 11)
        def _():
            for copy in chunk_copies(r, j + DEPTH):
                copy.start()

        each(j, grad_gate, grad_up, act)

    r.output[...] = r.grad_input[...].astype(bf)
    up = r.g_acc[...]
    mid = r.mid[...]
    inverse = lax.rsqrt(jnp.mean(mid * mid, -1, keepdims=True) + EPS)
    r.gains[1:2] = jnp.sum(up * mid * inverse, 0, keepdims=True)
    scaled = up * gain
    grad_mid = r.cot[...].astype(f32) + inverse * scaled - mid * (inverse * inverse * inverse) * jnp.mean(mid * scaled, -1, keepdims=True)
    r.mid[...] = grad_mid
    r.gb[...] = grad_mid.astype(bf)
    r.ga[...] = dot(r.gb[...], r.wo[...], 1, 1).T.astype(bf)


RING = 4
ORDERS = (("y", "z", "x"), ("z", "x", "y"), ("x", "y", "z"))
JOBS = 16
FEED, OUT, ONE = 0, 1, 2
PHASES = ("a", "b", "c", "d", "e", "f")


def beside(at, axis, step):
    return device({**at, axis: (at[axis] + step) % 4})


def other_core(at):
    return device({**at, "core": 1 - at["core"]})


def choose_rows(r, me, order, which):
    for mine in (True, False):
        core = me["core"] if mine else 1 - me["core"]
        parts = []
        for i in range(64):
            part = dict(zip(ORDERS[order], (i >> 4, (i >> 2) & 3, i & 3)))
            start = part["y"] * 256 + part["z"] * 32 + part["x"] * 8
            parts.append(r.nt[pl.ds(pl.multiple_of(core * 128 + start, 8), 8), :])
        picked = jnp.concatenate(parts, 0).astype(bf)
        if mine:
            r.at[order, which, :, 0:128] = picked
        else:
            r.at_send[order, which] = picked
    at_copy(r, me, order, which).start()


def at_copy(r, me, order, which):
    return remote(
        r.at_send.at[order, which], r.at.at[order, which, :, 128:256],
        r.at_sem.at[0, order, which], r.at_sem.at[1, order, which], other_core(me),
    )


def g_copy(r, me, order, job):
    return remote(
        r.g.at[order, job, 0:128], r.g.at[order, job, 128:256],
        r.g_send.at[order, job], r.g_recv.at[order, job], other_core(me),
    )


def give(r, me, order, job, value):
    r.g[order, job, 0:128] = value
    g_copy(r, me, order, job).start()


def dense_copy(r, me, which):
    return remote(
        r.dense_send.at[which], r.dense.at[which, :, 128:256],
        r.dense_sem.at[0, which], r.dense_sem.at[1, which], other_core(me),
    )


def give_heads(r, me, which, left, right):
    for mine in (True, False):
        core = me["core"] if mine else 1 - me["core"]
        for q in range(4):
            for g in range(2):
                e = q * 2 + core
                rows = lanes((g * 8 + e) * 64, 64)
                block = dot(left[rows, :], right[g, :, lanes(e * 128, 128)], 1, 1).astype(bf)
                if mine:
                    r.dense[which, q, g * 64 : g * 64 + 64] = block
                else:
                    r.dense_send[which, q, g * 64 : g * 64 + 64] = block
    dense_copy(r, me, which).start()


def message(r, me, order, phase, way, job):
    slot = job % RING
    kind = PHASES[phase]
    return remote(
        getattr(r, "s" + kind).at[order, slot, way],
        getattr(r, "r" + kind).at[order, slot, way],
        r.sum_send.at[order, phase, way, slot],
        r.sum_recv.at[order, phase, way, slot],
        beside(me, ORDERS[order][phase // 2], 1 if way == 0 else -1),
    )


def first_half(r, me, order, stage, job, block):
    phase = stage * 2

    @pl.when(job >= RING)
    def _():
        for way in (0, 1):
            message(r, me, order, phase, way, job - RING).wait_send()

    ref = getattr(r, "s" + PHASES[phase])
    for way in (0, 1):
        half = block[:, way * (W // 2) : (way + 1) * (W // 2)]
        ref[order, job % RING, way] = half.astype(ref.dtype)
        message(r, me, order, phase, way, job).start()


def second_half(r, me, order, stage, job, block_of):
    phase = stage * 2 + 1

    @pl.when(job >= RING)
    def _():
        for way in (0, 1):
            message(r, me, order, phase, way, job - RING).wait_send()

    ref, got = getattr(r, "s" + PHASES[phase]), getattr(r, "r" + PHASES[phase - 1])
    slot = job % RING
    for way in (0, 1):
        message(r, me, order, phase - 1, way, job).wait_recv()
        block = block_of(1 if way == 0 else -1)
        here = slice(way * (W // 2), (way + 1) * (W // 2))
        there = slice((1 - way) * (W // 2), (2 - way) * (W // 2))
        ref[order, slot, way, :, here] = (block[:, here] + got[order, slot, way].astype(f32)).astype(ref.dtype)
        ref[order, slot, way, :, there] = block[:, there].astype(ref.dtype)
        message(r, me, order, phase, way, job).start()


def total(r, me, order, stage, job, block):
    phase = stage * 2 + 1
    got = getattr(r, "r" + PHASES[phase])
    for way in (0, 1):
        message(r, me, order, phase, way, job).wait_recv()
        block = block + got[order, job % RING, way].astype(f32)
    return block


def block_of(r, me, order, stage, job):
    axis = ORDERS[order][stage]
    slot = job % RING

    def get(step):
        index = (me[axis] + step) % 4
        if stage == 0:
            return r.d[order, slot, lanes(index * 128, 128), :].astype(f32)
        if stage == 1:
            return r.s1[order, slot, lanes(index * 32, 32), :]
        return r.s2[order, slot, lanes(index * 8, 8), :]

    return get


def products(r, me, order, job):
    slot = job % RING

    def plain(which):
        g_copy(r, me, order, job).wait_recv()
        r.d[order, slot] = dot(r.at[order, which], r.g[order, job]).astype(bf)

    def thick(which):
        dense_copy(r, me, which).wait_recv()
        row = lax.broadcasted_iota(jnp.int32, (128, 256), 0)
        column = lax.broadcasted_iota(jnp.int32, (128, 256), 1) & 127
        if which < 2:
            row = ((row >> 2) & 1) * 64 + (row >> 3) * 4 + (row & 3)
        pick = (row == column).astype(bf)
        for q in range(4):
            r.d[order, slot, q * 128 : (q + 1) * 128] = dot(pick, r.dense[which, q]).astype(bf)

    if order == 0:
        pl.when(job < 11)(lambda: plain(FEED))
        pl.when(job == 11)(lambda: thick(0))
        pl.when(job == 12)(lambda: thick(1))
        pl.when((job == 13) | (job == 14))(lambda: plain(ONE))
        pl.when(job == 15)(lambda: thick(2))
    else:
        plain(jnp.where(job < 11, FEED, jnp.where(job < 13, OUT, ONE)))


def sum_step(r, me, order, k, job):
    get = block_of(r, me, order, min(k // 2, 2), job)
    if k == 0:
        products(r, me, order, job)
        first_half(r, me, order, 0, job, get(2))
    elif k % 2:
        second_half(r, me, order, k // 2, job, get)
    elif k == 2:
        r.s1[order, job % RING] = total(r, me, order, 0, job, block_of(r, me, order, 0, job)(0))
        first_half(r, me, order, 1, job, get(2))
    elif k == 4:
        r.s2[order, job % RING] = total(r, me, order, 1, job, block_of(r, me, order, 1, job)(0))
        first_half(r, me, order, 2, job, get(2))
    else:
        own = block_of(r, me, order, 2, job)(0)
        r.sums[order, :, lanes(job * W, W)] = total(r, me, order, 2, job, own)


def sum_slot(r, me, t):
    for k in reversed(range(7)):
        job = t - 2 * k

        @pl.when((job >= 0) & (job < JOBS))
        def _():
            for order in range(3):
                sum_step(r, me, order, k, job)


def sum_end(r, me):
    for order in range(3):
        for phase in range(6):
            for way in (0, 1):
                for job in range(JOBS - RING, JOBS):
                    message(r, me, order, phase, way, job).wait_send()
        for job in range(JOBS):
            if order or job < 11 or job in (13, 14):
                g_copy(r, me, order, job).wait_send()
        for which in (FEED, OUT, ONE):
            if order or which != OUT:
                at_copy(r, me, order, which).wait_send()
    for which in range(3):
        dense_copy(r, me, which).wait_send()


def wait_rows(r, me, which):
    for order in range(3):
        if order or which != OUT:
            at_copy(r, me, order, which).wait_recv()


def prepare_back(r):
    for g in range(2):
        r.qxn[g] = r.qxt[g].T
        for e in range(8):
            head = g * 8 + e
            cols = slice(e * 128, (e + 1) * 128)
            ga = r.ga[head * 64 : (head + 1) * 64]
            back = r.back[g : g + 1, cols]
            inner = jnp.sum(ga.astype(f32) * r.attt[head * 64 : (head + 1) * 64].astype(f32), 0, keepdims=True)
            r.inner[g : g + 1, cols] = inner * back
            r.qxt[g, 0:256, cols] = (dot(r.vt[g, e * 64 : (e + 1) * 64, :], ga, 0, 0) * back).astype(bf)
        r.dn[g] = r.qxt[g, 0:256].T
    r.acc[...] = jnp.zeros((2, 384, 1024), f32)
    r.own_z[...] = jnp.zeros((4, SPLIT, 128), bf)


def inward(r, seq, h, b, s, half):
    z, x = h // 4, h % 4
    row, column = b // 2, (2 * b + s) % 4
    slot = b % 4
    cols = lanes(slot * 256 + s * 128, 128)
    if half == 0:
        src, step = r.wo.at[0:SPLIT, cols], (z - row + 3) % 4
        copy = remote(src, r.in_z.at[step, column], r.in_send.at[slot, s, 0], r.in_z_recv.at[step, column], (seq, row * 4 + x))
        return copy, row < z, (row == z) & (2 * b + s <= h)
    src, step = r.wo.at[SPLIT:FEATURES, cols], (x - column + 3) % 4
    copy = remote(src, r.in_x.at[step, row], r.in_send.at[slot, s, 1], r.in_x_recv.at[step, row], (seq, z * 4 + column))
    return copy, (column != x) & (2 * b + s < h), (column == x) & (2 * b + s <= h)


def back_step(r, seq, h, b):
    @pl.when(b >= 4)
    def _():
        for s in (0, 1):
            for half in (0, 1):
                copy, sent, _ = inward(r, seq, h, b - 4, s, half)
                pl.when(sent)(copy.wait_send)

    load_latents(r, b)
    cols = lanes((b % 4) * 256, 256)
    for g, at in ((0, 0), (1, 384)):
        dp = dot(r.lx[:, at : at + 256], r.qxt[g, 0:256])
        p = r.p[b, g].astype(f32) * jnp.exp(r.tops[pl.ds(b * 2 + g, 1)] - r.top[g : g + 1])
        ds = (p * (dp - r.inner[g : g + 1])).astype(bf)
        gl = dot(ds, r.qxn[g])
        gp = dot(p.astype(bf), r.dn[g])
        r.acc[g, 0:304] += dot(r.lxt[b, g * 256 : g * 256 + 304], ds)
        if g == 0:
            r.wo[0:256, cols] = (gl[:, 0:256] + gp).astype(bf).T
            rope = gl[:, 256:384]
        else:
            r.wo[256:304, cols] = (rope + gl[:, 0:128]).astype(bf).T[0:48]
            r.wo[304:560, cols] = (gl[:, 128:384] + gp).astype(bf).T
    for s in (0, 1):
        for half in (0, 1):
            copy, sent, stays = inward(r, seq, h, b, s, half)
            pl.when(sent)(copy.start)

            @pl.when(stays)
            def _():
                cols = lanes((b % 4) * 256 + s * 128, 128)
                if half == 0:
                    r.own_z[(2 * b + s) % 4] = r.wo[0:SPLIT, cols]
                else:
                    r.own_x[b // 2] = r.wo[SPLIT:FEATURES, cols]


def back_sent(r, seq, h):
    last = h // 2
    for d in range(4):
        b = last - d
        for s in (0, 1):
            for half in (0, 1):
                copy, sent, _ = inward(r, seq, h, b, s, half)
                pl.when((b >= 0) & sent)(copy.wait_send)


def onward(r, seq, h, k, half):
    z, x = h // 4, h % 4
    if half == 0:
        column = (x + k) % 4
        copy = remote(r.out_x.at[k - 1], r.end_x.at[3 - k], r.out_send.at[0, k], r.end_recv.at[0, 3 - k], (seq, z * 4 + column))
        return copy, (z < 3) | (column < x)
    row = z - k
    copy = remote(r.out_z.at[k - 1], r.end_z.at[k - 1], r.out_send.at[1, k], r.end_recv.at[1, k - 1], (seq, (row % 4) * 4 + x))
    return copy, row >= 0


def sum_latents(r, seq, h):
    z, x = h // 4, h % 4
    for k in range(4):
        column = (x + k) % 4
        r.nt[0:SPLIT] = jnp.where((column <= x), r.own_z[column].astype(f32), 0.0)
        for step in range(3):
            @pl.when(z + 1 + step < 4)
            def _():
                ref = r.in_z.at[step, column]
                remote(ref, ref, r.in_send.at[0, 0, 0], r.in_z_recv.at[step, column], (seq, h)).wait_recv()
                r.nt[0:SPLIT] += r.in_z[step, column].astype(f32)

        if k == 0:
            r.own[0:SPLIT] = r.nt[0:SPLIT]
        else:
            r.out_x[k - 1] = r.nt[0:SPLIT].astype(bf)
            copy, sent = onward(r, seq, h, k, 0)
            pl.when(sent)(copy.start)
    for k in range(4):
        @pl.when(z - k >= 0)
        def _():
            row = z - k
            r.nt[SPLIT:FEATURES] = r.own_x[row].astype(f32)
            for step in range(3):
                @pl.when((k > 0) | ((x + 1 + step) % 4 > x))
                def _():
                    ref = r.in_x.at[step, row]
                    remote(ref, ref, r.in_send.at[0, 0, 0], r.in_x_recv.at[step, row], (seq, h)).wait_recv()
                    r.nt[SPLIT:FEATURES] += r.in_x[step, row].astype(f32)

            if k == 0:
                r.own[SPLIT:FEATURES] = r.nt[SPLIT:FEATURES]
            else:
                r.out_z[k - 1] = r.nt[SPLIT:FEATURES].astype(bf)
                onward(r, seq, h, k, 1)[0].start()


def latents_sent(r, seq, h):
    for k in range(1, 4):
        for half in (0, 1):
            copy, sent = onward(r, seq, h, k, half)
            pl.when(sent)(copy.wait_send)


def finish_queries(r, me):
    for g in range(2):
        at, rope = (0, 256) if g == 0 else (48, 0)
        r.ot[g] = (r.acc[g, at : at + 256] * SCALE).astype(bf)
        for e in range(8):
            head = g * 8 + e
            cols = slice(e * 128, (e + 1) * 128)
            r.attt[head * 64 : (head + 1) * 64] = dot(r.kt[g, e * 64 : (e + 1) * 64], r.ot[g, :, cols]).astype(bf)
            turned = (r.acc[g, rope : rope + 32, cols] * SCALE).astype(bf).astype(f32)
            r.nt[head * 32 : (head + 1) * 32] = turn(turned, r.cos[...], -r.sin[...])
    r.n2[...] = r.attt[...].T
    r.gb[:, 0:512] = r.nt[0:512].T.astype(bf)
    for c in range(2):
        give(r, me, 1, 13 + c, r.n2[:, c * 256 : (c + 1) * 256])
        give(r, me, 2, 13 + c, r.n2[:, 512 + c * 256 : 768 + c * 256])
    for c in range(2):
        give(r, me, 0, 13 + c, r.gb[:, c * 256 : (c + 1) * 256])
    give_heads(r, me, 1, r.qt, r.ot)


def finish_latent(r, me, seq, h):
    z, x = h // 4, h % 4
    for k in range(3):
        @pl.when((z < 3) | ((x + 1 + k) % 4 > x))
        def _():
            ref = r.end_x.at[k]
            remote(ref, ref, r.out_send.at[0, 0], r.end_recv.at[0, k], (seq, h)).wait_recv()
            r.own[0:SPLIT] += r.end_x[k].astype(f32)

        @pl.when(z + 1 + k < 4)
        def _():
            ref = r.end_z.at[k]
            remote(ref, ref, r.out_send.at[0, 0], r.end_recv.at[1, k], (seq, h)).wait_recv()
            r.own[SPLIT:FEATURES] += r.end_z[k].astype(f32)

    r.gb[:, 512:768] = r.own[0:256].T.astype(bf)
    r.gb[:, 768:1024] = r.own[304:560].T.astype(bf)
    give(r, me, 1, 15, r.gb[:, 512:768])
    give(r, me, 2, 15, r.gb[:, 768:1024])
    turned = r.own[256:288].astype(bf).astype(f32)
    kr = turn(turned, r.cos[...], -r.sin[...])
    r.gkr[...] = jnp.concatenate([kr, jnp.zeros((96, 128), f32)], 0).T.astype(bf)


def finish_input(r):
    grad = dot(r.gkr[:, 0:32], r.wkr[...])
    for i in range(2):
        grad = grad + dot(r.n2[:, i * 512 : (i + 1) * 512], r.pool[i], 1, 1)
    grad = grad + dot(r.gb[:, 0:512], r.pool[2], 1, 1) + dot(r.gb[:, 512:1024], r.pool[3], 1, 1)
    x = r.x[...].astype(f32)
    inverse = lax.rsqrt(jnp.mean(x * x, -1, keepdims=True) + EPS)
    r.gains[0:1] = jnp.sum(grad * x * inverse, 0, keepdims=True)
    scaled = grad * r.gain1[...].astype(f32)[None]
    r.grad_input[...] = r.mid[...] + inverse * scaled - x * (inverse * inverse * inverse) * jnp.mean(x * scaled, -1, keepdims=True)


def finish_rope(r, me):
    wide = jnp.concatenate([r.gkr[...], jnp.zeros((128, 128), bf)], 1)
    row = lax.broadcasted_iota(jnp.int32, (16, 256), 0)
    column = lax.broadcasted_iota(jnp.int32, (16, 256), 1)
    spread = ((row < 4) & (column == 32 + row // 2)).astype(bf)
    for mine in (True, False):
        core = me["core"] if mine else 1 - me["core"]
        for q in range(4):
            gains = r.gains[0:2, lanes(q * 256 + core * 128, 128)]
            high = gains.astype(bf).astype(f32)
            low = gains - high
            stack = jnp.concatenate([high[0:1], low[0:1], high[1:2], low[1:2], jnp.zeros((12, 128), f32)], 0).astype(bf)
            left = r.at[0, ONE, q * 128 : (q + 1) * 128, 0:128] if mine else r.at_send[0, ONE, q * 128 : (q + 1) * 128]
            block = (dot(left, wide) + dot(stack, spread, 0, 0)).astype(bf)
            if mine:
                r.dense[2, q, 0:128] = block
            else:
                r.dense_send[2, q] = block
    dense_copy(r, me, 2).start()


INPUTS = ("x", "cot", "second", "gain1", "gain2", "wkr", "kup", "vup", "wq", "wqr", "wl", "wo_hbm", "wg", "wu", "wd")


def scratch():
    vm = lambda *shape, kind=bf: pltpu.VMEM(shape, kind)
    dma = pltpu.SemaphoreType.DMA
    return dict(
        pool=vm(4, 1024, 512), wdpool=vm(4, 256, 1024), wo=vm(1024, 1024),
        first_sem=dma((5,)), chunk_sem=dma((4, 3)),
        n1=vm(128, 1024), n2=vm(128, 1024), gb=vm(128, 1024), ga=vm(1024, 128), attt=vm(1024, 128),
        cos=vm(16, 128, kind=f32), sin=vm(16, 128, kind=f32),
        lx=vm(256, 640), lxt=vm(8, FEATURES, 256), qt=vm(1024, 128), kt=vm(2, 512, 256), vt=vm(2, 512, 256),
        qxt=vm(2, 384, 1024), p=vm(8, 2, 256, 1024), acc=vm(2, 384, 1024, kind=f32), ot=vm(2, 256, 1024),
        top=vm(8, 1024, kind=f32), total=vm(8, 1024, kind=f32), back=vm(8, 1024, kind=f32), tops=vm(16, 1024, kind=f32),
        gains=vm(8, 1024, kind=f32), mid=vm(128, 1024, kind=f32), g_acc=vm(128, 1024, kind=f32),
        gather_send=dma((10, 4)), gather_recv=dma((2, 16)),
        nt=vm(1024, 128, kind=f32), qxn=vm(2, 1024, 384), dn=vm(2, 1024, 256),
        inner=vm(8, 1024, kind=f32), own=vm(FEATURES, 128, kind=f32),
        in_z=vm(3, 4, SPLIT, 128), in_x=vm(3, 4, FEATURES - SPLIT, 128), own_z=vm(4, SPLIT, 128), own_x=vm(4, FEATURES - SPLIT, 128),
        out_x=vm(3, SPLIT, 128), out_z=vm(3, FEATURES - SPLIT, 128), end_x=vm(3, SPLIT, 128), end_z=vm(3, FEATURES - SPLIT, 128),
        in_send=dma((4, 2, 2)), in_z_recv=dma((3, 4)), in_x_recv=dma((3, 4)), out_send=dma((2, 4)), end_recv=dma((2, 3)),
        gkr=vm(128, 128),
        at=vm(3, 3, 512, 256), at_send=vm(3, 3, 512, 128), at_sem=dma((2, 3, 3)),
        g=vm(3, JOBS, 256, W), g_send=dma((3, JOBS)), g_recv=dma((3, JOBS)),
        dense=vm(3, 4, 256, W), dense_send=vm(3, 4, 128, W), dense_sem=dma((2, 3)),
        d=vm(3, RING, 512, W), s1=vm(3, RING, 128, W, kind=f32), s2=vm(3, RING, 32, W, kind=f32),
        sum_send=dma((3, 6, 2, RING)), sum_recv=dma((3, 6, 2, RING)),
        **{
            side + name: vm(3, RING, 2, rows, width, kind=kind)
            for side in "sr"
            for name, rows, width, kind in (
                ("a", 128, W // 2, bf), ("b", 128, W, bf), ("c", 32, W // 2, bf),
                ("d", 32, W, bf), ("e", 8, W // 2, f32), ("f", 8, W, f32),
            )
        },
    )


def kernel(names, *refs):
    r = types.SimpleNamespace(**dict(zip(names, refs)))
    seq, h = lax.axis_index("seq"), lax.axis_index("head")
    me = place()
    load_first(r)
    barrier = pltpu.get_barrier_semaphore()
    peers = [(seq, (h + k) % 16) for k in range(1, 16)] + [other_core(me), beside(me, "y", 1), beside(me, "y", -1)]
    for peer in peers:
        pl.semaphore_signal(barrier, inc=1, device_id=peer, device_id_type=MESH)
    pl.semaphore_wait(barrier, len(peers))
    project(r, seq, h)
    gather_second(r, seq, h)
    r.nt[...] = r.cot[...].astype(f32).T
    choose_rows(r, me, 2, FEED)
    r.nt[...] = r.n1[...].astype(f32).T
    for order in range(3):
        choose_rows(r, me, order, ONE)
    attend(r, seq, h)
    r.nt[...] = r.attt[...].astype(f32)
    for order in (1, 2):
        choose_rows(r, me, order, OUT)

    def begin():
        r.nt[...] = r.n2[...].astype(f32).T
        for order in (0, 1):
            choose_rows(r, me, order, FEED)

    def each(j, grad_gate, grad_up, act):
        for order, value in enumerate((grad_gate, grad_up, act)):
            give(r, me, order, j, value)

        @pl.when(j % 2 == 1)
        def _():
            @pl.when(j == 1)
            def _():
                wait_rows(r, me, FEED)

            sum_slot(r, me, j // 2)

    feed(r, begin, each)
    load_first(r, again=True)
    for c in range(2):
        give(r, me, 1, 11 + c, r.gb[:, c * 256 : (c + 1) * 256])
        give(r, me, 2, 11 + c, r.gb[:, 512 + c * 256 : 768 + c * 256])
    give_heads(r, me, 0, r.ga, r.ot)
    prepare_back(r)
    wait_rows(r, me, OUT)

    @pl.loop(0, 8)
    def _(b):
        @pl.when(b <= h // 2)
        def _():
            back_step(r, seq, h, b)

        @pl.when(b < 7)
        def _():
            sum_slot(r, me, 5 + b)

    finish_queries(r, me)
    wait_rows(r, me, ONE)
    sum_slot(r, me, 12)
    sum_latents(r, seq, h)
    sum_slot(r, me, 13)
    sum_slot(r, me, 14)
    finish_latent(r, me, seq, h)
    for i in range(4):
        wait_first(r, i)
    finish_input(r)
    finish_rope(r, me)

    @pl.loop(15, 28)
    def _(t):
        sum_slot(r, me, t)

    sum_end(r, me)
    back_sent(r, seq, h)
    latents_sent(r, seq, h)
    gather_sent(r, seq, h)


def run(layer_input, second_start, mixer_gain, w_query, w_query_rope, w_latent, w_key_rope, w_key_up, w_value_up, w_out, feed_gain, w_gate, w_up, w_down, cotangent):
    args = dict(x=layer_input, cot=cotangent, second=second_start, gain1=mixer_gain, gain2=feed_gain,
        wkr=w_key_rope.T, kup=w_key_up, vup=w_value_up, wq=w_query, wqr=w_query_rope, wl=w_latent, wo_hbm=w_out, wg=w_gate, wu=w_up, wd=w_down)
    V, A, S = (pl.BlockSpec(memory_space=m) for m in (pltpu.VMEM, pl.ANY, pltpu.SMEM))
    specs = {n: V for n in INPUTS}
    specs["second"] = S
    for n in ("wq", "wqr", "wl", "wo_hbm", "wg", "wu", "wd"):
        specs[n] = A
    outs = dict(output=((128, 1024), bf), grad_input=((128, 1024), f32), sums=((3, 8, JOBS * W), f32))
    sc = scratch()
    names = INPUTS + tuple(outs) + tuple(sc)
    output, grad_input, sums = pl.pallas_call(
        lambda *refs: kernel(names, *refs),
        out_shape=[jax.ShapeDtypeStruct(*o) for o in outs.values()],
        in_specs=[specs[n] for n in INPUTS], out_specs=[V] * len(outs),
        scratch_shapes=list(sc.values()),
        compiler_params=pltpu.CompilerParams(collective_id=0, has_side_effects=True, vmem_limit_bytes=66900000),
        name="layer",
    )(*[args[n] for n in INPUTS])

    return place_results(output, grad_input, sums)


def place_kernel(output, grad_input, sums, *outs):
    first, second, third = (sums.at[i] for i in range(3))
    outs[0][...] = output[...]
    outs[1][...] = grad_input[...]
    rope = first[:, 3840:3968]
    turned = jnp.concatenate([rope, jnp.zeros((120, 128), f32)], 0).T
    outs[2][...] = turned[32:33, 0:8]
    outs[3][:, 0:512] = second[:, 3328:3840]
    outs[3][:, 512:1024] = third[:, 3328:3840]
    outs[4][...] = first[:, 3328:3840]
    outs[5][:, 0:256] = second[:, 3840:4096]
    outs[5][:, 256:512] = third[:, 3840:4096]
    outs[6][...] = rope[:, 0:32]
    for g in range(2):
        outs[7][g] = first[g * 4 : g * 4 + 4, 3072:3328]
        outs[8][g] = first[g * 4 : g * 4 + 4, 2816:3072]
    outs[9][:, 0:512] = second[:, 2816:3328]
    outs[9][:, 512:1024] = third[:, 2816:3328]
    outs[10][...] = turned[33:34, 0:8]
    outs[11][...] = first[:, 0:2816]
    outs[12][...] = second[:, 0:2816]
    outs[13][...] = third[:, 0:2816]


def place_results(output, grad_input, sums):
    shapes = [(1, 8), (8, 1024), (8, 512), (8, 512), (8, 32), (2, 4, 256), (2, 4, 256), (8, 1024), (1, 8), (8, 2816), (8, 2816), (8, 2816)]
    outs = list(pl.pallas_call(
        place_kernel,
        out_shape=[jax.ShapeDtypeStruct((128, 1024), bf), jax.ShapeDtypeStruct((128, 1024), f32)]
        + [jax.ShapeDtypeStruct(shape, f32) for shape in shapes],
        name="place",
    )(output, grad_input, sums))
    for i in (2, 10):
        outs[i] = outs[i].reshape(8)
    for i in (7, 8):
        outs[i] = outs[i].transpose(0, 2, 1)
    outs[13] = outs[13].T
    return tuple(outs)


def solution(mesh):
    in_specs = (
        P(("seq", "head"), None),
        P("seq"),
        P(),
        P(),
        P(),
        P(),
        P(),
        P(),
        P(),
        P(),
        P(),
        P(),
        P(),
        P(),
        P(("seq", "head"), None),
    )
    out_specs = (
        P(("seq", "head"), None),
        P(("seq", "head"), None),
        P(("seq", "head")),
        P(("seq", "head"), None),
        P(("seq", "head"), None),
        P(("seq", "head"), None),
        P(("seq", "head"), None),
        P(None, None, ("seq", "head")),
        P(None, None, ("seq", "head")),
        P(("seq", "head"), None),
        P(("seq", "head")),
        P(("seq", "head"), None),
        P(("seq", "head"), None),
        P(None, ("seq", "head")),
    )
    return jax.shard_map(run, mesh=mesh, in_specs=in_specs, out_specs=out_specs, check_vma=False)
```

```python
import math
import types
import numpy as np
import jax
import jax.numpy as jnp
from jax import lax
from jax.experimental import pallas as pl
from jax.experimental.pallas import tpu as pltpu
from jax.sharding import PartitionSpec as P

MESH = pl.DeviceIdType.MESH
bf, f32 = jnp.bfloat16, jnp.float32
W = 256
EPS = 1e-6
RATES = [float(v) for v in 10000.0 ** (-np.arange(16) * 2.0 / 32)]
SCALE = 1.0 / math.sqrt(96)
DEPTH = 4
FEATURES, SPLIT = 560, 288


def dot(a, b, ca=1, cb=0):
    return lax.dot_general(a, b, (((ca,), (cb,)), ((), ())), preferred_element_type=f32)


def place():
    s, h = lax.axis_index("seq"), lax.axis_index("head")
    return {"y": s // 2, "core": s % 2, "z": h // 4, "x": h % 4}


def device(at):
    return (at["y"] * 2 + at["core"], at["z"] * 4 + at["x"])


def remote(src, dst, send, recv, to):
    return pltpu.make_async_remote_copy(
        src_ref=src, dst_ref=dst, send_sem=send, recv_sem=recv, device_id=to, device_id_type=MESH
    )


def lanes(start, size):
    return pl.ds(pl.multiple_of(start, size), size)


def rows_of(block):
    return pl.ds(pl.multiple_of((block % 2) * 128, 128), 128)


def turn(u, cosine, sine):
    first, second = u[..., :16, :], u[..., 16:, :]
    return jnp.concatenate([first * cosine - second * sine, first * sine + second * cosine], -2)


def small_copy(r, name):
    return pltpu.make_async_copy(getattr(r, name + "_hbm"), getattr(r, name), r.small_sem.at[SMALL.index(name)])


def result_copy(r, name):
    return pltpu.make_async_copy(getattr(r, name), getattr(r, name + "_hbm"), r.result_sem.at[RESULTS.index(name)])


def load_first(r, again=False):
    if not again:
        for name in SMALL:
            small_copy(r, name).start()
    for i in range(2):
        pltpu.make_async_copy(r.wq.at[:, i * 512 : (i + 1) * 512], r.pool.at[i], r.first_sem.at[i]).start()
    pltpu.make_async_copy(r.wqr, r.pool.at[2], r.first_sem.at[2]).start()
    pltpu.make_async_copy(r.wl, r.pool.at[3], r.first_sem.at[3]).start()
    if not again:
        pltpu.make_async_copy(r.wo_hbm, r.wo, r.first_sem.at[4]).start()


def wait_first(r, i):
    ref = r.wo if i == 4 else r.pool.at[i]
    pltpu.make_async_copy(ref, ref, r.first_sem.at[i]).wait()


def chunk_copies(r, j):
    slot = j % DEPTH
    here = lanes(j * W, W)
    return (
        pltpu.make_async_copy(r.wg.at[:, here], r.pool.at[slot, :, 0:W], r.chunk_sem.at[slot, 0]),
        pltpu.make_async_copy(r.wu.at[:, here], r.pool.at[slot, :, W : 2 * W], r.chunk_sem.at[slot, 1]),
        pltpu.make_async_copy(r.wd.at[here, :], r.wdpool.at[slot], r.chunk_sem.at[slot, 2]),
    )


def project(r, seq, h):
    for name in ("x", "gain1", "wkr"):
        small_copy(r, name).wait()
    x = r.x[...].astype(f32)
    inverse = lax.rsqrt(jnp.mean(x * x, -1, keepdims=True) + EPS)
    n1 = (x * inverse * r.gain1[...].astype(f32)[None]).astype(bf)
    r.n1[...] = n1
    bound = r.second[0]
    token = h * 128 + lax.broadcasted_iota(jnp.int32, (16, 128), 1)
    position = token - jnp.where(token >= bound, bound, 0)
    step = lax.broadcasted_iota(jnp.int32, (16, 128), 0)
    rate = jnp.ones((16, 128), f32)
    for i in range(1, 16):
        rate = jnp.where(step == i, RATES[i], rate)
    angle = position.astype(f32) * rate
    cosine, sine = jnp.cos(angle), jnp.sin(angle)
    r.cos[...], r.sin[...] = cosine, sine
    wait_first(r, 3)
    lat = dot(n1, r.pool[3]).astype(bf)
    kr = turn(dot(r.wkr[...], n1, 1, 1), cosine, sine)
    flag = jnp.where(h == 15, 0.0, 1.0)
    flags = jnp.where(lax.broadcasted_iota(jnp.int32, (16, 128), 0) == 0, flag, 0.0)
    latt = lat.T
    mine = r.lxt.at[h // 2, :, lanes((h % 2) * 128, 128)]
    mine[0:256] = latt[0:256]
    mine[256:304] = jnp.concatenate([kr, flags], 0).astype(bf)
    mine[304:560] = latt[256:512]

    @pl.when(h % 2 == 0)
    def _():
        r.lxt[h // 2, SPLIT:FEATURES, 128:256] = jnp.zeros((FEATURES - SPLIT, 128), bf)

    gather_first(r, seq, h)

    for i in range(2):
        wait_first(r, i)
        r.qt[i * 512 : (i + 1) * 512] = dot(n1, r.pool[i]).T.astype(bf)
    wait_first(r, 2)
    qr = (turn(dot(n1, r.pool[2]).T.reshape(16, 32, 128), cosine, sine) * SCALE).astype(bf)
    for j in range(DEPTH):
        for copy in chunk_copies(r, j):
            copy.start()
    late = (h * 128 + (lax.broadcasted_iota(jnp.int32, (96, 1024), 1) & 127)) >= bound
    bias = jnp.where(late & (lax.broadcasted_iota(jnp.int32, (96, 1024), 0) == 0), -1e30, 0.0).astype(bf)
    for name in ("kup", "vup", "cot", "gain2"):
        small_copy(r, name).wait()
    for g in range(2):
        r.kt[g] = r.kup[g].T
        r.vt[g] = r.vup[g].T
        at, rope = (0, 256) if g == 0 else (128, 0)
        r.qxt[g, rope + 32 : rope + 128] = bias
        for e in range(8):
            head = g * 8 + e
            cols = slice(e * 128, (e + 1) * 128)
            r.qxt[g, rope : rope + 32, cols] = qr[head]
            r.qxt[g, at : at + 256, cols] = (
                dot(r.kt[g, e * 64 : (e + 1) * 64, :], r.qt[head * 64 : (head + 1) * 64], 0, 0) * SCALE
            ).astype(bf)


def latent_half(r, i, half):
    rows = slice(0, SPLIT) if half == 0 else slice(SPLIT, FEATURES)
    return r.lxt.at[i // 2, rows, lanes((i % 2) * 128, 128)]


def gather_copy(r, seq, i, half, send, to):
    ref = latent_half(r, i, half)
    return remote(ref, ref, send, r.gather_recv.at[half, i], (seq, to))


def first_targets(r, seq, h):
    z, x = h // 4, h % 4
    for k in range(1, 4):
        there = (z + k) % 4
        yield True, gather_copy(r, seq, h, 0, r.gather_send.at[0, k], z * 4 + (x + k) % 4)
        yield there > z, gather_copy(r, seq, h, 1, r.gather_send.at[1, k], there * 4 + x)


def second_targets(r, seq, h):
    z, x = h // 4, h % 4
    for j in range(4):
        i = z * 4 + (x + j) % 4
        sends = []
        for k in range(1, 4):
            there = (z + k) % 4
            sends.append((there > z, gather_copy(r, seq, i, 0, r.gather_send.at[2 + j, k], there * 4 + x)))
        yield (j > 0), gather_copy(r, seq, i, 0, r.gather_send.at[0, 0], h), sends
        row = (z + 4 - j) % 4
        i = row * 4 + x
        sends = []
        for k in range(1, 4):
            there = (x + k) % 4
            sends.append(((row < z) | ((row == z) & (there > x)), gather_copy(r, seq, i, 1, r.gather_send.at[6 + j, k], z * 4 + there)))
        yield (row < z), gather_copy(r, seq, i, 1, r.gather_send.at[0, 0], h), sends


def gather_first(r, seq, h):
    for use, copy in first_targets(r, seq, h):
        pl.when(use)(copy.start)


def gather_second(r, seq, h):
    for use, copy, sends in second_targets(r, seq, h):
        pl.when(use)(copy.wait_recv)
        for wanted, send in sends:
            pl.when(wanted)(send.start)


def gather_sent(r, seq, h):
    for use, copy in first_targets(r, seq, h):
        pl.when(use)(copy.wait_send)
    for _, _, sends in second_targets(r, seq, h):
        for wanted, send in sends:
            pl.when(wanted)(send.wait_send)


def gather_wait(r, seq, h, i):
    pl.when((i < h) & (i // 4 != h // 4))(gather_copy(r, seq, i, 0, r.gather_send.at[0, 0], h).wait_recv)
    pl.when((i < h) & (i % 4 != h % 4))(gather_copy(r, seq, i, 1, r.gather_send.at[0, 0], h).wait_recv)


def load_latents(r, b):
    r.lx[:, 0:256] = r.lxt[b, 0:256].T
    r.lx[:, 256:384] = jnp.concatenate([r.lxt[b, 256:304], jnp.zeros((80, 256), bf)], 0).T
    r.lx[:, 384:640] = r.lxt[b, 304:560].T


def attend_step(r, seq, h, b, diag):
    gather_wait(r, seq, h, 2 * b)
    gather_wait(r, seq, h, 2 * b + 1)
    load_latents(r, b)
    wide = 512
    units = [(g, slice(c * wide, (c + 1) * wide)) for g in range(2) for c in range(1024 // wide)]
    scores = [dot(r.lx[:, g * 256 : g * 256 + 384], r.qxt[g, :, cols]) for g, cols in units]
    if diag:
        bound = r.second[0]
        key = b * 256 + lax.broadcasted_iota(jnp.int32, (256, 128), 0)
        row = h * 128 + lax.broadcasted_iota(jnp.int32, (256, 128), 1)
        ok = (key <= row) & ((key >= bound) == (row >= bound))
        barred = jnp.where(ok, 0.0, 1.0)
        barred = jnp.concatenate([barred] * (wide // 128), 1)
    kept = []
    for (g, cols), s in zip(units, scores):
        if diag:
            s = jnp.where(barred > 0.5, -1e30, s)
        top = jnp.max(s, 0, keepdims=True)
        fade = None
        if not diag:
            before = r.top[g : g + 1, cols]
            top = jnp.maximum(top, before)
            fade = jnp.exp(before - top)
        p = jnp.exp(s - top)
        total = jnp.sum(p, 0, keepdims=True)
        if not diag:
            total = total + r.total[g : g + 1, cols] * fade
        p = p.astype(bf)
        r.p[b, g, :, cols] = p
        r.total[g : g + 1, cols] = total
        r.top[g : g + 1, cols] = top
        r.tops[pl.ds(b * 2 + g, 1), cols] = top
        kept.append((p, fade))
    for (g, cols), (p, fade) in zip(units, kept):
        at = 0 if g == 0 else 304
        o = dot(r.lxt[b, at : at + 256], p)
        r.acc[g, 0:256, cols] = o if diag else o + r.acc[g, 0:256, cols] * fade


def attend(r, seq, h):
    last = h // 2
    attend_step(r, seq, h, last, True)

    @pl.loop(0, last)
    def _(i):
        attend_step(r, seq, h, last - 1 - i, False)

    for g in range(2):
        back = 1.0 / r.total[g : g + 1]
        r.back[g : g + 1] = back
        r.ot[g] = (r.acc[g, 0:256] * back).astype(bf)
        for e in range(8):
            head = g * 8 + e
            r.attt[head * 64 : (head + 1) * 64] = dot(
                r.vt[g, e * 64 : (e + 1) * 64], r.ot[g, :, e * 128 : (e + 1) * 128]
            ).astype(bf)


def feed(r, begin, each):
    wait_first(r, 4)
    r.mid[...] = r.x[...].astype(f32) + dot(r.attt[...].T, r.wo[...])
    mid = r.mid[...]
    inverse = lax.rsqrt(jnp.mean(mid * mid, -1, keepdims=True) + EPS)
    gain = r.gain2[...].astype(f32)[None]
    r.n2[...] = (mid * inverse * gain).astype(bf)
    r.grad_input[...] = mid
    r.g_acc[...] = jnp.zeros((128, 1024), f32)
    begin()

    @pl.loop(0, 11)
    def _(j):
        slot = j % DEPTH
        for copy in chunk_copies(r, j):
            copy.wait()
        n2, cot = r.n2[...], r.cot[...]
        both = dot(n2, r.pool[slot])
        grad = dot(cot, r.wdpool[slot], 1, 1)
        gate, up = both[:, :W], both[:, W:]
        sigma = jax.nn.sigmoid(gate)
        swish = gate * sigma
        act = (swish * up).astype(bf)
        grad_gate = (grad * up * sigma * (1.0 + gate * (1.0 - sigma))).astype(bf)
        grad_up = (grad * swish).astype(bf)
        out = dot(act, r.wdpool[slot])
        back = dot(jnp.concatenate([grad_gate, grad_up], 1), r.pool[slot], 1, 1)
        r.grad_input[...] += out
        r.g_acc[...] += back

        @pl.when(j + DEPTH < 11)
        def _():
            for copy in chunk_copies(r, j + DEPTH):
                copy.start()

        each(j, grad_gate, grad_up, act)

    r.output[...] = r.grad_input[...].astype(bf)
    result_copy(r, "output").start()
    up = r.g_acc[...]
    mid = r.mid[...]
    inverse = lax.rsqrt(jnp.mean(mid * mid, -1, keepdims=True) + EPS)
    r.gains[1:2] = jnp.sum(up * mid * inverse, 0, keepdims=True)
    scaled = up * gain
    grad_mid = r.cot[...].astype(f32) + inverse * scaled - mid * (inverse * inverse * inverse) * jnp.mean(mid * scaled, -1, keepdims=True)
    r.mid[...] = grad_mid
    r.gb[...] = grad_mid.astype(bf)
    r.ga[...] = dot(r.gb[...], r.wo[...], 1, 1).T.astype(bf)


RING = 4
ORDERS = (("y", "z", "x"), ("z", "y", "x"), ("x", "y", "z"))
JOBS = 17
FEED, OUT, ONE = 0, 1, 2


def beside(at, axis, step):
    return device({**at, axis: (at[axis] + step) % 4})


def other_core(at):
    return device({**at, "core": 1 - at["core"]})


def choose_rows(r, me, order, which):
    for mine in (True, False):
        core = me["core"] if mine else 1 - me["core"]
        parts = []
        for i in range(64):
            part = dict(zip(ORDERS[order], (i >> 4, (i >> 2) & 3, i & 3)))
            start = part["y"] * 256 + part["z"] * 32 + part["x"] * 8
            parts.append(r.nt[pl.ds(pl.multiple_of(core * 128 + start, 8), 8), :])
        picked = jnp.concatenate(parts, 0).astype(bf)
        if mine:
            r.at[order, which, :, 0:128] = picked
        else:
            r.at_send[order, which] = picked
    at_copy(r, me, order, which).start()


def at_copy(r, me, order, which):
    return remote(
        r.at_send.at[order, which], r.at.at[order, which, :, 128:256],
        r.at_sem.at[0, order, which], r.at_sem.at[1, order, which], other_core(me),
    )


def g_copy(r, me, order, job):
    return remote(
        r.g.at[order, job, 0:128], r.g.at[order, job, 128:256],
        r.g_send.at[order, job], r.g_recv.at[order, job], other_core(me),
    )


def give(r, me, order, job, value):
    r.g[order, job, 0:128] = value
    g_copy(r, me, order, job).start()


def dense_copy(r, me, which):
    return remote(
        r.dense_send.at[which], r.dense.at[which, :, 128:256],
        r.dense_sem.at[0, which], r.dense_sem.at[1, which], other_core(me),
    )


def give_heads(r, me, which, left, right):
    for mine in (True, False):
        core = me["core"] if mine else 1 - me["core"]
        for q in range(4):
            for g in range(2):
                e = q * 2 + core
                rows = lanes((g * 8 + e) * 64, 64)
                block = dot(left[rows, :], right[g, :, lanes(e * 128, 128)], 1, 1).astype(bf)
                if mine:
                    r.dense[which, q, g * 64 : g * 64 + 64] = block
                else:
                    r.dense_send[which, q, g * 64 : g * 64 + 64] = block
    dense_copy(r, me, which).start()


def part_copy(r, me, order, way, job, whole):
    slot, kind = job % RING, "b" if whole else "a"
    return remote(
        getattr(r, "s" + kind).at[order, slot, way],
        getattr(r, "r" + kind).at[order, slot, way],
        r.part_send.at[order, int(whole), way, slot],
        r.part_recv.at[order, int(whole), way, slot],
        beside(me, ORDERS[order][0], 1 if way == 0 else -1),
    )


def direct_copy(r, me, order, stage, k, job):
    slot, kind = job % RING, "c" if stage == 1 else "d"
    return remote(
        getattr(r, "s" + kind).at[order, slot, k - 1],
        getattr(r, "r" + kind).at[order, slot, k - 1],
        r.direct_send.at[order, stage - 1, k - 1, slot],
        r.direct_recv.at[order, stage - 1, k - 1, slot],
        beside(me, ORDERS[order][stage], k),
    )


def sends_of(r, me, k, job, orders):
    for order in orders:
        if k < 2:
            for way in (0, 1):
                yield part_copy(r, me, order, way, job, k == 1)
        else:
            for step in (1, 2, 3):
                yield direct_copy(r, me, order, k - 1, step, job)


def products(r, me, job, orders):
    slot = job % RING

    def plain(which, orders):
        for order in orders:
            g_copy(r, me, order, job).wait_recv()
        blocks = [dot(r.at[order, which], r.g[order, job]) for order in orders]
        for order, block in zip(orders, blocks):
            r.d[order, slot] = block.astype(bf)

    def thick(which):
        dense_copy(r, me, which).wait_recv()
        row = lax.broadcasted_iota(jnp.int32, (128, 256), 0)
        column = lax.broadcasted_iota(jnp.int32, (128, 256), 1) & 127
        if which < 2:
            row = ((row >> 2) & 1) * 64 + (row >> 3) * 4 + (row & 3)
        pick = (row == column).astype(bf)
        blocks = [dot(pick, r.dense[which, q]) for q in range(4)]
        for q in range(4):
            r.d[0, slot, q * 128 : (q + 1) * 128] = blocks[q].astype(bf)

    if len(orders) == 1:
        thick(2)
        return
    pl.when(job < 11)(lambda: plain(FEED, (0, 1, 2)))
    pl.when((job == 13) | (job == 14))(lambda: plain(ONE, (0, 1, 2)))
    for number, kind, others in ((11, 0, OUT), (12, 1, OUT)):
        @pl.when(job == number)
        def _():
            thick(kind)
            plain(others, (1, 2))

    pl.when(job == 15)(lambda: plain(ONE, (1, 2)))


def rows_from(ref, index, count):
    return ref[lanes(index * count, count), :]


def sum_step(r, me, k, job, orders):
    slot = job % RING
    if k == 0:
        products(r, me, job, orders)
    if k < 4:
        @pl.when(job >= RING)
        def _():
            for copy in sends_of(r, me, k, job - RING, orders):
                copy.wait_send()

    if k:
        for copy in sends_of(r, me, k - 1, job, orders):
            copy.wait_recv()
    place_of = [[me[axis] for axis in ORDERS[order]] for order in range(3)]
    if k == 0:
        for order in orders:
            opposite = rows_from(r.d.at[order, slot], (place_of[order][0] + 2) % 4, 128)
            for way in (0, 1):
                r.sa[order, slot, way] = opposite[:, way * (W // 2) : (way + 1) * (W // 2)]
    elif k == 1:
        for order in orders:
            for way in (0, 1):
                block = rows_from(r.d.at[order, slot], (place_of[order][0] + (1 if way == 0 else 3)) % 4, 128)
                here = slice(way * (W // 2), (way + 1) * (W // 2))
                there = slice((1 - way) * (W // 2), (2 - way) * (W // 2))
                r.sb[order, slot, way, :, here] = (block[:, here].astype(f32) + r.ra[order, slot, way].astype(f32)).astype(bf)
                r.sb[order, slot, way, :, there] = block[:, there]
    elif k == 2:
        for order in orders:
            own = rows_from(r.d.at[order, slot], place_of[order][0], 128).astype(f32)
            r.s1[order] = own + r.rb[order, slot, 0].astype(f32) + r.rb[order, slot, 1].astype(f32)
        for order in orders:
            for step in (1, 2, 3):
                r.sc[order, slot, step - 1] = rows_from(r.s1.at[order], (place_of[order][1] + step) % 4, 32).astype(bf)
            r.own1[order, slot] = rows_from(r.s1.at[order], place_of[order][1], 32)
    elif k == 3:
        for order in orders:
            block = r.own1[order, slot]
            for step in range(3):
                block = block + r.rc[order, slot, step].astype(f32)
            r.s2[order] = block
        for order in orders:
            for step in (1, 2, 3):
                block = rows_from(r.s2.at[order], (place_of[order][2] + step) % 4, 8)
                r.sd[order, slot, step - 1] = jnp.concatenate([block[:, : W // 2], block[:, W // 2 :]], 0).astype(bf)
            r.own2[order, slot] = rows_from(r.s2.at[order], place_of[order][2], 8)
    else:
        for order in orders:
            block = r.own2[order, slot]
            for step in range(3):
                got = r.rd[order, slot, step].astype(f32)
                block = block + jnp.concatenate([got[:8], got[8:]], 1)
            r.sums[order, :, lanes(job * W, W)] = block
    if k < 4:
        for copy in sends_of(r, me, k, job, orders):
            copy.start()


def sum_slot(r, me, t):
    for k in reversed(range(5)):
        job = t - 2 * k

        @pl.when((job >= 0) & (job < JOBS - 1))
        def _():
            sum_step(r, me, k, job, (0, 1, 2))

        @pl.when(job == JOBS - 1)
        def _():
            sum_step(r, me, k, job, (0,))


def sum_end(r, me):
    for k in range(4):
        for back in range(RING):
            for copy in (*sends_of(r, me, k, JOBS - 1 - back, (0,)), *sends_of(r, me, k, JOBS - 2 - back, (1, 2))):
                copy.wait_send()
    for order in range(3):
        for job in range(16):
            if order or job < 11 or job in (13, 14):
                g_copy(r, me, order, job).wait_send()
        for which in (FEED, OUT, ONE):
            if order or which != OUT:
                at_copy(r, me, order, which).wait_send()
    for which in range(3):
        dense_copy(r, me, which).wait_send()


def wait_rows(r, me, which):
    for order in range(3):
        if order or which != OUT:
            at_copy(r, me, order, which).wait_recv()


def prepare_back(r):
    for g in range(2):
        r.qxn[g] = r.qxt[g].T
        for e in range(8):
            head = g * 8 + e
            cols = slice(e * 128, (e + 1) * 128)
            ga = r.ga[head * 64 : (head + 1) * 64]
            back = r.back[g : g + 1, cols]
            inner = jnp.sum(ga.astype(f32) * r.attt[head * 64 : (head + 1) * 64].astype(f32), 0, keepdims=True)
            r.inner[g : g + 1, cols] = inner * back
            r.qxt[g, 0:256, cols] = (dot(r.vt[g, e * 64 : (e + 1) * 64, :], ga, 0, 0) * back).astype(bf)
        r.dn[g] = r.qxt[g, 0:256].T
    r.acc[...] = jnp.zeros((2, 384, 1024), f32)
    r.own_z[...] = jnp.zeros((4, SPLIT, 128), bf)


def inward(r, seq, h, b, s, half):
    z, x = h // 4, h % 4
    row, column = b // 2, (2 * b + s) % 4
    slot = b % 4
    cols = lanes(slot * 256 + s * 128, 128)
    if half == 0:
        src, step = r.wo.at[0:SPLIT, cols], (z - row + 3) % 4
        copy = remote(src, r.in_z.at[step, column], r.in_send.at[slot, s, 0], r.in_z_recv.at[step, column], (seq, row * 4 + x))
        return copy, row < z, (row == z) & (2 * b + s <= h)
    src, step = r.wo.at[SPLIT:FEATURES, cols], (x - column + 3) % 4
    copy = remote(src, r.in_x.at[step, row], r.in_send.at[slot, s, 1], r.in_x_recv.at[step, row], (seq, z * 4 + column))
    return copy, (column != x) & (2 * b + s < h), (column == x) & (2 * b + s <= h)


def back_step(r, seq, h, b):
    @pl.when(b >= 4)
    def _():
        for s in (0, 1):
            for half in (0, 1):
                copy, sent, _ = inward(r, seq, h, b - 4, s, half)
                pl.when(sent)(copy.wait_send)

    load_latents(r, b)
    cols = lanes((b % 4) * 256, 256)
    for g, at in ((0, 0), (1, 384)):
        dp = dot(r.lx[:, at : at + 256], r.qxt[g, 0:256])
        p = r.p[b, g].astype(f32) * jnp.exp(r.tops[pl.ds(b * 2 + g, 1)] - r.top[g : g + 1])
        ds = (p * (dp - r.inner[g : g + 1])).astype(bf)
        gl = dot(ds, r.qxn[g])
        gp = dot(p.astype(bf), r.dn[g])
        r.acc[g, 0:304] += dot(r.lxt[b, g * 256 : g * 256 + 304], ds)
        if g == 0:
            r.wo[0:256, cols] = (gl[:, 0:256] + gp).astype(bf).T
            rope = gl[:, 256:384]
        else:
            r.wo[256:304, cols] = (rope + gl[:, 0:128]).astype(bf).T[0:48]
            r.wo[304:560, cols] = (gl[:, 128:384] + gp).astype(bf).T
    for s in (0, 1):
        for half in (0, 1):
            copy, sent, stays = inward(r, seq, h, b, s, half)
            pl.when(sent)(copy.start)

            @pl.when(stays)
            def _():
                cols = lanes((b % 4) * 256 + s * 128, 128)
                if half == 0:
                    r.own_z[(2 * b + s) % 4] = r.wo[0:SPLIT, cols]
                else:
                    r.own_x[b // 2] = r.wo[SPLIT:FEATURES, cols]


def back_sent(r, seq, h):
    last = h // 2
    for d in range(4):
        b = last - d
        for s in (0, 1):
            for half in (0, 1):
                copy, sent, _ = inward(r, seq, h, b, s, half)
                pl.when((b >= 0) & sent)(copy.wait_send)


def onward(r, seq, h, k, half):
    z, x = h // 4, h % 4
    if half == 0:
        column = (x + k) % 4
        copy = remote(r.out_x.at[k - 1], r.end_x.at[3 - k], r.out_send.at[0, k], r.end_recv.at[0, 3 - k], (seq, z * 4 + column))
        return copy, (z < 3) | (column < x)
    row = z - k
    copy = remote(r.out_z.at[k - 1], r.end_z.at[k - 1], r.out_send.at[1, k], r.end_recv.at[1, k - 1], (seq, (row % 4) * 4 + x))
    return copy, row >= 0


def sum_latents(r, seq, h):
    z, x = h // 4, h % 4
    for k in range(4):
        column = (x + k) % 4
        r.nt[0:SPLIT] = jnp.where((column <= x), r.own_z[column].astype(f32), 0.0)
        for step in range(3):
            @pl.when(z + 1 + step < 4)
            def _():
                ref = r.in_z.at[step, column]
                remote(ref, ref, r.in_send.at[0, 0, 0], r.in_z_recv.at[step, column], (seq, h)).wait_recv()
                r.nt[0:SPLIT] += r.in_z[step, column].astype(f32)

        if k == 0:
            r.own[0:SPLIT] = r.nt[0:SPLIT]
        else:
            r.out_x[k - 1] = r.nt[0:SPLIT].astype(bf)
            copy, sent = onward(r, seq, h, k, 0)
            pl.when(sent)(copy.start)
    for k in range(4):
        @pl.when(z - k >= 0)
        def _():
            row = z - k
            r.nt[SPLIT:FEATURES] = r.own_x[row].astype(f32)
            for step in range(3):
                @pl.when((k > 0) | ((x + 1 + step) % 4 > x))
                def _():
                    ref = r.in_x.at[step, row]
                    remote(ref, ref, r.in_send.at[0, 0, 0], r.in_x_recv.at[step, row], (seq, h)).wait_recv()
                    r.nt[SPLIT:FEATURES] += r.in_x[step, row].astype(f32)

            if k == 0:
                r.own[SPLIT:FEATURES] = r.nt[SPLIT:FEATURES]
            else:
                r.out_z[k - 1] = r.nt[SPLIT:FEATURES].astype(bf)
                onward(r, seq, h, k, 1)[0].start()


def latents_sent(r, seq, h):
    for k in range(1, 4):
        for half in (0, 1):
            copy, sent = onward(r, seq, h, k, half)
            pl.when(sent)(copy.wait_send)


def finish_queries(r, me):
    for g in range(2):
        at, rope = (0, 256) if g == 0 else (48, 0)
        r.ot[g] = (r.acc[g, at : at + 256] * SCALE).astype(bf)
        for e in range(8):
            head = g * 8 + e
            cols = slice(e * 128, (e + 1) * 128)
            r.attt[head * 64 : (head + 1) * 64] = dot(r.kt[g, e * 64 : (e + 1) * 64], r.ot[g, :, cols]).astype(bf)
            turned = (r.acc[g, rope : rope + 32, cols] * SCALE).astype(bf).astype(f32)
            r.nt[head * 32 : (head + 1) * 32] = turn(turned, r.cos[...], -r.sin[...])
    r.n2[...] = r.attt[...].T
    r.gb[:, 0:512] = r.nt[0:512].T.astype(bf)
    for c in range(2):
        give(r, me, 1, 13 + c, r.n2[:, c * 256 : (c + 1) * 256])
        give(r, me, 2, 13 + c, r.n2[:, 512 + c * 256 : 768 + c * 256])
    for c in range(2):
        give(r, me, 0, 13 + c, r.gb[:, c * 256 : (c + 1) * 256])
    give_heads(r, me, 1, r.qt, r.ot)


def finish_latent(r, me, seq, h):
    z, x = h // 4, h % 4
    for k in range(3):
        @pl.when((z < 3) | ((x + 1 + k) % 4 > x))
        def _():
            ref = r.end_x.at[k]
            remote(ref, ref, r.out_send.at[0, 0], r.end_recv.at[0, k], (seq, h)).wait_recv()
            r.own[0:SPLIT] += r.end_x[k].astype(f32)

        @pl.when(z + 1 + k < 4)
        def _():
            ref = r.end_z.at[k]
            remote(ref, ref, r.out_send.at[0, 0], r.end_recv.at[1, k], (seq, h)).wait_recv()
            r.own[SPLIT:FEATURES] += r.end_z[k].astype(f32)

    r.gb[:, 512:768] = r.own[0:256].T.astype(bf)
    r.gb[:, 768:1024] = r.own[304:560].T.astype(bf)
    give(r, me, 1, 15, r.gb[:, 512:768])
    give(r, me, 2, 15, r.gb[:, 768:1024])
    turned = r.own[256:288].astype(bf).astype(f32)
    kr = turn(turned, r.cos[...], -r.sin[...])
    r.gkr[...] = jnp.concatenate([kr, jnp.zeros((96, 128), f32)], 0).T.astype(bf)


def finish_input(r):
    grad = dot(r.gkr[:, 0:32], r.wkr[...])
    for i in range(2):
        grad = grad + dot(r.n2[:, i * 512 : (i + 1) * 512], r.pool[i], 1, 1)
    grad = grad + dot(r.gb[:, 0:512], r.pool[2], 1, 1) + dot(r.gb[:, 512:1024], r.pool[3], 1, 1)
    x = r.x[...].astype(f32)
    inverse = lax.rsqrt(jnp.mean(x * x, -1, keepdims=True) + EPS)
    r.gains[0:1] = jnp.sum(grad * x * inverse, 0, keepdims=True)
    scaled = grad * r.gain1[...].astype(f32)[None]
    r.grad_input[...] = r.mid[...] + inverse * scaled - x * (inverse * inverse * inverse) * jnp.mean(x * scaled, -1, keepdims=True)
    result_copy(r, "grad_input").start()


def finish_rope(r, me):
    wide = jnp.concatenate([r.gkr[...], jnp.zeros((128, 128), bf)], 1)
    row = lax.broadcasted_iota(jnp.int32, (16, 256), 0)
    column = lax.broadcasted_iota(jnp.int32, (16, 256), 1)
    spread = ((row < 4) & (column == 32 + row // 2)).astype(bf)
    for mine in (True, False):
        core = me["core"] if mine else 1 - me["core"]
        for q in range(4):
            gains = r.gains[0:2, lanes(q * 256 + core * 128, 128)]
            high = gains.astype(bf).astype(f32)
            low = gains - high
            stack = jnp.concatenate([high[0:1], low[0:1], high[1:2], low[1:2], jnp.zeros((12, 128), f32)], 0).astype(bf)
            left = r.at[0, ONE, q * 128 : (q + 1) * 128, 0:128] if mine else r.at_send[0, ONE, q * 128 : (q + 1) * 128]
            block = (dot(left, wide) + dot(stack, spread, 0, 0)).astype(bf)
            if mine:
                r.dense[2, q, 0:128] = block
            else:
                r.dense_send[2, q] = block
    dense_copy(r, me, 2).start()


RESULTS = ("output", "grad_input", "sums")
SMALL = ("x", "gain1", "wkr", "kup", "vup", "cot", "gain2")
INPUTS = tuple(n + "_hbm" for n in SMALL) + ("second", "wq", "wqr", "wl", "wo_hbm", "wg", "wu", "wd")


def scratch():
    vm = lambda *shape, kind=bf: pltpu.VMEM(shape, kind)
    dma = pltpu.SemaphoreType.DMA
    return dict(
        x=vm(128, 1024), gain1=vm(1024), wkr=vm(32, 1024), kup=vm(2, 256, 512), vup=vm(2, 256, 512), cot=vm(128, 1024), gain2=vm(1024),
        output=vm(128, 1024), grad_input=vm(128, 1024, kind=f32), sums=vm(3, 8, JOBS * W, kind=f32),
        small_sem=dma((len(SMALL),)), result_sem=dma((3,)),
        pool=vm(4, 1024, 512), wdpool=vm(4, 256, 1024), wo=vm(1024, 1024),
        first_sem=dma((5,)), chunk_sem=dma((4, 3)),
        n1=vm(128, 1024), n2=vm(128, 1024), gb=vm(128, 1024), ga=vm(1024, 128), attt=vm(1024, 128),
        cos=vm(16, 128, kind=f32), sin=vm(16, 128, kind=f32),
        lx=vm(256, 640), lxt=vm(8, FEATURES, 256), qt=vm(1024, 128), kt=vm(2, 512, 256), vt=vm(2, 512, 256),
        qxt=vm(2, 384, 1024), p=vm(8, 2, 256, 1024), acc=vm(2, 384, 1024, kind=f32), ot=vm(2, 256, 1024),
        top=vm(8, 1024, kind=f32), total=vm(8, 1024, kind=f32), back=vm(8, 1024, kind=f32), tops=vm(16, 1024, kind=f32),
        gains=vm(8, 1024, kind=f32), mid=vm(128, 1024, kind=f32), g_acc=vm(128, 1024, kind=f32),
        gather_send=dma((10, 4)), gather_recv=dma((2, 16)),
        nt=vm(1024, 128, kind=f32), qxn=vm(2, 1024, 384), dn=vm(2, 1024, 256),
        inner=vm(8, 1024, kind=f32), own=vm(FEATURES, 128, kind=f32),
        in_z=vm(3, 4, SPLIT, 128), in_x=vm(3, 4, FEATURES - SPLIT, 128), own_z=vm(4, SPLIT, 128), own_x=vm(4, FEATURES - SPLIT, 128),
        out_x=vm(3, SPLIT, 128), out_z=vm(3, FEATURES - SPLIT, 128), end_x=vm(3, SPLIT, 128), end_z=vm(3, FEATURES - SPLIT, 128),
        in_send=dma((4, 2, 2)), in_z_recv=dma((3, 4)), in_x_recv=dma((3, 4)), out_send=dma((2, 4)), end_recv=dma((2, 3)),
        gkr=vm(128, 128),
        at=vm(3, 3, 512, 256), at_send=vm(3, 3, 512, 128), at_sem=dma((2, 3, 3)),
        g=vm(3, 16, 256, W), g_send=dma((3, 16)), g_recv=dma((3, 16)),
        dense=vm(3, 4, 256, W), dense_send=vm(3, 4, 128, W), dense_sem=dma((2, 3)),
        d=vm(3, RING, 512, W), s1=vm(3, 128, W, kind=f32), s2=vm(3, 32, W, kind=f32),
        own1=vm(3, RING, 32, W, kind=f32), own2=vm(3, RING, 8, W, kind=f32),
        part_send=dma((3, 2, 2, RING)), part_recv=dma((3, 2, 2, RING)),
        direct_send=dma((3, 2, 3, RING)), direct_recv=dma((3, 2, 3, RING)),
        **{
            side + name: vm(3, RING, *shape, kind=kind)
            for side in "sr"
            for name, shape, kind in (
                ("a", (2, 128, W // 2), bf), ("b", (2, 128, W), bf), ("c", (3, 32, W), bf), ("d", (3, 16, W // 2), bf),
            )
        },
    )


def kernel(names, *refs):
    r = types.SimpleNamespace(**dict(zip(names, refs)))
    seq, h = lax.axis_index("seq"), lax.axis_index("head")
    me = place()
    load_first(r)
    barrier = pltpu.get_barrier_semaphore()
    peers = [(seq, (h + k) % 16) for k in range(1, 16)] + [other_core(me), beside(me, "y", 1), beside(me, "y", 2), beside(me, "y", 3)]
    for peer in peers:
        pl.semaphore_signal(barrier, inc=1, device_id=peer, device_id_type=MESH)
    pl.semaphore_wait(barrier, len(peers))
    project(r, seq, h)
    gather_second(r, seq, h)
    r.nt[...] = r.cot[...].astype(f32).T
    choose_rows(r, me, 2, FEED)
    r.nt[...] = r.n1[...].astype(f32).T
    for order in range(3):
        choose_rows(r, me, order, ONE)
    attend(r, seq, h)
    r.nt[...] = r.attt[...].astype(f32)
    for order in (1, 2):
        choose_rows(r, me, order, OUT)

    def begin():
        r.nt[...] = r.n2[...].astype(f32).T
        for order in (0, 1):
            choose_rows(r, me, order, FEED)

    def each(j, grad_gate, grad_up, act):
        for order, value in enumerate((grad_gate, grad_up, act)):
            give(r, me, order, j, value)

        @pl.when(j == 1)
        def _():
            wait_rows(r, me, FEED)

        @pl.when((j == 1) | (j == 3) | (j == 5) | (j == 7) | (j == 9) | (j == 10))
        def _():
            sum_slot(r, me, sum(jnp.where(j > c, 1, 0) for c in (1, 3, 5, 7, 9, 10,)))

    feed(r, begin, each)
    load_first(r, again=True)
    for c in range(2):
        give(r, me, 1, 11 + c, r.gb[:, c * 256 : (c + 1) * 256])
        give(r, me, 2, 11 + c, r.gb[:, 512 + c * 256 : 768 + c * 256])
    give_heads(r, me, 0, r.ga, r.ot)
    prepare_back(r)
    wait_rows(r, me, OUT)

    @pl.loop(0, 8)
    def _(b):
        @pl.when(b <= h // 2)
        def _():
            back_step(r, seq, h, b)

        @pl.when((b == 1) | (b == 3) | (b == 5) | (b == 6))
        def _():
            sum_slot(r, me, 6 + sum(jnp.where(b > c, 1, 0) for c in (1, 3, 5, 6,)))

    finish_queries(r, me)
    wait_rows(r, me, ONE)
    sum_slot(r, me, 10)
    sum_slot(r, me, 11)
    sum_latents(r, seq, h)
    sum_slot(r, me, 12)
    sum_slot(r, me, 13)
    sum_slot(r, me, 14)
    finish_latent(r, me, seq, h)
    sum_slot(r, me, 15)
    for i in range(4):
        wait_first(r, i)
    finish_input(r)
    finish_rope(r, me)

    @pl.loop(16, 25)
    def _(t):
        sum_slot(r, me, t)

    result_copy(r, "sums").start()
    sum_end(r, me)
    back_sent(r, seq, h)
    latents_sent(r, seq, h)
    gather_sent(r, seq, h)
    for name in RESULTS:
        result_copy(r, name).wait()


def run(layer_input, second_start, mixer_gain, w_query, w_query_rope, w_latent, w_key_rope, w_key_up, w_value_up, w_out, feed_gain, w_gate, w_up, w_down, cotangent):
    args = dict(x_hbm=layer_input, cot_hbm=cotangent, second=second_start, gain1_hbm=mixer_gain, gain2_hbm=feed_gain,
        wkr_hbm=w_key_rope.T, kup_hbm=w_key_up, vup_hbm=w_value_up, wq=w_query, wqr=w_query_rope, wl=w_latent, wo_hbm=w_out, wg=w_gate, wu=w_up, wd=w_down)
    A, S = (pl.BlockSpec(memory_space=m) for m in (pl.ANY, pltpu.SMEM))
    specs = {n: S if n == "second" else A for n in INPUTS}
    outs = dict(output_hbm=((128, 1024), bf), grad_input_hbm=((128, 1024), f32), sums_hbm=((3, 8, JOBS * W), f32))
    sc = scratch()
    names = INPUTS + tuple(outs) + tuple(sc)
    output, grad_input, sums = pl.pallas_call(
        lambda *refs: kernel(names, *refs),
        out_shape=[jax.ShapeDtypeStruct(*o) for o in outs.values()],
        in_specs=[specs[n] for n in INPUTS], out_specs=[A] * len(outs),
        scratch_shapes=list(sc.values()),
        compiler_params=pltpu.CompilerParams(collective_id=0, has_side_effects=True, vmem_limit_bytes=66900000),
        name="layer",
    )(*[args[n] for n in INPUTS])

    return place_results(output, grad_input, sums)


def place_kernel(output, grad_input, sums, *outs):
    first, second, third = (sums.at[i] for i in range(3))
    outs[0][...] = output[...]
    outs[1][...] = grad_input[...]
    rope = first[:, 4096:4224]
    turned = jnp.concatenate([rope, jnp.zeros((120, 128), f32)], 0).T
    outs[2][...] = turned[32:33, 0:8]
    outs[3][:, 0:512] = second[:, 3328:3840]
    outs[3][:, 512:1024] = third[:, 3328:3840]
    outs[4][...] = first[:, 3328:3840]
    outs[5][:, 0:256] = second[:, 3840:4096]
    outs[5][:, 256:512] = third[:, 3840:4096]
    outs[6][...] = rope[:, 0:32]
    for g in range(2):
        outs[7][g] = first[g * 4 : g * 4 + 4, 3072:3328]
        outs[8][g] = first[g * 4 : g * 4 + 4, 2816:3072]
    outs[9][:, 0:512] = second[:, 2816:3328]
    outs[9][:, 512:1024] = third[:, 2816:3328]
    outs[10][...] = turned[33:34, 0:8]
    outs[11][...] = first[:, 0:2816]
    outs[12][...] = second[:, 0:2816]
    outs[13][...] = third[:, 0:2816]


def place_results(output, grad_input, sums):
    shapes = [(1, 8), (8, 1024), (8, 512), (8, 512), (8, 32), (2, 4, 256), (2, 4, 256), (8, 1024), (1, 8), (8, 2816), (8, 2816), (8, 2816)]
    outs = list(pl.pallas_call(
        place_kernel,
        out_shape=[jax.ShapeDtypeStruct((128, 1024), bf), jax.ShapeDtypeStruct((128, 1024), f32)]
        + [jax.ShapeDtypeStruct(shape, f32) for shape in shapes],
        name="place",
    )(output, grad_input, sums))
    for i in (2, 10):
        outs[i] = outs[i].reshape(8)
    for i in (7, 8):
        outs[i] = outs[i].transpose(0, 2, 1)
    outs[13] = outs[13].T
    return tuple(outs)


def solution(mesh):
    in_specs = (
        P(("seq", "head"), None),
        P("seq"),
        P(),
        P(),
        P(),
        P(),
        P(),
        P(),
        P(),
        P(),
        P(),
        P(),
        P(),
        P(),
        P(("seq", "head"), None),
    )
    out_specs = (
        P(("seq", "head"), None),
        P(("seq", "head"), None),
        P(("seq", "head")),
        P(("seq", "head"), None),
        P(("seq", "head"), None),
        P(("seq", "head"), None),
        P(("seq", "head"), None),
        P(None, None, ("seq", "head")),
        P(None, None, ("seq", "head")),
        P(("seq", "head"), None),
        P(("seq", "head")),
        P(("seq", "head"), None),
        P(("seq", "head"), None),
        P(None, ("seq", "head")),
    )
    return jax.shard_map(run, mesh=mesh, in_specs=in_specs, out_specs=out_specs, check_vma=False)
```

```python
import math
import types
import numpy as np
import jax
import jax.numpy as jnp
from jax import lax
from jax.experimental import pallas as pl
from jax.experimental.pallas import tpu as pltpu
from jax.sharding import PartitionSpec as P

MESH = pl.DeviceIdType.MESH
bf, f32 = jnp.bfloat16, jnp.float32
W = 256
EPS = 1e-6
RATES = [float(v) for v in 10000.0 ** (-np.arange(16) * 2.0 / 32)]
SCALE = 1.0 / math.sqrt(96)
DEPTH = 4
FEATURES, SPLIT = 560, 256


def dot(a, b, ca=1, cb=0):
    return lax.dot_general(a, b, (((ca,), (cb,)), ((), ())), preferred_element_type=f32)


def place():
    s, h = lax.axis_index("seq"), lax.axis_index("head")
    return {"y": s // 2, "core": s % 2, "z": h // 4, "x": h % 4}


def device(at):
    return (at["y"] * 2 + at["core"], at["z"] * 4 + at["x"])


def remote(src, dst, send, recv, to):
    return pltpu.make_async_remote_copy(
        src_ref=src, dst_ref=dst, send_sem=send, recv_sem=recv, device_id=to, device_id_type=MESH
    )


def lanes(start, size):
    return pl.ds(pl.multiple_of(start, size), size)


def rows_of(block):
    return pl.ds(pl.multiple_of((block % 2) * 128, 128), 128)


def turn(u, cosine, sine):
    first, second = u[..., :16, :], u[..., 16:, :]
    return jnp.concatenate([first * cosine - second * sine, first * sine + second * cosine], -2)


def small_copy(r, name):
    return pltpu.make_async_copy(getattr(r, name + "_hbm"), getattr(r, name), r.small_sem.at[SMALL.index(name)])


def result_copy(r, name):
    return pltpu.make_async_copy(getattr(r, name), getattr(r, name + "_hbm"), r.result_sem.at[RESULTS.index(name)])


def load_first(r, again=False):
    if not again:
        for name in SMALL:
            small_copy(r, name).start()
    for i in range(2):
        pltpu.make_async_copy(r.wq.at[:, i * 512 : (i + 1) * 512], r.pool.at[i], r.first_sem.at[i]).start()
    pltpu.make_async_copy(r.wqr, r.pool.at[2], r.first_sem.at[2]).start()
    pltpu.make_async_copy(r.wl, r.pool.at[3], r.first_sem.at[3]).start()
    if not again:
        pltpu.make_async_copy(r.wo_hbm, r.wo, r.first_sem.at[4]).start()


def wait_first(r, i):
    ref = r.wo if i == 4 else r.pool.at[i]
    pltpu.make_async_copy(ref, ref, r.first_sem.at[i]).wait()


def chunk_copies(r, j):
    slot = j % DEPTH
    here = lanes(j * W, W)
    return (
        pltpu.make_async_copy(r.wg.at[:, here], r.pool.at[slot, :, 0:W], r.chunk_sem.at[slot, 0]),
        pltpu.make_async_copy(r.wu.at[:, here], r.pool.at[slot, :, W : 2 * W], r.chunk_sem.at[slot, 1]),
        pltpu.make_async_copy(r.wd.at[here, :], r.wdpool.at[slot], r.chunk_sem.at[slot, 2]),
    )


def project(r, seq, h):
    for name in ("x", "gain1", "wkr"):
        small_copy(r, name).wait()
    x = r.x[...].astype(f32)
    inverse = lax.rsqrt(jnp.mean(x * x, -1, keepdims=True) + EPS)
    n1 = (x * inverse * r.gain1[...].astype(f32)[None]).astype(bf)
    r.n1[...] = n1
    bound = r.second[0]
    token = h * 128 + lax.broadcasted_iota(jnp.int32, (16, 128), 1)
    position = token - jnp.where(token >= bound, bound, 0)
    step = lax.broadcasted_iota(jnp.int32, (16, 128), 0)
    rate = jnp.ones((16, 128), f32)
    for i in range(1, 16):
        rate = jnp.where(step == i, RATES[i], rate)
    angle = position.astype(f32) * rate
    cosine, sine = jnp.cos(angle), jnp.sin(angle)
    r.cos[...], r.sin[...] = cosine, sine
    wait_first(r, 3)
    lat = dot(n1, r.pool[3]).astype(bf)
    kr = turn(dot(r.wkr[...], n1, 1, 1), cosine, sine)
    flag = jnp.where(h == 15, 0.0, 1.0)
    flags = jnp.where(lax.broadcasted_iota(jnp.int32, (16, 128), 0) == 0, flag, 0.0)
    latt = lat.T
    mine = r.lxt.at[h // 2, :, lanes((h % 2) * 128, 128)]
    mine[0:256] = latt[0:256]
    mine[256:304] = jnp.concatenate([kr, flags], 0).astype(bf)
    mine[304:560] = latt[256:512]

    @pl.when(h % 2 == 0)
    def _():
        r.lxt[h // 2, SPLIT:FEATURES, 128:256] = jnp.zeros((FEATURES - SPLIT, 128), bf)

    gather_first(r, seq, h)

    for i in range(2):
        wait_first(r, i)
        r.qt[i * 512 : (i + 1) * 512] = dot(n1, r.pool[i]).T.astype(bf)
    wait_first(r, 2)
    qr = (turn(dot(n1, r.pool[2]).T.reshape(16, 32, 128), cosine, sine) * SCALE).astype(bf)
    for j in range(DEPTH):
        for copy in chunk_copies(r, j):
            copy.start()
    late = (h * 128 + (lax.broadcasted_iota(jnp.int32, (96, 1024), 1) & 127)) >= bound
    bias = jnp.where(late & (lax.broadcasted_iota(jnp.int32, (96, 1024), 0) == 0), -1e30, 0.0).astype(bf)
    for name in ("kup", "vup", "cot", "gain2"):
        small_copy(r, name).wait()
    for g in range(2):
        r.kt[g] = r.kup[g].T
        r.vt[g] = r.vup[g].T
        at, rope = (0, 256) if g == 0 else (128, 0)
        r.qxt[g, rope + 32 : rope + 128] = bias
        for e in range(8):
            head = g * 8 + e
            cols = slice(e * 128, (e + 1) * 128)
            r.qxt[g, rope : rope + 32, cols] = qr[head]
            r.qxt[g, at : at + 256, cols] = (
                dot(r.kt[g, e * 64 : (e + 1) * 64, :], r.qt[head * 64 : (head + 1) * 64], 0, 0) * SCALE
            ).astype(bf)


def latent_half(r, i, half):
    rows = slice(0, SPLIT) if half == 0 else slice(SPLIT, FEATURES)
    return r.lxt.at[i // 2, rows, lanes((i % 2) * 128, 128)]


def gather_copy(r, seq, i, half, send, to):
    ref = latent_half(r, i, half)
    return remote(ref, ref, send, r.gather_recv.at[half, i], (seq, to))


def first_targets(r, seq, h):
    z, x = h // 4, h % 4
    for k in range(1, 4):
        there = (z + k) % 4
        yield True, gather_copy(r, seq, h, 0, r.gather_send.at[0, k], z * 4 + (x + k) % 4)
        yield there > z, gather_copy(r, seq, h, 1, r.gather_send.at[1, k], there * 4 + x)


def second_targets(r, seq, h):
    z, x = h // 4, h % 4
    for j in range(4):
        i = z * 4 + (x + j) % 4
        sends = []
        for k in range(1, 4):
            there = (z + k) % 4
            sends.append((there > z, gather_copy(r, seq, i, 0, r.gather_send.at[2 + j, k], there * 4 + x)))
        yield (j > 0), gather_copy(r, seq, i, 0, r.gather_send.at[0, 0], h), sends
        row = (z + 4 - j) % 4
        i = row * 4 + x
        sends = []
        for k in range(1, 4):
            there = (x + k) % 4
            sends.append(((row < z) | ((row == z) & (there > x)), gather_copy(r, seq, i, 1, r.gather_send.at[6 + j, k], z * 4 + there)))
        yield (row < z), gather_copy(r, seq, i, 1, r.gather_send.at[0, 0], h), sends


def gather_first(r, seq, h):
    for use, copy in first_targets(r, seq, h):
        pl.when(use)(copy.start)


def gather_second(r, seq, h):
    for use, copy, sends in second_targets(r, seq, h):
        pl.when(use)(copy.wait_recv)
        for wanted, send in sends:
            pl.when(wanted)(send.start)


def gather_sent(r, seq, h):
    for use, copy in first_targets(r, seq, h):
        pl.when(use)(copy.wait_send)
    for _, _, sends in second_targets(r, seq, h):
        for wanted, send in sends:
            pl.when(wanted)(send.wait_send)


def gather_wait(r, seq, h, i):
    pl.when((i < h) & (i // 4 != h // 4))(gather_copy(r, seq, i, 0, r.gather_send.at[0, 0], h).wait_recv)
    pl.when((i < h) & (i % 4 != h % 4))(gather_copy(r, seq, i, 1, r.gather_send.at[0, 0], h).wait_recv)


def load_latents(r, b):
    r.lx[:, 0:256] = r.lxt[b, 0:256].T
    r.lx[:, 256:384] = jnp.concatenate([r.lxt[b, 256:304], jnp.zeros((80, 256), bf)], 0).T
    r.lx[:, 384:640] = r.lxt[b, 304:560].T


def attend_step(r, seq, h, b, diag):
    gather_wait(r, seq, h, 2 * b)
    gather_wait(r, seq, h, 2 * b + 1)
    load_latents(r, b)
    wide = 512
    units = [(g, slice(c * wide, (c + 1) * wide)) for g in range(2) for c in range(1024 // wide)]
    scores = [dot(r.lx[:, g * 256 : g * 256 + 384], r.qxt[g, :, cols]) for g, cols in units]
    if diag:
        bound = r.second[0]
        key = b * 256 + lax.broadcasted_iota(jnp.int32, (256, 128), 0)
        row = h * 128 + lax.broadcasted_iota(jnp.int32, (256, 128), 1)
        ok = (key <= row) & ((key >= bound) == (row >= bound))
        barred = jnp.where(ok, 0.0, 1.0)
        barred = jnp.concatenate([barred] * (wide // 128), 1)
    kept = []
    for (g, cols), s in zip(units, scores):
        if diag:
            s = jnp.where(barred > 0.5, -1e30, s)
        top = jnp.max(s, 0, keepdims=True)
        fade = None
        if not diag:
            before = r.top[g : g + 1, cols]
            top = jnp.maximum(top, before)
            fade = jnp.exp(before - top)
        p = jnp.exp(s - top)
        total = jnp.sum(p, 0, keepdims=True)
        if not diag:
            total = total + r.total[g : g + 1, cols] * fade
        p = p.astype(bf)
        r.p[b, g, :, cols] = p
        r.total[g : g + 1, cols] = total
        r.top[g : g + 1, cols] = top
        r.tops[pl.ds(b * 2 + g, 1), cols] = top
        kept.append((p, fade))
    for (g, cols), (p, fade) in zip(units, kept):
        at = 0 if g == 0 else 304
        o = dot(r.lxt[b, at : at + 256], p)
        r.acc[g, 0:256, cols] = o if diag else o + r.acc[g, 0:256, cols] * fade


def attend(r, seq, h):
    last = h // 2
    attend_step(r, seq, h, last, True)

    @pl.loop(0, last)
    def _(i):
        attend_step(r, seq, h, last - 1 - i, False)

    for g in range(2):
        back = 1.0 / r.total[g : g + 1]
        r.back[g : g + 1] = back
        r.ot[g] = (r.acc[g, 0:256] * back).astype(bf)
        for e in range(8):
            head = g * 8 + e
            r.attt[head * 64 : (head + 1) * 64] = dot(
                r.vt[g, e * 64 : (e + 1) * 64], r.ot[g, :, e * 128 : (e + 1) * 128]
            ).astype(bf)


def feed(r, begin, each):
    wait_first(r, 4)
    r.mid[...] = r.x[...].astype(f32) + dot(r.attt[...].T, r.wo[...])
    mid = r.mid[...]
    inverse = lax.rsqrt(jnp.mean(mid * mid, -1, keepdims=True) + EPS)
    gain = r.gain2[...].astype(f32)[None]
    r.n2[...] = (mid * inverse * gain).astype(bf)
    r.grad_input[...] = mid
    r.g_acc[...] = jnp.zeros((128, 1024), f32)
    begin()

    @pl.loop(0, 11)
    def _(j):
        slot = j % DEPTH
        for copy in chunk_copies(r, j):
            copy.wait()
        n2, cot = r.n2[...], r.cot[...]
        both = dot(n2, r.pool[slot])
        grad = dot(cot, r.wdpool[slot], 1, 1)
        gate, up = both[:, :W], both[:, W:]
        sigma = jax.nn.sigmoid(gate)
        swish = gate * sigma
        act = (swish * up).astype(bf)
        grad_gate = (grad * up * sigma * (1.0 + gate * (1.0 - sigma))).astype(bf)
        grad_up = (grad * swish).astype(bf)
        out = dot(act, r.wdpool[slot])
        back = dot(jnp.concatenate([grad_gate, grad_up], 1), r.pool[slot], 1, 1)
        r.grad_input[...] += out
        r.g_acc[...] += back

        @pl.when(j + DEPTH < 11)
        def _():
            for copy in chunk_copies(r, j + DEPTH):
                copy.start()

        each(j, grad_gate, grad_up, act)

    r.output[...] = r.grad_input[...].astype(bf)
    result_copy(r, "output").start()
    up = r.g_acc[...]
    mid = r.mid[...]
    inverse = lax.rsqrt(jnp.mean(mid * mid, -1, keepdims=True) + EPS)
    r.gains[1:2] = jnp.sum(up * mid * inverse, 0, keepdims=True)
    scaled = up * gain
    grad_mid = r.cot[...].astype(f32) + inverse * scaled - mid * (inverse * inverse * inverse) * jnp.mean(mid * scaled, -1, keepdims=True)
    r.mid[...] = grad_mid
    r.gb[...] = grad_mid.astype(bf)
    r.ga[...] = dot(r.gb[...], r.wo[...], 1, 1).T.astype(bf)


RING = 4
ORDERS = (("y", "z", "x"), ("z", "y", "x"), ("x", "y", "z"))
JOBS = 17
FEED, OUT, ONE = 0, 1, 2


def beside(at, axis, step):
    return device({**at, axis: (at[axis] + step) % 4})


def other_core(at):
    return device({**at, "core": 1 - at["core"]})


def choose_rows(r, me, order, which):
    for mine in (True, False):
        core = me["core"] if mine else 1 - me["core"]
        parts = []
        for i in range(64):
            part = dict(zip(ORDERS[order], (i >> 4, (i >> 2) & 3, i & 3)))
            start = part["y"] * 256 + part["z"] * 32 + part["x"] * 8
            parts.append(r.nt[pl.ds(pl.multiple_of(core * 128 + start, 8), 8), :])
        picked = jnp.concatenate(parts, 0).astype(bf)
        if mine:
            r.at[order, which, :, 0:128] = picked
        else:
            r.at_send[order, which] = picked
    at_copy(r, me, order, which).start()


def at_copy(r, me, order, which):
    return remote(
        r.at_send.at[order, which], r.at.at[order, which, :, 128:256],
        r.at_sem.at[0, order, which], r.at_sem.at[1, order, which], other_core(me),
    )


def g_copy(r, me, order, job):
    return remote(
        r.g.at[order, job, 0:128], r.g.at[order, job, 128:256],
        r.g_send.at[order, job], r.g_recv.at[order, job], other_core(me),
    )


def give(r, me, order, job, value):
    r.g[order, job, 0:128] = value
    g_copy(r, me, order, job).start()


def dense_copy(r, me, which):
    return remote(
        r.dense_send.at[which], r.dense.at[which, :, 128:256],
        r.dense_sem.at[0, which], r.dense_sem.at[1, which], other_core(me),
    )


def give_heads(r, me, which, left, right):
    for mine in (True, False):
        core = me["core"] if mine else 1 - me["core"]
        for q in range(4):
            for g in range(2):
                e = q * 2 + core
                rows = lanes((g * 8 + e) * 64, 64)
                block = dot(left[rows, :], right[g, :, lanes(e * 128, 128)], 1, 1).astype(bf)
                if mine:
                    r.dense[which, q, g * 64 : g * 64 + 64] = block
                else:
                    r.dense_send[which, q, g * 64 : g * 64 + 64] = block
    dense_copy(r, me, which).start()


def part_copy(r, me, order, way, job, whole):
    slot, kind = job % RING, "b" if whole else "a"
    return remote(
        getattr(r, "s" + kind).at[order, slot, way],
        getattr(r, "r" + kind).at[order, slot, way],
        r.part_send.at[order, int(whole), way, slot],
        r.part_recv.at[order, int(whole), way, slot],
        beside(me, ORDERS[order][0], 1 if way == 0 else -1),
    )


def direct_copy(r, me, order, stage, k, job):
    slot, kind = job % RING, "c" if stage == 1 else "d"
    return remote(
        getattr(r, "s" + kind).at[order, slot, k - 1],
        getattr(r, "r" + kind).at[order, slot, k - 1],
        r.direct_send.at[order, stage - 1, k - 1, slot],
        r.direct_recv.at[order, stage - 1, k - 1, slot],
        beside(me, ORDERS[order][stage], k),
    )


def sends_of(r, me, k, job, orders):
    for order in orders:
        if k < 2:
            for way in (0, 1):
                yield part_copy(r, me, order, way, job, k == 1)
        else:
            for step in (1, 2, 3):
                yield direct_copy(r, me, order, k - 1, step, job)


def products(r, me, job, orders):
    slot = job % RING

    def plain(which, orders):
        for order in orders:
            g_copy(r, me, order, job).wait_recv()
        blocks = [dot(r.at[order, which], r.g[order, job]) for order in orders]
        for order, block in zip(orders, blocks):
            r.d[order, slot] = block.astype(bf)

    def thick(which):
        dense_copy(r, me, which).wait_recv()
        row = lax.broadcasted_iota(jnp.int32, (128, 256), 0)
        column = lax.broadcasted_iota(jnp.int32, (128, 256), 1) & 127
        if which < 2:
            row = ((row >> 2) & 1) * 64 + (row >> 3) * 4 + (row & 3)
        pick = (row == column).astype(bf)
        blocks = [dot(pick, r.dense[which, q]) for q in range(4)]
        for q in range(4):
            r.d[0, slot, q * 128 : (q + 1) * 128] = blocks[q].astype(bf)

    if len(orders) == 1:
        thick(2)
        return
    pl.when(job < 11)(lambda: plain(FEED, (0, 1, 2)))
    pl.when((job == 13) | (job == 14))(lambda: plain(ONE, (0, 1, 2)))
    for number, kind, others in ((11, 0, OUT), (12, 1, OUT)):
        @pl.when(job == number)
        def _():
            thick(kind)
            plain(others, (1, 2))

    pl.when(job == 15)(lambda: plain(ONE, (1, 2)))


def rows_from(ref, index, count):
    return ref[lanes(index * count, count), :]


def sum_step(r, me, k, job, orders):
    slot = job % RING
    if k == 0:
        products(r, me, job, orders)
    if k < 4:
        @pl.when(job >= RING)
        def _():
            for copy in sends_of(r, me, k, job - RING, orders):
                copy.wait_send()

    if k:
        for copy in sends_of(r, me, k - 1, job, orders):
            copy.wait_recv()
    place_of = [[me[axis] for axis in ORDERS[order]] for order in range(3)]
    if k == 0:
        for order in orders:
            opposite = rows_from(r.d.at[order, slot], (place_of[order][0] + 2) % 4, 128)
            for way in (0, 1):
                r.sa[order, slot, way] = opposite[:, way * (W // 2) : (way + 1) * (W // 2)]
    elif k == 1:
        for order in orders:
            for way in (0, 1):
                block = rows_from(r.d.at[order, slot], (place_of[order][0] + (1 if way == 0 else 3)) % 4, 128)
                here = slice(way * (W // 2), (way + 1) * (W // 2))
                there = slice((1 - way) * (W // 2), (2 - way) * (W // 2))
                r.sb[order, slot, way, :, here] = (block[:, here].astype(f32) + r.ra[order, slot, way].astype(f32)).astype(bf)
                r.sb[order, slot, way, :, there] = block[:, there]
    elif k == 2:
        for order in orders:
            own = rows_from(r.d.at[order, slot], place_of[order][0], 128).astype(f32)
            r.s1[order] = own + r.rb[order, slot, 0].astype(f32) + r.rb[order, slot, 1].astype(f32)
        for order in orders:
            for step in (1, 2, 3):
                r.sc[order, slot, step - 1] = rows_from(r.s1.at[order], (place_of[order][1] + step) % 4, 32).astype(bf)
            r.own1[order, slot] = rows_from(r.s1.at[order], place_of[order][1], 32)
    elif k == 3:
        for order in orders:
            block = r.own1[order, slot]
            for step in range(3):
                block = block + r.rc[order, slot, step].astype(f32)
            r.s2[order] = block
        for order in orders:
            for step in (1, 2, 3):
                block = rows_from(r.s2.at[order], (place_of[order][2] + step) % 4, 8)
                r.sd[order, slot, step - 1] = jnp.concatenate([block[:, : W // 2], block[:, W // 2 :]], 0).astype(bf)
            r.own2[order, slot] = rows_from(r.s2.at[order], place_of[order][2], 8)
    else:
        for order in orders:
            block = r.own2[order, slot]
            for step in range(3):
                got = r.rd[order, slot, step].astype(f32)
                block = block + jnp.concatenate([got[:8], got[8:]], 1)
            r.sums[order, :, lanes(job * W, W)] = block
    if k < 4:
        for copy in sends_of(r, me, k, job, orders):
            copy.start()


def sum_slot(r, me, t):
    for k in reversed(range(5)):
        job = t - 2 * k

        @pl.when((job >= 0) & (job < JOBS - 1))
        def _():
            sum_step(r, me, k, job, (0, 1, 2))

        @pl.when(job == JOBS - 1)
        def _():
            sum_step(r, me, k, job, (0,))


def sum_end(r, me):
    for k in range(4):
        for back in range(RING):
            for copy in (*sends_of(r, me, k, JOBS - 1 - back, (0,)), *sends_of(r, me, k, JOBS - 2 - back, (1, 2))):
                copy.wait_send()
    for order in range(3):
        for job in range(16):
            if order or job < 11 or job in (13, 14):
                g_copy(r, me, order, job).wait_send()
        for which in (FEED, OUT, ONE):
            if order or which != OUT:
                at_copy(r, me, order, which).wait_send()
    for which in range(3):
        dense_copy(r, me, which).wait_send()


def wait_rows(r, me, which):
    for order in range(3):
        if order or which != OUT:
            at_copy(r, me, order, which).wait_recv()


def prepare_back(r):
    for g in range(2):
        r.qxn[g] = r.qxt[g].T
        for e in range(8):
            head = g * 8 + e
            cols = slice(e * 128, (e + 1) * 128)
            ga = r.ga[head * 64 : (head + 1) * 64]
            back = r.back[g : g + 1, cols]
            inner = jnp.sum(ga.astype(f32) * r.attt[head * 64 : (head + 1) * 64].astype(f32), 0, keepdims=True)
            r.inner[g : g + 1, cols] = inner * back
            r.qxt[g, 0:256, cols] = (dot(r.vt[g, e * 64 : (e + 1) * 64, :], ga, 0, 0) * back).astype(bf)
        r.dn[g] = r.qxt[g, 0:256].T
    r.acc[...] = jnp.zeros((2, 384, 1024), f32)
    r.own_z[...] = jnp.zeros((4, SPLIT, 128), bf)


def inward(r, seq, h, b, s, half):
    z, x = h // 4, h % 4
    row, column = b // 2, (2 * b + s) % 4
    slot = b % 4
    cols = lanes(slot * 256 + s * 128, 128)
    if half == 0:
        src, step = r.wo.at[0:SPLIT, cols], (z - row + 3) % 4
        copy = remote(src, r.in_z.at[step, column], r.in_send.at[slot, s, 0], r.in_z_recv.at[step, column], (seq, row * 4 + x))
        return copy, row < z, (row == z) & (2 * b + s <= h)
    src, step = r.wo.at[SPLIT:FEATURES, cols], (x - column + 3) % 4
    copy = remote(src, r.in_x.at[step, row], r.in_send.at[slot, s, 1], r.in_x_recv.at[step, row], (seq, z * 4 + column))
    return copy, (column != x) & (2 * b + s < h), (column == x) & (2 * b + s <= h)


def back_step(r, seq, h, b):
    @pl.when(b >= 4)
    def _():
        for s in (0, 1):
            for half in (0, 1):
                copy, sent, _ = inward(r, seq, h, b - 4, s, half)
                pl.when(sent)(copy.wait_send)

    load_latents(r, b)
    cols = lanes((b % 4) * 256, 256)
    for g, at in ((0, 0), (1, 384)):
        dp = dot(r.lx[:, at : at + 256], r.qxt[g, 0:256])
        p = r.p[b, g].astype(f32) * jnp.exp(r.tops[pl.ds(b * 2 + g, 1)] - r.top[g : g + 1])
        ds = (p * (dp - r.inner[g : g + 1])).astype(bf)
        gl = dot(ds, r.qxn[g])
        gp = dot(p.astype(bf), r.dn[g])
        r.acc[g, 0:304] += dot(r.lxt[b, g * 256 : g * 256 + 304], ds)
        if g == 0:
            r.wo[0:256, cols] = (gl[:, 0:256] + gp).astype(bf).T
            rope = gl[:, 256:384]
        else:
            r.wo[256:304, cols] = (rope + gl[:, 0:128]).astype(bf).T[0:48]
            r.wo[304:560, cols] = (gl[:, 128:384] + gp).astype(bf).T
    for s in (0, 1):
        for half in (0, 1):
            copy, sent, stays = inward(r, seq, h, b, s, half)
            pl.when(sent)(copy.start)

            @pl.when(stays)
            def _():
                cols = lanes((b % 4) * 256 + s * 128, 128)
                if half == 0:
                    r.own_z[(2 * b + s) % 4] = r.wo[0:SPLIT, cols]
                else:
                    r.own_x[b // 2] = r.wo[SPLIT:FEATURES, cols]


def back_sent(r, seq, h):
    last = h // 2
    for d in range(4):
        b = last - d
        for s in (0, 1):
            for half in (0, 1):
                copy, sent, _ = inward(r, seq, h, b, s, half)
                pl.when((b >= 0) & sent)(copy.wait_send)


def onward(r, seq, h, k, half):
    z, x = h // 4, h % 4
    if half == 0:
        column = (x + k) % 4
        copy = remote(r.out_x.at[k - 1], r.end_x.at[3 - k], r.out_send.at[0, k], r.end_recv.at[0, 3 - k], (seq, z * 4 + column))
        return copy, (z < 3) | (column < x)
    row = z - k
    copy = remote(r.out_z.at[k - 1], r.end_z.at[k - 1], r.out_send.at[1, k], r.end_recv.at[1, k - 1], (seq, (row % 4) * 4 + x))
    return copy, row >= 0


def sum_latents(r, seq, h):
    z, x = h // 4, h % 4
    for k in range(4):
        column = (x + k) % 4
        r.nt[0:SPLIT] = jnp.where((column <= x), r.own_z[column].astype(f32), 0.0)
        for step in range(3):
            @pl.when(z + 1 + step < 4)
            def _():
                ref = r.in_z.at[step, column]
                remote(ref, ref, r.in_send.at[0, 0, 0], r.in_z_recv.at[step, column], (seq, h)).wait_recv()
                r.nt[0:SPLIT] += r.in_z[step, column].astype(f32)

        if k == 0:
            r.own[0:SPLIT] = r.nt[0:SPLIT]
        else:
            r.out_x[k - 1] = r.nt[0:SPLIT].astype(bf)
            copy, sent = onward(r, seq, h, k, 0)
            pl.when(sent)(copy.start)
    for k in range(4):
        @pl.when(z - k >= 0)
        def _():
            row = z - k
            r.nt[SPLIT:FEATURES] = r.own_x[row].astype(f32)
            for step in range(3):
                @pl.when((k > 0) | ((x + 1 + step) % 4 > x))
                def _():
                    ref = r.in_x.at[step, row]
                    remote(ref, ref, r.in_send.at[0, 0, 0], r.in_x_recv.at[step, row], (seq, h)).wait_recv()
                    r.nt[SPLIT:FEATURES] += r.in_x[step, row].astype(f32)

            if k == 0:
                r.own[SPLIT:FEATURES] = r.nt[SPLIT:FEATURES]
            else:
                r.out_z[k - 1] = r.nt[SPLIT:FEATURES].astype(bf)
                onward(r, seq, h, k, 1)[0].start()


def latents_sent(r, seq, h):
    for k in range(1, 4):
        for half in (0, 1):
            copy, sent = onward(r, seq, h, k, half)
            pl.when(sent)(copy.wait_send)


def finish_queries(r, me):
    for g in range(2):
        at, rope = (0, 256) if g == 0 else (48, 0)
        r.ot[g] = (r.acc[g, at : at + 256] * SCALE).astype(bf)
        for e in range(8):
            head = g * 8 + e
            cols = slice(e * 128, (e + 1) * 128)
            r.attt[head * 64 : (head + 1) * 64] = dot(r.kt[g, e * 64 : (e + 1) * 64], r.ot[g, :, cols]).astype(bf)
            turned = (r.acc[g, rope : rope + 32, cols] * SCALE).astype(bf).astype(f32)
            r.nt[head * 32 : (head + 1) * 32] = turn(turned, r.cos[...], -r.sin[...])
    r.n2[...] = r.attt[...].T
    r.gb[:, 0:512] = r.nt[0:512].T.astype(bf)
    for c in range(2):
        give(r, me, 1, 13 + c, r.n2[:, c * 256 : (c + 1) * 256])
        give(r, me, 2, 13 + c, r.n2[:, 512 + c * 256 : 768 + c * 256])
    for c in range(2):
        give(r, me, 0, 13 + c, r.gb[:, c * 256 : (c + 1) * 256])
    give_heads(r, me, 1, r.qt, r.ot)


def finish_latent(r, me, seq, h):
    z, x = h // 4, h % 4
    for k in range(3):
        @pl.when((z < 3) | ((x + 1 + k) % 4 > x))
        def _():
            ref = r.end_x.at[k]
            remote(ref, ref, r.out_send.at[0, 0], r.end_recv.at[0, k], (seq, h)).wait_recv()
            r.own[0:SPLIT] += r.end_x[k].astype(f32)

        @pl.when(z + 1 + k < 4)
        def _():
            ref = r.end_z.at[k]
            remote(ref, ref, r.out_send.at[0, 0], r.end_recv.at[1, k], (seq, h)).wait_recv()
            r.own[SPLIT:FEATURES] += r.end_z[k].astype(f32)

    r.gb[:, 512:768] = r.own[0:256].T.astype(bf)
    r.gb[:, 768:1024] = r.own[304:560].T.astype(bf)
    give(r, me, 1, 15, r.gb[:, 512:768])
    give(r, me, 2, 15, r.gb[:, 768:1024])
    turned = r.own[256:288].astype(bf).astype(f32)
    kr = turn(turned, r.cos[...], -r.sin[...])
    r.gkr[...] = jnp.concatenate([kr, jnp.zeros((96, 128), f32)], 0).T.astype(bf)


def finish_input(r):
    grad = dot(r.gkr[:, 0:32], r.wkr[...])
    for i in range(2):
        grad = grad + dot(r.n2[:, i * 512 : (i + 1) * 512], r.pool[i], 1, 1)
    grad = grad + dot(r.gb[:, 0:512], r.pool[2], 1, 1) + dot(r.gb[:, 512:1024], r.pool[3], 1, 1)
    x = r.x[...].astype(f32)
    inverse = lax.rsqrt(jnp.mean(x * x, -1, keepdims=True) + EPS)
    r.gains[0:1] = jnp.sum(grad * x * inverse, 0, keepdims=True)
    scaled = grad * r.gain1[...].astype(f32)[None]
    r.grad_input[...] = r.mid[...] + inverse * scaled - x * (inverse * inverse * inverse) * jnp.mean(x * scaled, -1, keepdims=True)
    result_copy(r, "grad_input").start()


def finish_rope(r, me):
    wide = jnp.concatenate([r.gkr[...], jnp.zeros((128, 128), bf)], 1)
    row = lax.broadcasted_iota(jnp.int32, (16, 256), 0)
    column = lax.broadcasted_iota(jnp.int32, (16, 256), 1)
    spread = ((row < 4) & (column == 32 + row // 2)).astype(bf)
    for mine in (True, False):
        core = me["core"] if mine else 1 - me["core"]
        for q in range(4):
            gains = r.gains[0:2, lanes(q * 256 + core * 128, 128)]
            high = gains.astype(bf).astype(f32)
            low = gains - high
            stack = jnp.concatenate([high[0:1], low[0:1], high[1:2], low[1:2], jnp.zeros((12, 128), f32)], 0).astype(bf)
            left = r.at[0, ONE, q * 128 : (q + 1) * 128, 0:128] if mine else r.at_send[0, ONE, q * 128 : (q + 1) * 128]
            block = (dot(left, wide) + dot(stack, spread, 0, 0)).astype(bf)
            if mine:
                r.dense[2, q, 0:128] = block
            else:
                r.dense_send[2, q] = block
    dense_copy(r, me, 2).start()


RESULTS = ("output", "grad_input", "sums")
SMALL = ("x", "gain1", "wkr", "kup", "vup", "cot", "gain2")
INPUTS = tuple(n + "_hbm" for n in SMALL) + ("second", "wq", "wqr", "wl", "wo_hbm", "wg", "wu", "wd")


def scratch():
    vm = lambda *shape, kind=bf: pltpu.VMEM(shape, kind)
    dma = pltpu.SemaphoreType.DMA
    return dict(
        x=vm(128, 1024), gain1=vm(1024), wkr=vm(32, 1024), kup=vm(2, 256, 512), vup=vm(2, 256, 512), cot=vm(128, 1024), gain2=vm(1024),
        output=vm(128, 1024), grad_input=vm(128, 1024, kind=f32), sums=vm(3, 8, JOBS * W, kind=f32),
        small_sem=dma((len(SMALL),)), result_sem=dma((3,)),
        pool=vm(4, 1024, 512), wdpool=vm(4, 256, 1024), wo=vm(1024, 1024),
        first_sem=dma((5,)), chunk_sem=dma((4, 3)),
        n1=vm(128, 1024), n2=vm(128, 1024), gb=vm(128, 1024), ga=vm(1024, 128), attt=vm(1024, 128),
        cos=vm(16, 128, kind=f32), sin=vm(16, 128, kind=f32),
        lx=vm(256, 640), lxt=vm(8, FEATURES, 256), qt=vm(1024, 128), kt=vm(2, 512, 256), vt=vm(2, 512, 256),
        qxt=vm(2, 384, 1024), p=vm(8, 2, 256, 1024), acc=vm(2, 384, 1024, kind=f32), ot=vm(2, 256, 1024),
        top=vm(8, 1024, kind=f32), total=vm(8, 1024, kind=f32), back=vm(8, 1024, kind=f32), tops=vm(16, 1024, kind=f32),
        gains=vm(8, 1024, kind=f32), mid=vm(128, 1024, kind=f32), g_acc=vm(128, 1024, kind=f32),
        gather_send=dma((10, 4)), gather_recv=dma((2, 16)),
        nt=vm(1024, 128, kind=f32), qxn=vm(2, 1024, 384), dn=vm(2, 1024, 256),
        inner=vm(8, 1024, kind=f32), own=vm(FEATURES, 128, kind=f32),
        in_z=vm(3, 4, SPLIT, 128), in_x=vm(3, 4, FEATURES - SPLIT, 128), own_z=vm(4, SPLIT, 128), own_x=vm(4, FEATURES - SPLIT, 128),
        out_x=vm(3, SPLIT, 128), out_z=vm(3, FEATURES - SPLIT, 128), end_x=vm(3, SPLIT, 128), end_z=vm(3, FEATURES - SPLIT, 128),
        in_send=dma((4, 2, 2)), in_z_recv=dma((3, 4)), in_x_recv=dma((3, 4)), out_send=dma((2, 4)), end_recv=dma((2, 3)),
        gkr=vm(128, 128),
        at=vm(3, 3, 512, 256), at_send=vm(3, 3, 512, 128), at_sem=dma((2, 3, 3)),
        g=vm(3, 16, 256, W), g_send=dma((3, 16)), g_recv=dma((3, 16)),
        dense=vm(3, 4, 256, W), dense_send=vm(3, 4, 128, W), dense_sem=dma((2, 3)),
        d=vm(3, RING, 512, W), s1=vm(3, 128, W, kind=f32), s2=vm(3, 32, W, kind=f32),
        own1=vm(3, RING, 32, W, kind=f32), own2=vm(3, RING, 8, W, kind=f32),
        part_send=dma((3, 2, 2, RING)), part_recv=dma((3, 2, 2, RING)),
        direct_send=dma((3, 2, 3, RING)), direct_recv=dma((3, 2, 3, RING)),
        **{
            side + name: vm(3, RING, *shape, kind=kind)
            for side in "sr"
            for name, shape, kind in (
                ("a", (2, 128, W // 2), bf), ("b", (2, 128, W), bf), ("c", (3, 32, W), bf), ("d", (3, 16, W // 2), bf),
            )
        },
    )


def kernel(names, *refs):
    r = types.SimpleNamespace(**dict(zip(names, refs)))
    seq, h = lax.axis_index("seq"), lax.axis_index("head")
    me = place()
    load_first(r)
    barrier = pltpu.get_barrier_semaphore()
    peers = [(seq, (h + k) % 16) for k in range(1, 16)] + [other_core(me), beside(me, "y", 1), beside(me, "y", 2), beside(me, "y", 3)]
    for peer in peers:
        pl.semaphore_signal(barrier, inc=1, device_id=peer, device_id_type=MESH)
    pl.semaphore_wait(barrier, len(peers))
    project(r, seq, h)
    gather_second(r, seq, h)
    r.nt[...] = r.cot[...].astype(f32).T
    choose_rows(r, me, 2, FEED)
    r.nt[...] = r.n1[...].astype(f32).T
    for order in range(3):
        choose_rows(r, me, order, ONE)
    attend(r, seq, h)
    r.nt[...] = r.attt[...].astype(f32)
    for order in (1, 2):
        choose_rows(r, me, order, OUT)

    def begin():
        r.nt[...] = r.n2[...].astype(f32).T
        for order in (0, 1):
            choose_rows(r, me, order, FEED)

    def each(j, grad_gate, grad_up, act):
        for order, value in enumerate((grad_gate, grad_up, act)):
            give(r, me, order, j, value)

        @pl.when(j == 1)
        def _():
            wait_rows(r, me, FEED)

        @pl.when((j == 1) | (j == 3) | (j == 5) | (j == 7) | (j == 9) | (j == 10))
        def _():
            sum_slot(r, me, sum(jnp.where(j > c, 1, 0) for c in (1, 3, 5, 7, 9, 10,)))

    feed(r, begin, each)
    load_first(r, again=True)
    for c in range(2):
        give(r, me, 1, 11 + c, r.gb[:, c * 256 : (c + 1) * 256])
        give(r, me, 2, 11 + c, r.gb[:, 512 + c * 256 : 768 + c * 256])
    give_heads(r, me, 0, r.ga, r.ot)
    prepare_back(r)
    wait_rows(r, me, OUT)

    @pl.loop(0, 8)
    def _(b):
        @pl.when(b <= h // 2)
        def _():
            back_step(r, seq, h, b)

        @pl.when((b == 1) | (b == 3) | (b == 5) | (b == 6))
        def _():
            sum_slot(r, me, 6 + sum(jnp.where(b > c, 1, 0) for c in (1, 3, 5, 6,)))

    finish_queries(r, me)
    wait_rows(r, me, ONE)
    sum_slot(r, me, 10)
    sum_slot(r, me, 11)
    sum_latents(r, seq, h)
    sum_slot(r, me, 12)
    sum_slot(r, me, 13)
    sum_slot(r, me, 14)
    finish_latent(r, me, seq, h)
    sum_slot(r, me, 15)
    for i in range(4):
        wait_first(r, i)
    finish_input(r)
    finish_rope(r, me)

    @pl.loop(16, 25)
    def _(t):
        sum_slot(r, me, t)

    result_copy(r, "sums").start()
    sum_end(r, me)
    back_sent(r, seq, h)
    latents_sent(r, seq, h)
    gather_sent(r, seq, h)
    for name in RESULTS:
        result_copy(r, name).wait()


def run(layer_input, second_start, mixer_gain, w_query, w_query_rope, w_latent, w_key_rope, w_key_up, w_value_up, w_out, feed_gain, w_gate, w_up, w_down, cotangent):
    args = dict(x_hbm=layer_input, cot_hbm=cotangent, second=second_start, gain1_hbm=mixer_gain, gain2_hbm=feed_gain,
        wkr_hbm=w_key_rope.T, kup_hbm=w_key_up, vup_hbm=w_value_up, wq=w_query, wqr=w_query_rope, wl=w_latent, wo_hbm=w_out, wg=w_gate, wu=w_up, wd=w_down)
    A, S = (pl.BlockSpec(memory_space=m) for m in (pl.ANY, pltpu.SMEM))
    specs = {n: S if n == "second" else A for n in INPUTS}
    outs = dict(output_hbm=((128, 1024), bf), grad_input_hbm=((128, 1024), f32), sums_hbm=((3, 8, JOBS * W), f32))
    sc = scratch()
    names = INPUTS + tuple(outs) + tuple(sc)
    output, grad_input, sums = pl.pallas_call(
        lambda *refs: kernel(names, *refs),
        out_shape=[jax.ShapeDtypeStruct(*o) for o in outs.values()],
        in_specs=[specs[n] for n in INPUTS], out_specs=[A] * len(outs),
        scratch_shapes=list(sc.values()),
        compiler_params=pltpu.CompilerParams(collective_id=0, has_side_effects=True, vmem_limit_bytes=66900000),
        name="layer",
    )(*[args[n] for n in INPUTS])

    return place_results(output, grad_input, sums)


def place_kernel(output, grad_input, sums, *outs):
    first, second, third = (sums.at[i] for i in range(3))
    outs[0][...] = output[...]
    outs[1][...] = grad_input[...]
    rope = first[:, 4096:4224]
    turned = jnp.concatenate([rope, jnp.zeros((120, 128), f32)], 0).T
    outs[2][...] = turned[32:33, 0:8]
    outs[3][:, 0:512] = second[:, 3328:3840]
    outs[3][:, 512:1024] = third[:, 3328:3840]
    outs[4][...] = first[:, 3328:3840]
    outs[5][:, 0:256] = second[:, 3840:4096]
    outs[5][:, 256:512] = third[:, 3840:4096]
    outs[6][...] = rope[:, 0:32]
    for g in range(2):
        outs[7][g] = first[g * 4 : g * 4 + 4, 3072:3328]
        outs[8][g] = first[g * 4 : g * 4 + 4, 2816:3072]
    outs[9][:, 0:512] = second[:, 2816:3328]
    outs[9][:, 512:1024] = third[:, 2816:3328]
    outs[10][...] = turned[33:34, 0:8]
    outs[11][...] = first[:, 0:2816]
    outs[12][...] = second[:, 0:2816]
    outs[13][...] = third[:, 0:2816]


def place_results(output, grad_input, sums):
    shapes = [(1, 8), (8, 1024), (8, 512), (8, 512), (8, 32), (2, 4, 256), (2, 4, 256), (8, 1024), (1, 8), (8, 2816), (8, 2816), (8, 2816)]
    outs = list(pl.pallas_call(
        place_kernel,
        out_shape=[jax.ShapeDtypeStruct((128, 1024), bf), jax.ShapeDtypeStruct((128, 1024), f32)]
        + [jax.ShapeDtypeStruct(shape, f32) for shape in shapes],
        name="place",
    )(output, grad_input, sums))
    for i in (2, 10):
        outs[i] = outs[i].reshape(8)
    for i in (7, 8):
        outs[i] = outs[i].transpose(0, 2, 1)
    outs[13] = outs[13].T
    return tuple(outs)


def solution(mesh):
    in_specs = (
        P(("seq", "head"), None),
        P("seq"),
        P(),
        P(),
        P(),
        P(),
        P(),
        P(),
        P(),
        P(),
        P(),
        P(),
        P(),
        P(),
        P(("seq", "head"), None),
    )
    out_specs = (
        P(("seq", "head"), None),
        P(("seq", "head"), None),
        P(("seq", "head")),
        P(("seq", "head"), None),
        P(("seq", "head"), None),
        P(("seq", "head"), None),
        P(("seq", "head"), None),
        P(None, None, ("seq", "head")),
        P(None, None, ("seq", "head")),
        P(("seq", "head"), None),
        P(("seq", "head")),
        P(("seq", "head"), None),
        P(("seq", "head"), None),
        P(None, ("seq", "head")),
    )
    return jax.shard_map(run, mesh=mesh, in_specs=in_specs, out_specs=out_specs, check_vma=False)
```
